32 devices in a mesh: dp: 8 (over z, core), fsdp: 4 (over y, x).
Axes of the slice: x: 2, y: 2, z: 4, core: 2. Of those that a mesh axis runs over, the one named last changes fastest.
Arguments:
- tokens: bfloat16 [32, 512, 1024], P(('dp', 'fsdp')), may hold values from -6 to 6
- segment_ids: int32 [32, 512], P(('dp', 'fsdp')), may hold values from 0 to 7, never falling along the last dimension, each value on 1 to 256 neighbouring positions
- rel_bucket: int32 [1023], replicated, may hold values from 0 to 511, as said below
- query_weight: float32 [1024, 1024], P(('dp', 'fsdp')), may hold values from -0.25 to 0.25
- query_bias: float32 [1024], P(('dp', 'fsdp')), may hold values from -3 to 3
- key_weight: float32 [1024, 1024], P(('dp', 'fsdp')), may hold values from -0.25 to 0.25
- key_bias: float32 [1024], P(('dp', 'fsdp')), may hold values from -3 to 3
- value_weight: float32 [1024, 1024], P(('dp', 'fsdp')), may hold values from -0.1875 to 0.1875
- value_bias: float32 [1024], P(('dp', 'fsdp')), may hold values from -3 to 3
- out_weight: float32 [1024, 1024], P(None, ('dp', 'fsdp')), may hold values from -0.75 to 0.75
- out_bias: float32 [1024], P(('dp', 'fsdp')), may hold values from -3 to 3
- attention_gain: float32 [1024], P(('dp', 'fsdp')), may hold values from 0.1 to 1.9
- attention_shift: float32 [1024], P(('dp', 'fsdp')), may hold values from -2 to 2
- up_weight: float32 [1024, 4096], P(('dp', 'fsdp')), may hold values from -0.1875 to 0.1875
- up_bias: float32 [4096], P(('dp', 'fsdp')), may hold values from -3 to 3
- down_weight: float32 [4096, 1024], P(None, ('dp', 'fsdp')), may hold values from -0.125 to 0.125
- down_bias: float32 [1024], P(('dp', 'fsdp')), may hold values from -3 to 3
- output_gain: float32 [1024], P(('dp', 'fsdp')), may hold values from 0.1 to 1.9
- output_shift: float32 [1024], P(('dp', 'fsdp')), may hold values from -2 to 2
- position_table: float32 [512, 1024], P(None, ('dp', 'fsdp')), may hold values from -6 to 6
- cotangent: bfloat16 [32, 512, 1024], P(('dp', 'fsdp')), may hold values from -8 to 8
Outputs:
- layer_out: bfloat16 [32, 512, 1024], P(('dp', 'fsdp'))
- tokens_grad: bfloat16 [32, 512, 1024], P(('dp', 'fsdp'))
- query_weight_grad: float32 [1024, 1024], P(('dp', 'fsdp'))
- query_bias_grad: float32 [1024], P(('dp', 'fsdp'))
- key_weight_grad: float32 [1024, 1024], P(('dp', 'fsdp'))
- key_bias_grad: float32 [1024], P(('dp', 'fsdp'))
- value_weight_grad: float32 [1024, 1024], P(('dp', 'fsdp'))
- value_bias_grad: float32 [1024], P(('dp', 'fsdp'))
- out_weight_grad: float32 [1024, 1024], P(None, ('dp', 'fsdp'))
- out_bias_grad: float32 [1024], P(('dp', 'fsdp'))
- attention_gain_grad: float32 [1024], P(('dp', 'fsdp'))
- attention_shift_grad: float32 [1024], P(('dp', 'fsdp'))
- up_weight_grad: float32 [1024, 4096], P(('dp', 'fsdp'))
- up_bias_grad: float32 [4096], P(('dp', 'fsdp'))
- down_weight_grad: float32 [4096, 1024], P(None, ('dp', 'fsdp'))
- down_bias_grad: float32 [1024], P(('dp', 'fsdp'))
- output_gain_grad: float32 [1024], P(('dp', 'fsdp'))
- output_shift_grad: float32 [1024], P(('dp', 'fsdp'))
- position_table_grad: float32 [512, 1024], P(None, ('dp', 'fsdp'))
The draws below stay inside these ranges and needn't reach their ends.
Inputs may be any that keep to these rules, and one draw needn't show every extreme that they name: `segment_ids`: within each sequence the document numbers never fall; a document spans 1 to half of 512 tokens, and in each sequence one spans exactly that many. `rel_bucket`: never falls along its length; the entry for distance zero is half of 512, the first entry is 0 and the last is 511.
All inputs are finite; a program needn't handle non-finite values.
Results may differ from the reference program's by a relative error of at most 0.023.
Values may be sent and summed in bfloat16 or wider, within the bound.
No kernel may reach another device: no remote copies, remote signals or barrier semaphores. Data moves between devices by JAX's collectives and lax.ppermute only.
A program may use at most 384 MiB of HBM per device.

```python
import math
from functools import partial
import jax
import jax.numpy as jnp
import numpy as np
from jax import lax

D = 1024
HEADS = 16
FF = 4096
BUCKETS = 512
LEN = 512
DOCS = 8
SEQS = 32


def draw_rel_bucket(key, part):
    half_span = BUCKETS // 2
    middle = half_span // 2
    key_upper, key_lower = jax.random.split(jax.random.fold_in(key, 7))
    distance = jnp.arange(1, LEN, dtype=jnp.int32)

    def reach(rand_key, top_value):
        coin_draws = jax.random.randint(rand_key, (LEN - 1,), 0, 3)
        rise_steps = jnp.where((coin_draws == 0) & (distance > middle), 1, 0).astype(jnp.int32)
        grown_steps = jnp.where(distance <= middle, distance, middle + jnp.cumsum(rise_steps))
        grown_steps = jnp.minimum(grown_steps, top_value)
        return jnp.where(distance == LEN - 1, top_value, grown_steps).astype(jnp.int32)
    upper_side = half_span + reach(key_upper, half_span - 1)
    lower_side = half_span - reach(key_lower, half_span)
    centre_entry = jnp.full((1,), half_span, jnp.int32)
    return jnp.concatenate([lower_side[::-1], centre_entry, upper_side]).astype(jnp.int32)


def raised(drawn, rng, source, target, shards_of, factor):
    def block_of(position):
        return (jnp.arange(drawn.shape[position]) // (drawn.shape[position] // shards_of)).reshape((-1,) + (1,) * (drawn.ndim - 1 - position))

    one_side = jax.random.permutation(rng, shards_of)[block_of(target)]
    far = (block_of(target) + shards_of // 2) % shards_of
    return jnp.where((block_of(source) == one_side) | (block_of(source) == far), factor * drawn, drawn)


def levels(own_key, shape, cuts, least, largest):
    loudness, own = 1.0, jax.random.fold_in(own_key, 6)
    for dim, blocks in cuts:
        draws = jnp.exp(jax.random.uniform(jax.random.fold_in(own, dim), (blocks,), jnp.float32, least / len(cuts), largest / len(cuts)))
        loudness = loudness * jnp.repeat(draws, shape[dim] // blocks).reshape([-1 if axis == dim else 1 for axis in range(len(shape))])
    return loudness


def profile(count, total, bound, skew):
    loads = [(1 << 20) // math.isqrt(grade ** skew) + 1 for grade in range(2, count + 1)]
    surplus, counts = total - bound - (count - 1), [1] * (count - 1)
    while surplus > 0:
        candidates = [i for i in range(count - 1) if counts[i] < bound]
        pool, budget = sum([loads[i] for i in candidates]), surplus
        for i in candidates:
            addition = min(bound - counts[i], max(1, budget * loads[i] // pool), surplus)
            counts[i] = counts[i] + addition
            surplus = surplus - addition
    return np.array([bound] + counts)


def ragged(key, count, total, bound, skew):
    if count == 2:
        one = jax.random.randint(key, (), max(1, total - bound), min(bound, total - 1) + 1)
        return jnp.stack([one, total - one])
    tallies = jnp.asarray(profile(count, total, bound, skew), jnp.int32)
    couples = (count - 1) // 2
    donor, receiver = tallies[1:1 + 2 * couples:2], tallies[2:2 + 2 * couples:2]
    slack = jnp.minimum(donor - 1, bound - receiver)
    shifted = jax.random.randint(jax.random.fold_in(key, 1), (couples,), 0, 1 << 20) % (slack + 1)
    tallies = tallies.at[1:1 + 2 * couples:2].set(donor - shifted).at[2:2 + 2 * couples:2].set(receiver + shifted)
    return tallies[jax.random.permutation(jax.random.fold_in(key, 2), count)]


def noise(stream_key, dims, width, limit, cuts=(), kind=jnp.bfloat16):
    drawn = jax.random.normal(stream_key, dims, jnp.float32) * width
    if len(cuts) > 0:
        drawn = levels(stream_key, dims, cuts, -0.22, 0.18) * drawn
    return jnp.clip(drawn, min=-limit, max=limit).astype(kind)


def noise_with(key, extent, width, most, cuts, heavy, kind=jnp.bfloat16):
    drawn = width * jax.random.normal(key, extent, jnp.float32)
    if cuts:
        drawn = drawn * levels(key, extent, cuts, -0.22, 0.18)
    return jnp.clip(raised(drawn, jax.random.fold_in(key, 3), *heavy), -most, most).astype(kind)


def setup_inputs(seed: int = 0) -> dict:
    splits = jax.random.split(jax.random.key(seed), 22)
    tokens = noise(splits[0], (SEQS, LEN, D), 1.0, 6.0, ((0, 32),))
    segment_ids = jax.vmap(lambda own: jnp.searchsorted(jnp.cumsum(ragged(own, DOCS, LEN, LEN // 2, 2)), jnp.arange(LEN), side="right"))(jax.random.split(splits[1], SEQS)).reshape((SEQS, LEN)).astype(jnp.int32)
    rel_bucket = draw_rel_bucket(jax.random.fold_in(splits[21], 71), 0)
    query_weight = noise(splits[3], (D, D), (D // 2) ** -0.5, 0.25, ((0, 32),), jnp.float32)
    query_bias = noise(splits[4], (D,), 0.5, 3.0, ((0, 32),), jnp.float32)
    key_weight = noise(splits[5], (D, D), (D // 2) ** -0.5, 0.25, ((0, 32),), jnp.float32)
    key_bias = noise(splits[6], (D,), 0.5, 3.0, ((0, 32),), jnp.float32)
    value_weight = noise(splits[7], (D, D), D ** -0.5, 0.1875, ((0, 32),), jnp.float32)
    value_bias = noise(splits[8], (D,), 0.5, 3.0, ((0, 32),), jnp.float32)
    out_weight = noise(splits[9], (D, D), (D // 16) ** -0.5, 0.75, ((1, 32),), jnp.float32)
    out_bias = noise(splits[10], (D,), 0.5, 3.0, ((0, 32),), jnp.float32)
    attention_gain = jnp.clip(1.0 + 0.18 * jax.random.normal(splits[11], (D,), jnp.float32), 0.1, 1.9)
    attention_shift = noise(splits[12], (D,), 0.3, 2.0, ((0, 32),), jnp.float32)
    up_weight = noise(splits[13], (D, FF), D ** -0.5, 0.1875, ((0, 32),), jnp.float32)
    up_bias = noise(splits[14], (FF,), 0.5, 3.0, ((0, 32),), jnp.float32)
    down_weight = noise(splits[15], (FF, D), (FF // 2) ** -0.5, 0.125, ((1, 32),), jnp.float32)
    down_bias = noise(splits[16], (D,), 0.5, 3.0, ((0, 32),), jnp.float32)
    output_gain = jnp.clip(1.0 + 0.18 * jax.random.normal(splits[17], (D,), jnp.float32), 0.1, 1.9)
    output_shift = noise(splits[18], (D,), 0.3, 2.0, ((0, 32),), jnp.float32)
    position_table = noise(splits[19], (BUCKETS, D), 1.0, 6.0, ((1, 32),), jnp.float32)
    cotangent = noise_with(splits[20], (SEQS, LEN, D), 1.0, 8.0, ((0, 32),), (0, 2, 32, 2.75))
    return {"tokens": tokens, "segment_ids": segment_ids, "rel_bucket": rel_bucket, "query_weight": query_weight, "query_bias": query_bias, "key_weight": key_weight, "key_bias": key_bias, "value_weight": value_weight, "value_bias": value_bias, "out_weight": out_weight, "out_bias": out_bias, "attention_gain": attention_gain, "attention_shift": attention_shift, "up_weight": up_weight, "up_bias": up_bias, "down_weight": down_weight, "down_bias": down_bias, "output_gain": output_gain, "output_shift": output_shift, "position_table": position_table, "cotangent": cotangent}


NORM_EPS = 1e-07

@jax.custom_vjp
def low(v):
    return lax.optimization_barrier(v.astype(jnp.bfloat16)).astype(jnp.float32)

@jax.custom_vjp
def low_back(v):
    return v

def low_keep(v):
    return (low(v), None)

def low_pass(kept, grad):
    return (grad,)

def back_keep(v):
    return (v, None)

def back_low(kept, grad):
    return (low(grad),)
low.defvjp(low_keep, low_pass)
low_back.defvjp(back_keep, back_low)

def dense(left, right):
    return jnp.dot(left, right, precision=lax.Precision.HIGHEST, preferred_element_type=jnp.float32)

def contract_product(form, left, right):
    return jnp.einsum(form, left, right, precision=lax.Precision.HIGHEST, preferred_element_type=jnp.float32)

def divide_into_heads(matrix):
    return matrix.reshape(matrix.shape[0], HEADS, -1).transpose(1, 0, 2)

def layer_norm(values_in, gain_vec, shift_vec):
    row_mean = lax.optimization_barrier(jnp.mean(values_in, axis=-1, keepdims=True))
    centered = values_in - row_mean
    row_variance = lax.optimization_barrier(jnp.mean(centered * centered, axis=-1, keepdims=True))
    return centered * lax.rsqrt(row_variance + NORM_EPS) * gain_vec + shift_vec

def layer_forward(weight_list, inputs, segment_row, bucket_table):
    query_weight, query_bias, key_weight, key_bias, value_weight, value_bias, out_weight, out_bias, attention_gain, attention_shift, up_weight, up_bias, down_weight, down_bias, output_gain, output_shift, position_table = [low(member) for member in weight_list]
    seq_len = inputs.shape[0]
    head_size = query_weight.shape[1] // HEADS
    score_scale = 1.0 / math.sqrt(3.0 * head_size)
    queries = low(low_back(dense(inputs, query_weight) + query_bias))
    keys_all = low(low_back(dense(inputs, key_weight) + key_bias))
    values_all = low(low_back(dense(inputs, value_weight) + value_bias))
    position_key_rows = low(low_back(dense(position_table, key_weight) + key_bias))
    pos_queries = low(low_back(dense(position_table, query_weight) + query_bias))
    query_split_heads = divide_into_heads(queries)
    key_heads = divide_into_heads(keys_all)
    value_heads = divide_into_heads(values_all)
    query_position_rows = low_back(contract_product('rtk,rxk->rtx', query_split_heads, divide_into_heads(position_key_rows)))
    key_position_rows = low_back(contract_product('hjd,hbd->hjb', key_heads, divide_into_heads(pos_queries)))
    block_rows = min(512, seq_len)
    positions = jnp.arange(seq_len, dtype=jnp.int32)

    def attend(row_start):
        row_ids = row_start + jnp.arange(block_rows, dtype=jnp.int32)
        query_block = lax.dynamic_slice_in_dim(query_split_heads, row_start, block_rows, 1)
        qpos_block = lax.dynamic_slice_in_dim(query_position_rows, row_start, block_rows, 1)
        index_one = jnp.take(bucket_table, row_ids[:, None] - positions[None, :] + (seq_len - 1))
        index_two = jnp.take(bucket_table, positions[:, None] - row_ids[None, :] + (seq_len - 1))
        to_content = jax.vmap(partial(jnp.take_along_axis, indices=index_one, axis=1))(qpos_block)
        from_content = jax.vmap(partial(jnp.take_along_axis, indices=index_two, axis=1))(key_position_rows)
        content = contract_product('hid,hjd->hij', query_block, key_heads)
        scores = low_back((content + to_content + from_content.transpose(0, 2, 1)) * score_scale)
        same_doc = jnp.take(segment_row, row_ids)[:, None] == segment_row[None, :]
        weights_soft = low(jax.nn.softmax(jnp.where(same_doc[None], scores, -1e+30), axis=-1))
        return contract_product('hij,hjd->hid', weights_soft, value_heads)
    starts = jnp.arange(seq_len // block_rows, dtype=jnp.int32) * block_rows
    blocks = lax.map(jax.checkpoint(attend), starts)
    context = low(low_back(blocks.transpose(0, 2, 1, 3).reshape(seq_len, -1)))
    attn_out = low_back(dense(context, out_weight) + out_bias)
    mixed_one = layer_norm(inputs + attn_out, attention_gain, attention_shift)
    up_proj = low_back(dense(low(mixed_one), up_weight) + up_bias)
    activated = low(jax.nn.gelu(up_proj, approximate=False))
    ffn_out = low_back(dense(activated, down_weight) + down_bias)
    return layer_norm(mixed_one + ffn_out, output_gain, output_shift)

def reference(tokens, segment_ids, rel_bucket, query_weight, query_bias, key_weight, key_bias, value_weight, value_bias, out_weight, out_bias, attention_gain, attention_shift, up_weight, up_bias, down_weight, down_bias, output_gain, output_shift, position_table, cotangent):
    params = tuple((member.astype(jnp.float32) for member in (query_weight, query_bias, key_weight, key_bias, value_weight, value_bias, out_weight, out_bias, attention_gain, attention_shift, up_weight, up_bias, down_weight, down_bias, output_gain, output_shift, position_table)))

    def sequence_step(grad_sums, seq_items):
        seq_tokens, seq_segments, seq_cot = seq_items

        def forward_fn(weight_list, acts):
            return layer_forward(weight_list, acts, seq_segments, rel_bucket)
        outputs, pullback = jax.vjp(forward_fn, params, seq_tokens.astype(jnp.float32))
        weight_grads, input_grad = pullback(seq_cot.astype(jnp.float32))
        updated_sums = tuple((total + part_grad for total, part_grad in zip(grad_sums, weight_grads)))
        return (updated_sums, (outputs.astype(jnp.bfloat16), input_grad.astype(jnp.bfloat16)))
    initial = tuple((jnp.zeros(member.shape, jnp.float32) for member in params))
    totals, (layer_outs, input_grads) = lax.scan(sequence_step, initial, (tokens, segment_ids, cotangent))
    return (layer_outs, input_grads) + tuple(totals)
```

```python
import math
import jax, jax.numpy as jnp
from jax import lax
from jax.sharding import PartitionSpec as P
import jax.experimental.pallas as pl, jax.experimental.pallas.tpu as pltpu
HEADS=16
BF=jnp.bfloat16
F32=jnp.float32

def mm(a,b,ca,cb):
    return lax.dot_general(a,b,(((ca,),(cb,)),((),())),preferred_element_type=F32)

def attend_kernel(scale, q_ref,k_ref,v_ref,ek_ref,eq_ref,segc_ref,segr_ref,ctx_ref,p_ref):
    t=q_ref.shape[0]; half=t//2
    hd=q_ref.shape[1]//2
    same=segc_ref[...]==segr_ref[...]
    lane=lax.broadcasted_iota(jnp.int32,q_ref.shape,1)
    ctx=None
    for h in range(2):
        mine=(lane>=h*hd)&(lane<(h+1)*hd)
        pick=lambda r: jnp.where(mine,r[...],jnp.zeros((),BF))
        q=pick(q_ref); k=pick(k_ref)
        s=mm(q,k_ref[...],1,1)
        to=pltpu.roll(mm(q,ek_ref[...],1,1),half,1,stride=1,stride_axis=0)
        fr=pltpu.roll(mm(k,eq_ref[...],1,1),half,1,stride=1,stride_axis=0)
        s=jnp.where(same,s+to+fr.T,-1e30)
        top=jnp.max(s,axis=1,keepdims=True)
        e=jnp.exp((s-top)*scale)
        p=(e*(1.0/jnp.sum(e,axis=1,keepdims=True))).astype(BF)
        p_ref[h]=p
        part=mm(p,pick(v_ref),1,0)
        ctx=part if ctx is None else ctx+part
    ctx_ref[...]=ctx.astype(BF)

def attend(q,k,v,ek,eq,seg,scale):
    t,d=q.shape
    w=2*d//HEADS
    col=pl.BlockSpec((t,w),lambda i:(0,i))
    return pl.pallas_call(
        lambda *r: attend_kernel(scale,*r),
        grid=(HEADS//2,),
        in_specs=[col]*5+[pl.BlockSpec((t,1),lambda i:(0,0)),pl.BlockSpec((1,t),lambda i:(0,0))],
        out_specs=[col,pl.BlockSpec((2,t,t),lambda i:(i,0,0))],
        out_shape=[jax.ShapeDtypeStruct((t,d),BF),jax.ShapeDtypeStruct((HEADS,t,t),BF)],
        compiler_params=pltpu.CompilerParams(vmem_limit_bytes=48*2**20),
    )(q,k,v,ek,eq,seg.reshape(t,1),seg.reshape(1,t))

def attend_back_kernel(scale,q_ref,k_ref,v_ref,ek_ref,eq_ref,dc_ref,p_ref,dq_ref,dk_ref,dv_ref,dek_ref,deq_ref):
    t=q_ref.shape[0]; half=t//2
    hd=q_ref.shape[1]//2
    r=lax.broadcasted_iota(jnp.int32,(half,half),0); c=lax.broadcasted_iota(jnp.int32,(half,half),1)
    flip=(r+c==half-1).astype(BF)
    lane=lax.broadcasted_iota(jnp.int32,q_ref.shape,1)
    def turn(x):
        return jnp.concatenate([mm(flip,x[:half],1,0),mm(flip,x[half:],1,0)],0)
    def turn_t(x):
        return jnp.concatenate([mm(flip,x[:,:half],1,1),mm(flip,x[:,half:],1,1)],0)
    def unroll(x):
        return jnp.concatenate([pltpu.roll(x[:half],1,1,stride=1,stride_axis=0),pltpu.roll(x[half:],half+1,1,stride=1,stride_axis=0)],0)
    q_turned=turn(q_ref[...]).astype(BF); k_turned=turn(k_ref[...]).astype(BF)
    dqt=dkt=dv=dek=deq=None
    plus=lambda a,b: b if a is None else a+b
    for h in range(2):
        mine=(lane>=h*hd)&(lane<(h+1)*hd)
        pick=lambda x: jnp.where(mine,x,jnp.zeros((),BF))
        p=p_ref[h]; dc=pick(dc_ref[...])
        dp=mm(dc,v_ref[...],1,1)
        pf=p.astype(F32)
        w=pf*dp
        ds=(w-pf*jnp.sum(w,axis=1,keepdims=True)).astype(BF)
        dv=plus(dv,mm(p,dc,0,0))
        a=turn(ds).astype(BF); au=unroll(a)
        b=turn_t(ds).astype(BF); bu=unroll(b)
        dqt=plus(dqt,mm(a,pick(k_ref[...]),1,0)+mm(au,pick(ek_ref[...]),1,0))
        dkt=plus(dkt,mm(b,pick(q_ref[...]),1,0)+mm(bu,pick(eq_ref[...]),1,0))
        dek=plus(dek,mm(au,pick(q_turned),0,0))
        deq=plus(deq,mm(bu,pick(k_turned),0,0))
    dq_ref[...]=turn((dqt*scale).astype(BF)).astype(BF)
    dk_ref[...]=turn((dkt*scale).astype(BF)).astype(BF)
    dv_ref[...]=dv.astype(BF)
    dek_ref[...]=(dek*scale).astype(BF)
    deq_ref[...]=(deq*scale).astype(BF)

def attend_back(q,k,v,ek,eq,dc,p,scale):
    t,d=q.shape
    w=2*d//HEADS
    col=pl.BlockSpec((t,w),lambda i:(0,i))
    return pl.pallas_call(
        lambda *r: attend_back_kernel(scale,*r),
        grid=(HEADS//2,),
        in_specs=[col]*6+[pl.BlockSpec((2,t,t),lambda i:(i,0,0))],
        out_specs=[col]*5,
        out_shape=[jax.ShapeDtypeStruct((t,d),BF)]*5,
        compiler_params=pltpu.CompilerParams(vmem_limit_bytes=48*2**20),
    )(q,k,v,ek,eq,dc,p)


NORM_EPS = 1e-7
SPLIT = 9


def norm_parts(v):
    mean = jnp.mean(v, axis=-1, keepdims=True)
    c = v - mean
    r = lax.rsqrt(jnp.mean(c * c, axis=-1, keepdims=True) + NORM_EPS)
    return c * r, r


def norm_back(g, gain, n, r):
    u = g * gain
    d = r * (u - jnp.mean(u, -1, keepdims=True) - n * jnp.mean(u * n, -1, keepdims=True))
    return d, jnp.sum(g * n, 0), jnp.sum(g, 0)


class Tree:
    def __init__(self, width):
        self.nf, self.ndp = lax.axis_size("fsdp"), lax.axis_size("dp")
        self.n = self.nf * self.ndp
        self.nz = self.ndp // 2
        self.rows = width // self.n
        self.width = width

    def place(self):
        me = lax.axis_index("dp") * self.nf + lax.axis_index("fsdp")
        d = lax.broadcasted_iota(jnp.int32, (self.width, self.width), 0)
        j = lax.broadcasted_iota(jnp.int32, (self.width, self.width), 1)
        rel = (d // self.rows) ^ me
        f = rel % self.nf
        core = (rel // self.nf) % 2
        z = rel // (2 * self.nf)
        at = ((core * self.nf + f) * self.nz + z) * self.rows + d % self.rows
        return (at == j).astype(BF)

    def swap(self, a, axis, bit):
        size = self.nf if axis == "fsdp" else self.ndp
        return lax.ppermute(a, axis, [(i, i ^ bit) for i in range(size)])

    def finish(self, mine, flipped):
        step = self.nz * self.rows
        parts = [mine[i * step : (i + 1) * step] for i in range(self.nf)]
        bits = [1 << b for b in range(self.nf.bit_length() - 1)]
        for bit in bits[::-1] if flipped else bits:
            live = [i for i in range(len(parts)) if parts[i] is not None]
            for i in live:
                if i & bit:
                    got = self.swap(parts[i], "fsdp", bit)
                    parts[i ^ bit] = (parts[i ^ bit].astype(F32) + got.astype(F32)).astype(BF)
                    parts[i] = None
        total = parts[0]
        bit = self.nz // 2
        while bit:
            h = total.shape[0] // 2
            got = self.swap(total[h:], "dp", 2 * bit)
            total = total[:h].astype(F32) + got.astype(F32)
            bit //= 2
            if bit:
                total = total.astype(BF)
        return total

    def core_sum(self, pairs):
        h = self.width // 2
        cat = lambda xs: xs[0] if len(xs) == 1 else jnp.concatenate(xs, 1)
        away = cat([mm(a[:, h:], b, 0, cb).astype(BF) for a, b, cb in pairs])
        got = self.swap(away, "dp", 1)
        mine = cat([mm(a[:, :h], b, 0, cb) for a, b, cb in pairs])
        return (mine + got.astype(F32)).astype(BF)


def per_device(
    tokens, segment_ids, rel_bucket, query_weight, query_bias, key_weight, key_bias, value_weight, value_bias,
    out_weight, out_bias, attention_gain, attention_shift, up_weight, up_bias, down_weight, down_bias,
    output_gain, output_shift, position_table, cotangent,
):
    x = tokens[0]
    t, d = x.shape
    seg = segment_ids[0]
    tree = Tree(d)
    rows = tree.rows
    ff = up_weight.shape[1]
    spread = ff // d
    buckets = position_table.shape[0]
    scale = 1.0 / math.sqrt(3.0 * (d // HEADS))
    vectors = (query_bias, key_bias, value_bias, out_bias, attention_gain, attention_shift, down_bias, output_gain, output_shift)
    small = jnp.concatenate([v[:, None] for v in vectors] + [up_bias.reshape(spread, rows).T], axis=1).astype(BF)
    small = jnp.pad(small, ((0, 0), (0, 128 - small.shape[1])))
    first = jnp.concatenate(
        [query_weight.astype(BF), key_weight.astype(BF), value_weight.astype(BF), position_table.T.astype(BF), small], axis=1
    )
    second = jnp.concatenate([out_weight.T.astype(BF), up_weight.astype(BF), down_weight.T.astype(BF)], axis=1)
    w1 = lax.all_gather(first, ("dp", "fsdp"), axis=0, tiled=True)
    w2 = lax.all_gather(second, ("dp", "fsdp"), axis=0, tiled=True)
    wq, wk, wv = w1[:, :d], w1[:, d : 2 * d], w1[:, 2 * d : 3 * d]
    table_t = w1[:, 3 * d : 3 * d + buckets]
    vec = w1[:, 3 * d + buckets :].T.astype(F32)
    bq, bk, bv, bo, gain1, shift1, bd, gain2, shift2 = [vec[i] for i in range(SPLIT)]
    bu = vec[SPLIT : SPLIT + spread].reshape(spread, tree.n, rows).transpose(1, 0, 2).reshape(ff)
    wo_t, wu, wd_t = w2[:, :d], w2[:, d : d + ff], w2[:, d + ff :]

    half = t // 2
    picked = lax.rev(rel_bucket[t - half : 2 * t - half], (0,))
    onehot = (picked[:, None] == lax.broadcasted_iota(jnp.int32, (t, buckets), 1)).astype(BF)
    q = (mm(x, wq, 1, 0) + bq).astype(BF)
    k = (mm(x, wk, 1, 0) + bk).astype(BF)
    v = (mm(x, wv, 1, 0) + bv).astype(BF)
    spread_table = mm(onehot, table_t, 1, 1).astype(BF)
    ek = (mm(spread_table, wk, 1, 0) + bk).astype(BF)
    eq = (mm(spread_table, wq, 1, 0) + bq).astype(BF)
    context, probs = attend(q, k, v, ek, eq, seg, scale)

    place = tree.place()
    n1, r1 = norm_parts(x.astype(F32) + mm(context, wo_t, 1, 1) + bo)
    mixed = n1 * gain1 + shift1
    mixed_low = mixed.astype(BF)
    up = mm(mixed_low, wu, 1, 0) + bu
    cdf = 0.5 * (1.0 + lax.erf(up * math.sqrt(0.5)))
    act = (up * cdf).astype(BF)
    slope = cdf + up * (jnp.exp(-0.5 * up * up) * (1.0 / math.sqrt(2.0 * math.pi)))
    n2, r2 = norm_parts(mixed + mm(act, wd_t, 1, 1) + bd)
    layer_out = (n2 * gain2 + shift2).astype(BF)
    d_sum, d_gain2, d_shift2 = norm_back(cotangent[0].astype(F32), gain2, n2, r2)
    d_ffn = d_sum.astype(BF)
    d_bd = jnp.sum(d_ffn.astype(F32), 0)
    arrange = lambda m: mm(m, place, 1, 0).astype(BF)
    down_mine = tree.core_sum([(arrange(d_ffn), act, 0)])
    d_up = (mm(d_ffn, wd_t, 1, 0) * slope).astype(BF)
    d_bu = jnp.sum(d_up.astype(F32), 0)
    up_mine = tree.core_sum([(arrange(mixed_low), d_up, 0)])
    d_mixed = d_sum + mm(d_up, wu, 1, 1)
    d_first, d_gain1, d_shift1 = norm_back(d_mixed, gain1, n1, r1)
    d_attn = d_first.astype(BF)
    d_bo = jnp.sum(d_attn.astype(F32), 0)
    d_context = mm(d_attn, wo_t, 1, 0).astype(BF)
    out_mine = tree.core_sum([(arrange(d_attn), context, 0)])
    down_grad = tree.finish(down_mine, True)
    up_grad = tree.finish(up_mine, False)
    out_grad = tree.finish(out_mine, True)

    dq, dk, dv, dek, deq = attend_back(q, k, v, ek, eq, d_context, probs, scale)
    d_pos_keys = mm(onehot, dek, 0, 0).astype(BF)
    d_pos_queries = mm(onehot, deq, 0, 0).astype(BF)
    colsum = lambda m: jnp.sum(m.astype(F32), 0)
    d_bq = colsum(dq) + colsum(d_pos_queries)
    d_bk = colsum(dk) + colsum(d_pos_keys)
    d_bv = colsum(dv)
    x_arranged = arrange(x)
    table_arranged = mm(table_t, place, 0, 0).astype(BF)
    left = jnp.concatenate([x_arranged, table_arranged], 0)
    d_table = (mm(d_pos_keys, wk, 1, 1) + mm(d_pos_queries, wq, 1, 1)).astype(BF)
    lines = jnp.stack([d_bq, d_bk, d_bv, d_bo, d_gain1, d_shift1, d_bd, d_gain2, d_shift2])
    lines = jnp.concatenate([lines, d_bu.reshape(tree.n, spread, rows).transpose(1, 0, 2).reshape(spread, d)], 0)
    lines = jnp.pad(lines, ((0, 128 - lines.shape[0]), (0, 0))).astype(BF)
    rest_mine = tree.core_sum([
        (left, jnp.concatenate([dq, d_pos_queries], 0), 0),
        (left, jnp.concatenate([dk, d_pos_keys], 0), 0),
        (x_arranged, dv, 0),
        (place, d_table, 1),
        (place, lines, 1),
    ])
    rest = tree.finish(rest_mine, False)
    input_grad = (d_first + mm(dq, wq, 1, 1) + mm(dk, wk, 1, 1) + mm(dv, wv, 1, 1)).astype(BF)
    tail = rest[:, 3 * d + buckets :]
    vecs = [tail[:, i] for i in range(SPLIT)]
    d_up_bias = tail[:, SPLIT : SPLIT + spread].T.reshape(-1)
    return (
        layer_out[None], input_grad[None],
        rest[:, :d], vecs[0], rest[:, d : 2 * d], vecs[1], rest[:, 2 * d : 3 * d], vecs[2],
        out_grad.T, vecs[3], vecs[4], vecs[5], up_grad, d_up_bias, down_grad.T, vecs[6], vecs[7], vecs[8],
        rest[:, 3 * d : 3 * d + buckets].T,
    )


def solution(mesh):
    both = ("dp", "fsdp")
    row, col, vec = P(both, None), P(None, both), P(both)
    seq = P(both, None, None)
    params = (row, vec, row, vec, row, vec, col, vec, vec, vec, row, vec, col, vec, vec, vec, col)
    return jax.shard_map(
        per_device, mesh=mesh, in_specs=(seq, row, P()) + params + (seq,), out_specs=(seq, seq) + params, check_vma=False
    )
```

```python
import math
import jax, jax.numpy as jnp
from jax import lax
from jax.sharding import PartitionSpec as P
import jax.experimental.pallas as pl, jax.experimental.pallas.tpu as pltpu
HEADS=16
BF=jnp.bfloat16
F32=jnp.float32
COST=pl.CostEstimate(flops=10**9,bytes_accessed=10**6,transcendentals=0)

def mm(a,b,ca,cb):
    return lax.dot_general(a,b,(((ca,),(cb,)),((),())),preferred_element_type=F32)

def attend_kernel(scale, q_ref,k_ref,v_ref,ek_ref,eq_ref,segc_ref,segr_ref,ctx_ref,p_ref):
    t=q_ref.shape[0]; half=t//2
    hd=q_ref.shape[1]//2
    same=segc_ref[...]==segr_ref[...]
    lane=lax.broadcasted_iota(jnp.int32,q_ref.shape,1)
    ctx=None
    for h in range(2):
        mine=(lane>=h*hd)&(lane<(h+1)*hd)
        pick=lambda r: jnp.where(mine,r[...],jnp.zeros((),BF))
        q=pick(q_ref); k=pick(k_ref)
        s=mm(q,k_ref[...],1,1)
        to=pltpu.roll(mm(q,ek_ref[...],1,1),half,1,stride=1,stride_axis=0)
        fr=pltpu.roll(mm(k,eq_ref[...],1,1),half,1,stride=1,stride_axis=0)
        s=jnp.where(same,s+to+fr.T,-1e30)
        top=jnp.max(s,axis=1,keepdims=True)
        e=jnp.exp((s-top)*scale)
        p=(e*(1.0/jnp.sum(e,axis=1,keepdims=True))).astype(BF)
        p_ref[h]=p
        part=mm(p,pick(v_ref),1,0)
        ctx=part if ctx is None else ctx+part
    ctx_ref[...]=ctx.astype(BF)

def attend(q,k,v,ek,eq,seg,scale):
    t,d=q.shape
    w=2*d//HEADS
    col=pl.BlockSpec((t,w),lambda i:(0,i))
    return pl.pallas_call(
        lambda *r: attend_kernel(scale,*r),
        grid=(HEADS//2,),
        in_specs=[col]*5+[pl.BlockSpec((t,1),lambda i:(0,0)),pl.BlockSpec((1,t),lambda i:(0,0))],
        out_specs=[col,pl.BlockSpec((2,t,t),lambda i:(i,0,0))],
        out_shape=[jax.ShapeDtypeStruct((t,d),BF),jax.ShapeDtypeStruct((HEADS,t,t),BF)],
        cost_estimate=COST,
        compiler_params=pltpu.CompilerParams(vmem_limit_bytes=48*2**20),
    )(q,k,v,ek,eq,seg.reshape(t,1),seg.reshape(1,t))

def attend_back_kernel(scale,q_ref,k_ref,v_ref,ek_ref,eq_ref,dc_ref,p_ref,dq_ref,dk_ref,dv_ref,dek_ref,deq_ref):
    t=q_ref.shape[0]; half=t//2
    hd=q_ref.shape[1]//2
    r=lax.broadcasted_iota(jnp.int32,(half,half),0); c=lax.broadcasted_iota(jnp.int32,(half,half),1)
    flip=(r+c==half-1).astype(BF)
    lane=lax.broadcasted_iota(jnp.int32,q_ref.shape,1)
    def turn(x):
        return jnp.concatenate([mm(flip,x[:half],1,0),mm(flip,x[half:],1,0)],0)
    def turn_t(x):
        return jnp.concatenate([mm(flip,x[:,:half],1,1),mm(flip,x[:,half:],1,1)],0)
    def unroll(x):
        return jnp.concatenate([pltpu.roll(x[:half],1,1,stride=1,stride_axis=0),pltpu.roll(x[half:],half+1,1,stride=1,stride_axis=0)],0)
    q_turned=turn(q_ref[...]).astype(BF); k_turned=turn(k_ref[...]).astype(BF)
    dqt=dkt=dv=dek=deq=None
    plus=lambda a,b: b if a is None else a+b
    for h in range(2):
        mine=(lane>=h*hd)&(lane<(h+1)*hd)
        pick=lambda x: jnp.where(mine,x,jnp.zeros((),BF))
        p=p_ref[h]; dc=pick(dc_ref[...])
        dp=mm(dc,v_ref[...],1,1)
        pf=p.astype(F32)
        w=pf*dp
        ds=(w-pf*jnp.sum(w,axis=1,keepdims=True)).astype(BF)
        dv=plus(dv,mm(p,dc,0,0))
        a=turn(ds).astype(BF); au=unroll(a)
        b=turn_t(ds).astype(BF); bu=unroll(b)
        dqt=plus(dqt,mm(a,pick(k_ref[...]),1,0)+mm(au,pick(ek_ref[...]),1,0))
        dkt=plus(dkt,mm(b,pick(q_ref[...]),1,0)+mm(bu,pick(eq_ref[...]),1,0))
        dek=plus(dek,mm(au,pick(q_turned),0,0))
        deq=plus(deq,mm(bu,pick(k_turned),0,0))
    dq_ref[...]=turn((dqt*scale).astype(BF)).astype(BF)
    dk_ref[...]=turn((dkt*scale).astype(BF)).astype(BF)
    dv_ref[...]=dv.astype(BF)
    dek_ref[...]=(dek*scale).astype(BF)
    deq_ref[...]=(deq*scale).astype(BF)

def attend_back(q,k,v,ek,eq,dc,p,scale,grads,at,count):
    t,d=q.shape
    w=2*d//HEADS
    col=pl.BlockSpec((t,w),lambda i:(0,i+at))
    grads=[] if grads is None else list(grads)
    return pl.pallas_call(
        lambda *r: attend_back_kernel(scale,*r[:7],*r[len(r)-5:]),
        grid=(count,),
        in_specs=[col]*6+[pl.BlockSpec((2,t,t),lambda i:(i+at,0,0))]+[pl.BlockSpec(memory_space=pl.ANY)]*len(grads),
        out_specs=[col]*5,
        out_shape=[jax.ShapeDtypeStruct((t,d),BF)]*5,
        input_output_aliases={7+i:i for i in range(len(grads))},
        cost_estimate=COST,
        compiler_params=pltpu.CompilerParams(vmem_limit_bytes=48*2**20),
    )(q,k,v,ek,eq,dc,p,*grads)


NORM_EPS = 1e-7
SPLIT = 9


def norm_parts(v):
    mean = jnp.mean(v, axis=-1, keepdims=True)
    c = v - mean
    r = lax.rsqrt(jnp.mean(c * c, axis=-1, keepdims=True) + NORM_EPS)
    return c * r, r


def norm_back(g, gain, n, r):
    u = g * gain
    d = r * (u - jnp.mean(u, -1, keepdims=True) - n * jnp.mean(u * n, -1, keepdims=True))
    return d, jnp.sum(g * n, 0), jnp.sum(g, 0)


class Tree:
    def __init__(self, width):
        self.nf, self.ndp = lax.axis_size("fsdp"), lax.axis_size("dp")
        self.n = self.nf * self.ndp
        self.nz = self.ndp // 2
        self.rows = width // self.n
        self.width = width

    def place(self):
        me = lax.axis_index("dp") * self.nf + lax.axis_index("fsdp")
        d = lax.broadcasted_iota(jnp.int32, (self.width, self.width), 0)
        j = lax.broadcasted_iota(jnp.int32, (self.width, self.width), 1)
        rel = (d // self.rows) ^ me
        f = rel % self.nf
        core = (rel // self.nf) % 2
        z = rel // (2 * self.nf)
        at = ((core * self.nf + f) * self.nz + z) * self.rows + d % self.rows
        return (at == j).astype(BF)

    def swap(self, a, axis, bit):
        size = self.nf if axis == "fsdp" else self.ndp
        return lax.ppermute(a, axis, [(i, i ^ bit) for i in range(size)])

    def job(self, mine, flipped):
        return Job(self, mine, flipped)

    def core_sum(self, pairs):
        h = self.width // 2
        cat = lambda xs: xs[0] if len(xs) == 1 else jnp.concatenate(xs, 1)
        away = cat([mm(a[:, h:], b, 0, cb).astype(BF) for a, b, cb in pairs])
        got = self.swap(away, "dp", 1)
        mine = cat([mm(a[:, :h], b, 0, cb) for a, b, cb in pairs])
        return (mine + got.astype(F32)).astype(BF)


class Job:
    def __init__(self, tree, mine, flipped):
        self.tree = tree
        step = tree.nz * tree.rows
        self.parts = {i: mine[i * step : (i + 1) * step] for i in range(tree.nf)}
        bits = [1 << b for b in range(tree.nf.bit_length() - 1)]
        self.stages = [("fsdp", b) for b in (bits[::-1] if flipped else bits)]
        bit = 1
        while bit < tree.nz:
            self.stages.append(("dp", 2 * bit))
            bit *= 2

    def open(self):
        axis, bit = self.stages[0]
        if axis == "dp" and set(self.parts) == {0}:
            total = self.parts.pop(0)
            self.parts = {2 * i: total[i * self.tree.rows : (i + 1) * self.tree.rows] for i in range(self.tree.nz)}
            if self.tree.nz == 1:
                self.parts = {0: total}
        return [i for i in self.parts if i & bit]

    def send(self):
        axis, bit = self.stages[0]
        away = self.open()
        if axis == "dp":
            block = jnp.concatenate([self.parts[i] for i in away], 0) if len(away) > 1 else self.parts[away[0]]
            return [self.tree.swap(block, axis, bit)]
        return [self.tree.swap(self.parts[i], axis, bit) for i in away]

    def add(self, got):
        axis, bit = self.stages.pop(0)
        away = [i for i in self.parts if i & bit]
        if axis == "dp":
            got = [got[0][i * self.tree.rows : (i + 1) * self.tree.rows] for i in range(len(away))]
        last = not self.stages
        for i, g in zip(away, got):
            total = self.parts[i ^ bit].astype(F32) + g.astype(F32)
            self.parts[i ^ bit] = total if last else total.astype(BF)
            del self.parts[i]

    def hold(self, *others):
        keys = list(self.parts)
        out = lax.optimization_barrier((tuple(self.parts[i] for i in keys), others))
        self.parts = dict(zip(keys, out[0]))
        return out[1]

    def run(self):
        while self.stages:
            self.add(self.send())
        return self.parts[0]


def per_device(
    tokens, segment_ids, rel_bucket, query_weight, query_bias, key_weight, key_bias, value_weight, value_bias,
    out_weight, out_bias, attention_gain, attention_shift, up_weight, up_bias, down_weight, down_bias,
    output_gain, output_shift, position_table, cotangent,
):
    x = tokens[0]
    t, d = x.shape
    seg = segment_ids[0]
    tree = Tree(d)
    rows = tree.rows
    ff = up_weight.shape[1]
    spread = ff // d
    buckets = position_table.shape[0]
    scale = 1.0 / math.sqrt(3.0 * (d // HEADS))
    vectors = (query_bias, key_bias, value_bias, out_bias, attention_gain, attention_shift, down_bias, output_gain, output_shift)
    small = jnp.concatenate([v[:, None] for v in vectors] + [up_bias.reshape(spread, rows).T], axis=1).astype(BF)
    small = jnp.pad(small, ((0, 0), (0, 128 - small.shape[1])))
    first = jnp.concatenate(
        [query_weight.astype(BF), key_weight.astype(BF), value_weight.astype(BF), position_table.T.astype(BF), small], axis=1
    )
    second = jnp.concatenate([out_weight.T.astype(BF), up_weight.astype(BF), down_weight.T.astype(BF)], axis=1)
    w1 = lax.all_gather(first, ("dp", "fsdp"), axis=0, tiled=True)
    w2 = lax.all_gather(second, ("dp", "fsdp"), axis=0, tiled=True)
    wq, wk, wv = w1[:, :d], w1[:, d : 2 * d], w1[:, 2 * d : 3 * d]
    table_t = w1[:, 3 * d : 3 * d + buckets]
    vec = w1[:, 3 * d + buckets :].T.astype(F32)
    bq, bk, bv, bo, gain1, shift1, bd, gain2, shift2 = [vec[i] for i in range(SPLIT)]
    bu = vec[SPLIT : SPLIT + spread].reshape(spread, tree.n, rows).transpose(1, 0, 2).reshape(ff)
    wo_t, wu, wd_t = w2[:, :d], w2[:, d : d + ff], w2[:, d + ff :]

    half = t // 2
    picked = lax.rev(rel_bucket[t - half : 2 * t - half], (0,))
    onehot = (picked[:, None] == lax.broadcasted_iota(jnp.int32, (t, buckets), 1)).astype(BF)
    q = (mm(x, wq, 1, 0) + bq).astype(BF)
    k = (mm(x, wk, 1, 0) + bk).astype(BF)
    v = (mm(x, wv, 1, 0) + bv).astype(BF)
    spread_table = mm(onehot, table_t, 1, 1).astype(BF)
    ek = (mm(spread_table, wk, 1, 0) + bk).astype(BF)
    eq = (mm(spread_table, wq, 1, 0) + bq).astype(BF)
    context, probs = attend(q, k, v, ek, eq, seg, scale)

    place = tree.place()
    n1, r1 = norm_parts(x.astype(F32) + mm(context, wo_t, 1, 1) + bo)
    mixed = n1 * gain1 + shift1
    mixed_low = mixed.astype(BF)
    up = mm(mixed_low, wu, 1, 0) + bu
    cdf = 0.5 * (1.0 + lax.erf(up * math.sqrt(0.5)))
    act = (up * cdf).astype(BF)
    slope = cdf + up * (jnp.exp(-0.5 * up * up) * (1.0 / math.sqrt(2.0 * math.pi)))
    n2, r2 = norm_parts(mixed + mm(act, wd_t, 1, 1) + bd)
    layer_out = (n2 * gain2 + shift2).astype(BF)
    d_sum, d_gain2, d_shift2 = norm_back(cotangent[0].astype(F32), gain2, n2, r2)
    d_ffn = d_sum.astype(BF)
    d_bd = jnp.sum(d_ffn.astype(F32), 0)
    arrange = lambda m: mm(m, place, 1, 0).astype(BF)
    down_mine = tree.core_sum([(arrange(d_ffn), act, 0)])
    d_up = (mm(d_ffn, wd_t, 1, 0) * slope).astype(BF)
    d_bu = jnp.sum(d_up.astype(F32), 0)
    up_mine = tree.core_sum([(arrange(mixed_low), d_up, 0)])
    d_mixed = d_sum + mm(d_up, wu, 1, 1)
    d_first, d_gain1, d_shift1 = norm_back(d_mixed, gain1, n1, r1)
    d_attn = d_first.astype(BF)
    d_bo = jnp.sum(d_attn.astype(F32), 0)
    d_context = mm(d_attn, wo_t, 1, 0).astype(BF)
    out_mine = tree.core_sum([(arrange(d_attn), context, 0)])
    down, up_job, out_job = tree.job(down_mine, True), tree.job(up_mine, False), tree.job(out_mine, True)
    (d_context,) = down.hold(d_context)
    (d_context,) = up_job.hold(d_context)
    grads = attend_back(q, k, v, ek, eq, d_context, probs, scale, None, 0, 8)
    got_d, got_u = down.send(), up_job.send()
    grads, got_d, got_u = lax.optimization_barrier((grads, got_d, got_u))
    down.add(got_d)
    up_job.add(got_u)
    dq, dk, dv, dek, deq = grads
    d_pos_keys = mm(onehot, dek, 0, 0).astype(BF)
    d_pos_queries = mm(onehot, deq, 0, 0).astype(BF)
    colsum = lambda m: jnp.sum(m.astype(F32), 0)
    d_bq = colsum(dq) + colsum(d_pos_queries)
    d_bk = colsum(dk) + colsum(d_pos_keys)
    d_bv = colsum(dv)
    x_arranged = arrange(x)
    table_arranged = mm(table_t, place, 0, 0).astype(BF)
    left = jnp.concatenate([x_arranged, table_arranged], 0)
    d_table = (mm(d_pos_keys, wk, 1, 1) + mm(d_pos_queries, wq, 1, 1)).astype(BF)
    lines = jnp.stack([d_bq, d_bk, d_bv, d_bo, d_gain1, d_shift1, d_bd, d_gain2, d_shift2])
    lines = jnp.concatenate([lines, d_bu.reshape(tree.n, spread, rows).transpose(1, 0, 2).reshape(spread, d)], 0)
    lines = jnp.pad(lines, ((0, 128 - lines.shape[0]), (0, 0))).astype(BF)
    rest_mine = tree.core_sum([
        (left, jnp.concatenate([dq, d_pos_queries], 0), 0),
        (left, jnp.concatenate([dk, d_pos_keys], 0), 0),
        (x_arranged, dv, 0),
        (place, d_table, 1),
        (place, lines, 1),
    ])
    down_grad, up_grad, out_grad = down.run(), up_job.run(), out_job.run()
    rest = tree.job(rest_mine, False).run()
    input_grad = (d_first + mm(dq, wq, 1, 1) + mm(dk, wk, 1, 1) + mm(dv, wv, 1, 1)).astype(BF)
    tail = rest[:, 3 * d + buckets :]
    vecs = [tail[:, i] for i in range(SPLIT)]
    d_up_bias = tail[:, SPLIT : SPLIT + spread].T.reshape(-1)
    return (
        layer_out[None], input_grad[None],
        rest[:, :d], vecs[0], rest[:, d : 2 * d], vecs[1], rest[:, 2 * d : 3 * d], vecs[2],
        out_grad.T, vecs[3], vecs[4], vecs[5], up_grad, d_up_bias, down_grad.T, vecs[6], vecs[7], vecs[8],
        rest[:, 3 * d : 3 * d + buckets].T,
    )


def solution(mesh):
    both = ("dp", "fsdp")
    row, col, vec = P(both, None), P(None, both), P(both)
    seq = P(both, None, None)
    params = (row, vec, row, vec, row, vec, col, vec, vec, vec, row, vec, col, vec, vec, vec, col)
    return jax.shard_map(
        per_device, mesh=mesh, in_specs=(seq, row, P()) + params + (seq,), out_specs=(seq, seq) + params, check_vma=False
    )
```

```python
import math
import jax, jax.numpy as jnp
from jax import lax
from jax.sharding import PartitionSpec as P
import jax.experimental.pallas as pl, jax.experimental.pallas.tpu as pltpu
HEADS=16
BF=jnp.bfloat16
F32=jnp.float32
COST=pl.CostEstimate(flops=10**9,bytes_accessed=10**6,transcendentals=0)

def mm(a,b,ca,cb):
    return lax.dot_general(a,b,(((ca,),(cb,)),((),())),preferred_element_type=F32)

def attend_kernel(scale, q_ref,k_ref,v_ref,ek_ref,eq_ref,segc_ref,segr_ref,ctx_ref,p_ref):
    t=q_ref.shape[0]; half=t//2
    hd=q_ref.shape[1]//2
    same=segc_ref[...]==segr_ref[...]
    lane=lax.broadcasted_iota(jnp.int32,q_ref.shape,1)
    ctx=None
    for h in range(2):
        mine=(lane>=h*hd)&(lane<(h+1)*hd)
        pick=lambda r: jnp.where(mine,r[...],jnp.zeros((),BF))
        q=pick(q_ref); k=pick(k_ref)
        s=mm(q,k_ref[...],1,1)
        to=pltpu.roll(mm(q,ek_ref[...],1,1),half,1,stride=1,stride_axis=0)
        fr=pltpu.roll(mm(k,eq_ref[...],1,1),half,1,stride=1,stride_axis=0)
        s=jnp.where(same,s+to+fr.T,-1e30)
        top=jnp.max(s,axis=1,keepdims=True)
        e=jnp.exp((s-top)*scale)
        p=(e*(1.0/jnp.sum(e,axis=1,keepdims=True))).astype(BF)
        p_ref[h]=p
        part=mm(p,pick(v_ref),1,0)
        ctx=part if ctx is None else ctx+part
    ctx_ref[...]=ctx.astype(BF)

def attend(q,k,v,ek,eq,seg,scale,made,at,count):
    t,d=q.shape
    w=2*d//HEADS
    col=pl.BlockSpec((t,w),lambda i:(0,i+at))
    made=[] if made is None else list(made)
    return pl.pallas_call(
        lambda *r: attend_kernel(scale,*r[:7],*r[len(r)-2:]),
        grid=(count,),
        in_specs=[col]*5+[pl.BlockSpec((t,1),lambda i:(0,0)),pl.BlockSpec((1,t),lambda i:(0,0))]+[pl.BlockSpec(memory_space=pl.ANY)]*len(made),
        out_specs=[col,pl.BlockSpec((2,t,t),lambda i:(i+at,0,0))],
        out_shape=[jax.ShapeDtypeStruct((t,d),BF),jax.ShapeDtypeStruct((HEADS,t,t),BF)],
        input_output_aliases={7+i:i for i in range(len(made))},
        cost_estimate=COST,
        compiler_params=pltpu.CompilerParams(vmem_limit_bytes=48*2**20),
    )(q,k,v,ek,eq,seg.reshape(t,1),seg.reshape(1,t),*made)

def attend_back_kernel(scale,q_ref,k_ref,v_ref,ek_ref,eq_ref,dc_ref,p_ref,dq_ref,dk_ref,dv_ref,dek_ref,deq_ref):
    t=q_ref.shape[0]; half=t//2
    hd=q_ref.shape[1]//2
    r=lax.broadcasted_iota(jnp.int32,(half,half),0); c=lax.broadcasted_iota(jnp.int32,(half,half),1)
    flip=(r+c==half-1).astype(BF)
    lane=lax.broadcasted_iota(jnp.int32,q_ref.shape,1)
    def turn(x):
        return jnp.concatenate([mm(flip,x[:half],1,0),mm(flip,x[half:],1,0)],0)
    def turn_t(x):
        return jnp.concatenate([mm(flip,x[:,:half],1,1),mm(flip,x[:,half:],1,1)],0)
    def unroll(x):
        return jnp.concatenate([pltpu.roll(x[:half],1,1,stride=1,stride_axis=0),pltpu.roll(x[half:],half+1,1,stride=1,stride_axis=0)],0)
    q_turned=turn(q_ref[...]).astype(BF); k_turned=turn(k_ref[...]).astype(BF)
    dqt=dkt=dv=dek=deq=None
    plus=lambda a,b: b if a is None else a+b
    for h in range(2):
        mine=(lane>=h*hd)&(lane<(h+1)*hd)
        pick=lambda x: jnp.where(mine,x,jnp.zeros((),BF))
        p=p_ref[h]; dc=pick(dc_ref[...])
        dp=mm(dc,v_ref[...],1,1)
        pf=p.astype(F32)
        w=pf*dp
        ds=(w-pf*jnp.sum(w,axis=1,keepdims=True)).astype(BF)
        dv=plus(dv,mm(p,dc,0,0))
        a=turn(ds).astype(BF); au=unroll(a)
        b=turn_t(ds).astype(BF); bu=unroll(b)
        dqt=plus(dqt,mm(a,pick(k_ref[...]),1,0)+mm(au,pick(ek_ref[...]),1,0))
        dkt=plus(dkt,mm(b,pick(q_ref[...]),1,0)+mm(bu,pick(eq_ref[...]),1,0))
        dek=plus(dek,mm(au,pick(q_turned),0,0))
        deq=plus(deq,mm(bu,pick(k_turned),0,0))
    dq_ref[...]=turn((dqt*scale).astype(BF)).astype(BF)
    dk_ref[...]=turn((dkt*scale).astype(BF)).astype(BF)
    dv_ref[...]=dv.astype(BF)
    dek_ref[...]=(dek*scale).astype(BF)
    deq_ref[...]=(deq*scale).astype(BF)

def attend_back(q,k,v,ek,eq,dc,p,scale,grads,at,count):
    t,d=q.shape
    w=2*d//HEADS
    col=pl.BlockSpec((t,w),lambda i:(0,i+at))
    grads=[] if grads is None else list(grads)
    return pl.pallas_call(
        lambda *r: attend_back_kernel(scale,*r[:7],*r[len(r)-5:]),
        grid=(count,),
        in_specs=[col]*6+[pl.BlockSpec((2,t,t),lambda i:(i+at,0,0))]+[pl.BlockSpec(memory_space=pl.ANY)]*len(grads),
        out_specs=[col]*5,
        out_shape=[jax.ShapeDtypeStruct((t,d),BF)]*5,
        input_output_aliases={7+i:i for i in range(len(grads))},
        cost_estimate=COST,
        compiler_params=pltpu.CompilerParams(vmem_limit_bytes=48*2**20),
    )(q,k,v,ek,eq,dc,p,*grads)


NORM_EPS = 1e-7
SPLIT = 9
TILE = 512


def norm_parts(v):
    mean = jnp.mean(v, axis=-1, keepdims=True)
    c = v - mean
    r = lax.rsqrt(jnp.mean(c * c, axis=-1, keepdims=True) + NORM_EPS)
    return c * r, r


def norm_back(g, gain, n, r):
    u = g * gain
    d = r * (u - jnp.mean(u, -1, keepdims=True) - n * jnp.mean(u * n, -1, keepdims=True))
    return d, jnp.sum(g * n, 0, keepdims=True), jnp.sum(g, 0, keepdims=True)


def stack(refs):
    return jnp.concatenate([r[...] for r in refs], 0) if len(refs) > 1 else refs[0][...]


def whole(shape):
    return pl.BlockSpec(shape, lambda j: (0,) * len(shape))


def arrays(pieces):
    return [a for a, _ in pieces]


def piece_blocks(pieces, width, block):
    out = []
    for array, column in pieces:
        out.append(pl.BlockSpec((array.shape[0], width), lambda j, base=column // width: (0, base + block(j))))
    return out


def column_blocks(pieces, width, first, step=1):
    return piece_blocks(pieces, width, lambda j: first + step * j)


def feed_forward(vecs, bu, up, dn, first, count, start=None, end=None):
    opening = len(start) == 3 and isinstance(start[2], list)
    n = len(up)
    if opening:
        context, x, wo = start
        t, d = x.shape
        ins = [context, x] + [a for a, _ in wo]
        specs = [whole((t, d))] * 2 + column_blocks(wo, d, 0, 0)
    else:
        t, d = start[0].shape
        ins, specs = list(start), [whole((t, d))] * 3
    n_start = len(ins)
    ins += [vecs, bu] + [a for a, _ in up] + [a for a, _ in dn] + ([] if end is None else [end])
    specs += [whole(vecs.shape), pl.BlockSpec((1, TILE), lambda j: (0, j + first))]
    specs += column_blocks(up, TILE, 0) + column_blocks(dn, TILE, 0) + ([] if end is None else [whole((t, d))])
    shape = jax.ShapeDtypeStruct
    tile_out = pl.BlockSpec((t, TILE), lambda j: (0, j))
    outs = [(shape((t, count * TILE), BF), tile_out)] * 2
    full = lambda dt: (shape((t, d), dt), whole((t, d)))
    if opening:
        outs += [full(F32), (shape((t, 1), F32), whole((t, 1))), full(F32), full(BF)]
    if end is None:
        outs += [full(F32)]
    else:
        outs += [full(BF), full(F32), full(BF), (shape((8, d), F32), whole((8, d)))]

    def kernel(*refs):
        j = pl.program_id(0)
        begin, refs = refs[:n_start], refs[n_start:]
        vec_ref, bu_ref, refs = refs[0], refs[1], refs[2:]
        up_refs, dn_refs, refs = refs[:n], refs[n : 2 * n], refs[2 * n :]
        if end is not None:
            cot_ref, refs = refs[0], refs[1:]
        act_ref, slope_ref, refs = refs[0], refs[1], refs[2:]
        if opening:
            n1_ref, r1_ref, mixed_ref, low_ref = refs[:4]
            refs = refs[4:]
        else:
            mixed_ref, low_ref = begin[:2]
        acc = refs[-1]

        @pl.when(j == 0)
        def _():
            if opening:
                v = begin[1][...].astype(F32) + mm(begin[0][...], stack(begin[2:]), 1, 1) + vec_ref[0:1, :]
                n1, r1 = norm_parts(v)
                n1_ref[...] = n1
                r1_ref[...] = r1
                mixed = n1 * vec_ref[1:2, :] + vec_ref[2:3, :]
                mixed_ref[...] = mixed
                low_ref[...] = mixed.astype(BF)
                acc[...] = jnp.zeros(acc.shape, F32)
            else:
                acc[...] = begin[2][...]

        up_val = mm(low_ref[...], stack(up_refs), 1, 0) + bu_ref[...]
        cdf = 0.5 * (1.0 + lax.erf(up_val * math.sqrt(0.5)))
        act = (up_val * cdf).astype(BF)
        act_ref[...] = act
        slope_ref[...] = (cdf + up_val * (jnp.exp(-0.5 * up_val * up_val) * (1.0 / math.sqrt(2.0 * math.pi)))).astype(BF)
        acc[...] += mm(act, stack(dn_refs), 1, 1)

        @pl.when(j == count - 1)
        def _():
            if end is None:
                refs[0][...] = acc[...]
            else:
                out_ref, d_sum_ref, d_ffn_ref, sums_ref = refs[:4]
                n2, r2 = norm_parts(mixed_ref[...] + acc[...] + vec_ref[3:4, :])
                gain = vec_ref[4:5, :]
                out_ref[...] = (n2 * gain + vec_ref[5:6, :]).astype(BF)
                d_sum, d_gain, d_shift = norm_back(cot_ref[...].astype(F32), gain, n2, r2)
                d_sum_ref[...] = d_sum
                low = d_sum.astype(BF)
                d_ffn_ref[...] = low
                sums_ref[0:1, :] = jnp.sum(low.astype(F32), 0, keepdims=True)
                sums_ref[1:2, :] = d_gain
                sums_ref[2:3, :] = d_shift
                sums_ref[3:8, :] = jnp.zeros((5, d), F32)

    return pl.pallas_call(
        kernel, grid=(count,), in_specs=specs, out_specs=[o[1] for o in outs], out_shape=[o[0] for o in outs],
        scratch_shapes=[pltpu.VMEM((t, d), F32)], cost_estimate=COST,
        compiler_params=pltpu.CompilerParams(vmem_limit_bytes=56 * 2**20),
    )(*ins)


def split_out(tree, n):
    quarter = tree.width // 4
    spec = pl.BlockSpec((quarter, TILE), lambda j: (0, j))
    return [(jax.ShapeDtypeStruct((quarter, n), BF), spec)] * 2


def write_split(tree, flipped, away_ref, column, low_ref, high_ref, kept, value):
    step = tree.nz * tree.rows
    order = tree.f_order(flipped)
    half, quarter = tree.width // 2, tree.width // 4
    n = value.shape[1]
    for at, f in enumerate(order):
        row = at * step
        away_ref[row : row + step, pl.ds(column, n)] = value[half + f * step : half + (f + 1) * step].astype(BF)
        ref, row = (low_ref, row) if row < quarter else (high_ref, row - quarter)
        ref[row : row + step, pl.ds(kept, n)] = value[f * step : (f + 1) * step].astype(BF)


def feed_back(tree, d_ffn, mixed_low, act, slope, up, dn, total, count, tail=None):
    t, d = d_ffn.shape
    n = len(up)
    tile = pl.BlockSpec((t, TILE), lambda j: (0, j))
    ins = [d_ffn, mixed_low, act, slope, total] + [a for a, _ in up] + [a for a, _ in dn]
    specs = [whole((t, d))] * 2 + [tile] * 2 + [whole((t, d))] + column_blocks(up, TILE, 0) + column_blocks(dn, TILE, 0)
    shape = jax.ShapeDtypeStruct
    full = lambda dt: (shape((t, d), dt), whole((t, d)))
    n_up = count * TILE + (0 if tail is None else d)
    n_dn = count * TILE
    quarter = d // 4
    big = lambda r, c: (shape((r, c), BF), whole((r, c)))
    outs = [big(d // 2, n_up + n_dn), big(quarter, n_up), big(quarter, n_up), big(quarter, n_dn), big(quarter, n_dn)]
    outs += [(shape((1, count * TILE), F32), pl.BlockSpec((1, TILE), lambda j: (0, j)))]
    if tail is None:
        outs += [full(F32)]
    else:
        context, wo, n1, r1, gain = tail
        ins += [context, n1, r1, gain] + [a for a, _ in wo]
        specs += [whole((t, d)), whole((t, d)), whole((t, 1)), whole((1, d))] + column_blocks(wo, d, 0, 0)
        outs += [full(BF), full(BF), full(BF), (shape((8, d), F32), whole((8, d)))]

    def kernel(*refs):
        j = pl.program_id(0)
        d_ffn_ref, low_ref, act_ref, slope_ref, total_ref = refs[:5]
        refs = refs[5:]
        up_refs, dn_refs, refs = refs[:n], refs[n : 2 * n], refs[2 * n :]
        if tail is not None:
            ctx_ref, n1_ref, r1_ref, gain_ref = refs[:4]
            wo_refs, refs = refs[4 : 4 + n], refs[4 + n :]
        away_ref, up_lo, up_hi, dn_lo, dn_hi, d_bu_ref = refs[:6]
        refs = refs[6:]
        acc, d_ffn_t, low_t = refs[-3:]

        @pl.when(j == 0)
        def _():
            acc[...] = total_ref[...]
            d_ffn_t[...] = d_ffn_ref[...].T
            low_t[...] = low_ref[...].T

        d_up = (mm(d_ffn_ref[...], stack(dn_refs), 1, 0) * slope_ref[...].astype(F32)).astype(BF)
        d_bu_ref[...] = jnp.sum(d_up.astype(F32), 0, keepdims=True)
        at = pl.multiple_of(j * TILE, TILE)
        write_split(tree, True, away_ref, n_up + at, dn_lo, dn_hi, at, mm(d_ffn_t[...], act_ref[...], 1, 0))
        write_split(tree, False, away_ref, at, up_lo, up_hi, at, mm(low_t[...], d_up, 1, 0))
        acc[...] += mm(d_up, stack(up_refs), 1, 1)

        @pl.when(j == count - 1)
        def _():
            if tail is None:
                refs[0][...] = acc[...]
            else:
                d_attn_ref, rest_ref, d_ctx_ref, sums_ref = refs[:4]
                d_first, d_gain, d_shift = norm_back(acc[...], gain_ref[...], n1_ref[...], r1_ref[...])
                d_attn = d_first.astype(BF)
                d_attn_ref[...] = d_attn
                rest_ref[...] = (d_first - d_attn.astype(F32)).astype(BF)
                d_ctx_ref[...] = mm(d_attn, stack(wo_refs), 1, 0).astype(BF)
                d_ffn_t[...] = d_attn.T
                write_split(tree, False, away_ref, n_dn, up_lo, up_hi, n_dn, mm(d_ffn_t[...], ctx_ref[...], 1, 0))
                sums_ref[0:1, :] = jnp.sum(d_attn.astype(F32), 0, keepdims=True)
                sums_ref[1:2, :] = d_gain
                sums_ref[2:3, :] = d_shift
                sums_ref[3:8, :] = jnp.zeros((5, d), F32)

    return pl.pallas_call(
        kernel, grid=(count,), in_specs=specs, out_specs=[o[1] for o in outs], out_shape=[o[0] for o in outs],
        scratch_shapes=[pltpu.VMEM((t, d), F32), pltpu.VMEM((d, t), BF), pltpu.VMEM((d, t), BF)], cost_estimate=COST,
        compiler_params=pltpu.CompilerParams(vmem_limit_bytes=60 * 2**20),
    )(*ins)


def project(x_p, onehot, low, high, bias, tile):
    t, d = x_p.shape
    buckets = onehot.shape[1]
    n = len(low)
    per = d // tile
    clip = lambda j, a: jnp.clip(j - a * per, 0, per - 1)
    specs = [whole((t, d)), whole(onehot.shape), pl.BlockSpec((1, tile), lambda j: (0, j))]
    specs += piece_blocks(low, tile, lambda j: jnp.minimum(j, 2 * per - 1))
    specs += piece_blocks(high, tile, lambda j: clip(j, 2))
    specs += piece_blocks(high, buckets, lambda j: d // buckets)
    out = lambda a: pl.BlockSpec((t, tile), lambda j: (0, clip(j, a)))

    def kernel(x_ref, hot_ref, bias_ref, *refs):
        lows, highs, tables, refs = refs[:n], refs[n : 2 * n], refs[2 * n : 3 * n], refs[3 * n :]
        q_ref, k_ref, v_ref, ek_ref, eq_ref, table = refs
        j = pl.program_id(0)

        @pl.when(j == 0)
        def _():
            table[...] = mm(hot_ref[...], stack(tables), 1, 1).astype(BF)

        def both(out_ref, e_ref):
            w = stack(lows)
            out_ref[...] = (mm(x_ref[...], w, 1, 0) + bias_ref[...]).astype(BF)
            e_ref[...] = (mm(table[...], w, 1, 0) + bias_ref[...]).astype(BF)

        pl.when(j < per)(lambda: both(q_ref, eq_ref))
        pl.when((j >= per) & (j < 2 * per))(lambda: both(k_ref, ek_ref))

        @pl.when(j >= 2 * per)
        def _():
            v_ref[...] = (mm(x_ref[...], stack(highs), 1, 0) + bias_ref[...]).astype(BF)

    return pl.pallas_call(
        kernel, grid=(3 * per,), in_specs=specs, out_specs=[out(0), out(1), out(2), out(1), out(0)],
        out_shape=[jax.ShapeDtypeStruct((t, d), BF)] * 5, scratch_shapes=[pltpu.VMEM((t, d), BF)], cost_estimate=COST,
        compiler_params=pltpu.CompilerParams(vmem_limit_bytes=48 * 2**20),
    )(x_p, onehot, bias, *arrays(low), *arrays(high), *arrays(high))


def attention_grads(tree, x_p, onehot, low, high, dq, dk, dv, dek, deq, lines, ordered, place_t, tile):
    t, d = x_p.shape
    buckets = onehot.shape[1]
    n = len(low)
    per = d // tile
    clip = lambda j, a: jnp.clip(j - a * per, 0, per - 1)
    half = d // 2
    col = lambda a: pl.BlockSpec((t, tile), lambda j: (0, clip(j, a)))
    specs = [whole((t, d)), whole(onehot.shape), col(0), col(1), col(2), col(1), col(0)]
    specs += [whole(lines.shape), whole(ordered.shape), whole((d, d))]
    specs += piece_blocks(low, tile, lambda j: jnp.minimum(j, 2 * per - 1))
    specs += piece_blocks(high, buckets, lambda j: d // buckets)
    wide = d + buckets + 128
    shape = jax.ShapeDtypeStruct
    quarter = d // 4
    big = lambda r, c: (shape((r, c), BF), whole((r, c)))
    outs = [big(half, 2 * d + wide), big(quarter, 2 * d), big(quarter, 2 * d), big(quarter, wide), big(quarter, wide)]

    def kernel(*refs):
        x_ref, hot_ref, dq_ref, dk_ref, dv_ref, dek_ref, deq_ref, lines_ref, ordered_ref, place_ref = refs[:10]
        lows, tables, refs = refs[10 : 10 + n], refs[10 + n : 10 + 2 * n], refs[10 + 2 * n :]
        away_ref, qk_lo, qk_hi, wide_lo, wide_hi = refs[:5]
        x_t, table, d_table, sums = refs[5:]
        j = pl.program_id(0)

        @pl.when(j == 0)
        def _():
            x_t[...] = x_ref[...].T
            table[...] = stack(tables)
            d_table[...] = jnp.zeros(d_table.shape, F32)

        def wide_write(at, value):
            write_split(tree, True, away_ref, 2 * d + at, wide_lo, wide_hi, at, value)

        def both(g_ref, e_ref, row, at):
            pos = mm(hot_ref[...], e_ref[...], 0, 0).astype(BF)
            g = g_ref[...]
            value = mm(x_t[...], g, 1, 0) + mm(table[...], pos, 1, 0)
            write_split(tree, False, away_ref, row * d + at, qk_lo, qk_hi, row * d + at, value)
            sums[row : row + 1, at : at + tile] = jnp.sum(g.astype(F32), 0, keepdims=True) + jnp.sum(
                pos.astype(F32), 0, keepdims=True
            )
            d_table[...] += mm(stack(lows), pos, 1, 1)

        for c in range(per):
            pl.when(j == c)(lambda c=c: both(dq_ref, deq_ref, 0, c * tile))
            pl.when(j == per + c)(lambda c=c: both(dk_ref, dek_ref, 1, c * tile))

            @pl.when(j == 2 * per + c)
            def _(c=c):
                g = dv_ref[...]
                wide_write(c * tile, mm(x_t[...], g, 1, 0))
                sums[2:3, c * tile : (c + 1) * tile] = jnp.sum(g.astype(F32), 0, keepdims=True)

        @pl.when(j == 3 * per - 1)
        def _():
            wide_write(d, d_table[...])
            vectors = jnp.concatenate([sums[0:3, :], lines_ref[...]], 0)
            pad = lambda v, lead: jnp.concatenate(
                ([jnp.zeros((lead, d), F32)] if lead else []) + [v, jnp.zeros((128 - lead - v.shape[0], d), F32)], 0
            )
            natural = mm(place_ref[...], pad(vectors, 0).astype(BF), 1, 1)
            wide_write(d + buckets, natural + pad(ordered_ref[...], 16).T)

    return pl.pallas_call(
        kernel, grid=(3 * per,), in_specs=specs, out_specs=[o[1] for o in outs], out_shape=[o[0] for o in outs],
        scratch_shapes=[
            pltpu.VMEM((d, t), BF), pltpu.VMEM((d, buckets), BF), pltpu.VMEM((d, buckets), F32), pltpu.VMEM((8, d), F32),
        ],
        cost_estimate=COST, compiler_params=pltpu.CompilerParams(vmem_limit_bytes=56 * 2**20),
    )(x_p, onehot, dq, dk, dv, dek, deq, lines, ordered, place_t, *arrays(low), *arrays(high))


def input_grads(d_attn, d_rest, low, high, dq, dk, dv, out_p, place_t, tile):
    t, d = d_attn.shape
    n = len(low)
    per = d // tile
    clip = lambda j, a: jnp.clip(j - a * per, 0, per - 1)
    col = lambda a: pl.BlockSpec((t, tile), lambda j: (0, clip(j, a)))
    specs = [whole((t, d)), whole((t, d)), col(0), col(1), col(2), whole((t, d)), whole((d, d))]
    specs += piece_blocks(low, tile, lambda j: jnp.minimum(j, 2 * per - 1))
    specs += piece_blocks(high, tile, lambda j: clip(j, 2))

    def kernel(*refs):
        a_ref, r_ref, dq_ref, dk_ref, dv_ref, out_ref, place_ref = refs[:7]
        lows, highs, refs = refs[7 : 7 + n], refs[7 + n : 7 + 2 * n], refs[7 + 2 * n :]
        grad_ref, layer_ref, acc = refs
        j = pl.program_id(0)

        @pl.when(j == 0)
        def _():
            acc[...] = a_ref[...].astype(F32) + r_ref[...].astype(F32)
            layer_ref[...] = mm(out_ref[...], place_ref[...], 1, 0).astype(BF)

        def add(g_ref, ws):
            acc[...] += mm(g_ref[...], stack(ws), 1, 1)

        pl.when(j < per)(lambda: add(dq_ref, lows))
        pl.when((j >= per) & (j < 2 * per))(lambda: add(dk_ref, lows))
        pl.when(j >= 2 * per)(lambda: add(dv_ref, highs))

        @pl.when(j == 3 * per - 1)
        def _():
            grad_ref[...] = mm(acc[...].astype(BF), place_ref[...], 1, 0).astype(BF)

    return pl.pallas_call(
        kernel, grid=(3 * per,), in_specs=specs, out_specs=[whole((t, d))] * 2,
        out_shape=[jax.ShapeDtypeStruct((t, d), BF)] * 2, scratch_shapes=[pltpu.VMEM((t, d), F32)], cost_estimate=COST,
        compiler_params=pltpu.CompilerParams(vmem_limit_bytes=48 * 2**20),
    )(d_attn, d_rest, dq, dk, dv, out_p, place_t, *arrays(low), *arrays(high))


class Tree:
    def __init__(self, width):
        self.nf, self.ndp = lax.axis_size("fsdp"), lax.axis_size("dp")
        self.n = self.nf * self.ndp
        self.nz = self.ndp // 2
        self.rows = width // self.n
        self.width = width
        self.f_bits = [1 << b for b in range(self.nf.bit_length() - 1)]
        self.z_bits = [1 << b for b in range(self.nz.bit_length() - 1)]

    def place(self, transposed):
        me = lax.axis_index("dp") * self.nf + lax.axis_index("fsdp")
        d = jnp.arange(self.width, dtype=jnp.int32)
        rel = (d // self.rows) ^ me
        f = rel % self.nf
        core = (rel // self.nf) % 2
        z = sum(((rel // (2 * self.nf * b)) % 2) * (self.nz // (2 * b)) for b in self.z_bits)
        at = ((core * self.nf + f) * self.nz + z) * self.rows + d % self.rows
        j = lax.broadcasted_iota(jnp.int32, (self.width, self.width), 0 if transposed else 1)
        return ((at[None, :] if transposed else at[:, None]) == j).astype(BF)

    def swap(self, a, axis, bit):
        size = self.nf if axis == "fsdp" else self.ndp
        return lax.ppermute(a, axis, [(i, i ^ bit) for i in range(size)])

    def f_order(self, flipped):
        order = self.f_bits[::-1] if flipped else self.f_bits
        key = lambda f: [f & bit != 0 for bit in order]
        return sorted(range(self.nf), key=key)

    def gather(self, sides):
        cur = jnp.concatenate([a for a, _ in sides], 1)
        columns = [0]
        for a, _ in sides:
            columns.append(columns[-1] + a.shape[1])
        for bit in self.z_bits[::-1]:
            (got,) = yield [self.swap(cur, "dp", 2 * bit)]
            cur = jnp.concatenate([cur, got], 0)
        found = [{0: (cur, c)} for c in columns[:-1]]
        orders = [self.f_bits[::-1] if flipped else self.f_bits for _, flipped in sides]

        def keep(keys, array, whole_row):
            for s, i in keys:
                found[s][i] = (array, columns[s] if whole_row else 0)

        every = range(len(sides))
        sends = [([(s, bit) for s in every], True, self.swap(cur, "fsdp", bit)) for bit in self.f_bits]
        cores = [([(s, self.nf) for s in every], True, self.swap(cur, "dp", 1))]
        level = 1
        while sends or cores:
            got = yield [x for _, _, x in sends + cores]
            for (keys, whole_row, _), g in zip(sends + cores, got):
                keep(keys, g, whole_row)
            arrived, sends, cores = sends, [], []
            for keys, whole_row, _ in arrived:
                i = keys[0][1]
                cores.append(([(s, self.nf + i) for s, _ in keys], whole_row, self.swap(found[keys[0][0]][i][0], "dp", 1)))
                for s, _ in keys:
                    array, column = found[s][i]
                    last = max(at for at, bit in enumerate(orders[s]) if i & bit)
                    for bit in orders[s][last + 1 :]:
                        part = array[:, column : column + columns[s + 1] - columns[s]]
                        sends.append(([(s, i | bit)], False, self.swap(part, "fsdp", bit)))
            level += 1
        return [[f[i] for i in range(2 * self.nf)] for f in found]


class Job:
    def __init__(self, tree, away, *sides):
        self.tree = tree
        self.away = away
        self.sides = [list(sides[:2]), list(sides[2:])]
        self.stages = ["core"] + list(range(len(tree.f_bits))) + [("z", b) for b in tree.z_bits]
        self.total = None

    def send(self):
        stage = self.stages[0]
        if stage == "core":
            return [self.tree.swap(self.away, "dp", 1)]
        if isinstance(stage, int):
            bits = self.tree.f_bits
            return [self.tree.swap(side[1], "fsdp", b[stage]) for side, b in zip(self.sides, (bits, bits[::-1]))]
        return [self.tree.swap(self.total[1], "dp", 2 * stage[1])]

    def add(self, got):
        stage = self.stages.pop(0)
        more = bool(self.stages)
        sums = lambda a, g: (a.astype(F32) + g.astype(F32)).astype(BF)
        if stage == "core":
            column = 0
            for side in self.sides:
                r, n = side[0].shape
                side[0] = sums(side[0], got[0][:r, column : column + n])
                side[1] = sums(side[1], got[0][r:, column : column + n])
                column += n
        elif isinstance(stage, int):
            for side, g in zip(self.sides, got):
                r = side[0].shape[0] // 2
                side[0], side[1] = sums(side[0][:r], g[:r]), sums(side[0][r:], g[r:])
            if not isinstance(self.stages[0], int):
                self.total = [jnp.concatenate([side[i] for side in self.sides], 1) for i in range(2)]
        else:
            keep = self.total[0]
            if more:
                r = keep.shape[0] // 2
                self.total = [sums(keep[:r], got[0][:r]), sums(keep[r:], got[0][r:])]
            else:
                self.total = keep.astype(F32) + got[0].astype(F32)

    def run(self):
        while self.stages:
            self.add(self.send())
        return self.total


class Flow:
    def __init__(self, steps):
        self.steps = steps
        self.value = None
        self.sends = next(steps)

    def take(self, got):
        try:
            self.sends = self.steps.send(got)
        except StopIteration as end:
            self.sends, self.value = [], end.value


def drain(flow):
    while flow.value is None:
        window([flow])


def window(flows, jobs=(), others=()):
    flows = [f for f in flows if f.value is None]
    jobs = [j for j in jobs if j.stages]
    sent = [list(f.sends) for f in flows] + [j.send() for j in jobs]
    sent, others = lax.optimization_barrier((sent, tuple(others)))
    for f, got in zip(flows, sent):
        f.take(list(got))
    for j, got in zip(jobs, sent[len(flows):]):
        j.add(list(got))
    return others


def per_device(
    tokens, segment_ids, rel_bucket, query_weight, query_bias, key_weight, key_bias, value_weight, value_bias,
    out_weight, out_bias, attention_gain, attention_shift, up_weight, up_bias, down_weight, down_bias,
    output_gain, output_shift, position_table, cotangent,
):
    x = tokens[0]
    t, d = x.shape
    seg = segment_ids[0]
    tree = Tree(d)
    rows = tree.rows
    ff = up_weight.shape[1]
    spread = ff // d
    buckets = position_table.shape[0]
    scale = 1.0 / math.sqrt(3.0 * (d // HEADS))
    vectors = (query_bias, key_bias, value_bias, out_bias, attention_gain, attention_shift, down_bias, output_gain, output_shift)
    small = jnp.concatenate([v[:, None] for v in vectors] + [up_bias.reshape(spread, rows).T], axis=1).astype(BF)
    small = jnp.pad(small, ((0, 0), (0, 128 - small.shape[1])))
    rest_cols = jnp.concatenate([value_weight.astype(BF), position_table.T.astype(BF), small], axis=1)
    query_key = jnp.concatenate([query_weight.astype(BF), key_weight.astype(BF)], axis=1)
    down_t = down_weight.T.astype(BF)
    cut = ff // 2
    out_up = jnp.concatenate([out_weight.T.astype(BF), up_weight[:, :cut].astype(BF)], axis=1)
    one = Flow(tree.gather([(query_key, False), (rest_cols, True)]))
    two = Flow(tree.gather([(out_up, False), (down_t[:, :cut], True)]))
    three = Flow(tree.gather([(up_weight[:, cut:].astype(BF), False), (down_t[:, cut:], True)]))

    place = tree.place(False)
    place_t = tree.place(True)
    half = t // 2
    picked = lax.rev(rel_bucket[t - half : 2 * t - half], (0,))
    onehot = (picked[:, None] == lax.broadcasted_iota(jnp.int32, (t, buckets), 1)).astype(BF)
    place, place_t, onehot = window([one], (), (place, place_t, onehot))
    arrange = lambda m: mm(m, place, 1, 0).astype(BF)
    x_p = arrange(x)
    (x_p,) = window([one, two], (), (x_p,))
    cot_p = arrange(cotangent[0])
    (cot_p,) = window([one, two], (), (cot_p,))
    window([one, three])
    drain(one)
    low, high = one.value

    small = jnp.concatenate([a[:, c + d + buckets : c + d + buckets + 128] for a, c in high], 0)
    vec = mm(small, place, 0, 1)
    vecs = small.T[3:11].astype(F32)
    bias = vec[:3].reshape(1, 3 * d)
    bu = vec[SPLIT : SPLIT + spread].reshape(spread, tree.n, rows).transpose(1, 0, 2).reshape(1, ff)
    q, k, v, ek, eq = project(x_p, onehot, low, high, bias, TILE)
    q, k, v, ek, eq = window([two, three], (), (q, k, v, ek, eq))
    n_pairs = HEADS // 2
    made = attend(q, k, v, ek, eq, seg, scale, None, 0, n_pairs // 2)
    made = window([two, three], (), made)
    made = attend(q, k, v, ek, eq, seg, scale, made, n_pairs // 2, n_pairs // 2)
    context, probs = window([two, three], (), made)

    drain(two)
    wo = two.value[0]
    shifted = lambda pieces, by: [(a, c + by) for a, c in pieces]
    up_a, dn_a = shifted(wo, d), two.value[1]
    count = cut // TILE
    act_a, slope_a, n1, r1, mixed, mixed_low, so_far = feed_forward(vecs, bu, up_a, dn_a, 0, count, (context, x_p, wo))
    (so_far,) = window([three], (), (so_far,))
    drain(three)
    up_b, dn_b = three.value
    act_b, slope_b, out_p, d_sum, d_ffn, sums2 = feed_forward(
        vecs, bu, up_b, dn_b, count, count, (mixed, mixed_low, so_far), cot_p
    )
    back = feed_back(tree, d_ffn, mixed_low, act_a, slope_a, up_a, dn_a, d_sum, count)
    job_1 = Job(tree, *back[:5])
    d_bu_a, total = back[5:]
    back = feed_back(
        tree, d_ffn, mixed_low, act_b, slope_b, up_b, dn_b, total, count, (context, wo, n1, r1, vecs[1:2])
    )
    job_2 = Job(tree, *back[:5])
    d_bu_b, d_attn, d_rest, d_context, sums1 = back[5:]
    (d_context,) = window([], [job_1], (d_context,))

    args = (q, k, v, ek, eq, d_context, probs, scale)
    grads = attend_back(*args, None, 0, n_pairs // 2)
    grads = window([], [job_1, job_2], grads)
    grads = attend_back(*args, grads, n_pairs // 2, n_pairs // 2)
    dq, dk, dv, dek, deq = window([], [job_1, job_2], grads)
    d_bu = jnp.concatenate([d_bu_a, d_bu_b], 1)
    lines = d_bu.reshape(tree.n, spread, rows).transpose(1, 0, 2).reshape(spread, d)
    ordered = jnp.concatenate([sums1[:3], sums2[:3]], 0)
    ordered = jnp.concatenate([ordered, jnp.zeros((2, d), F32)], 0)
    split = attention_grads(tree, x_p, onehot, low, high, dq, dk, dv, dek, deq, lines, ordered, place_t, TILE)
    split = window([], [job_1, job_2], split)
    job_3 = Job(tree, *split)
    d_attn, d_rest = window([], [job_3], (d_attn, d_rest))
    grad_layer = input_grads(d_attn, d_rest, low, high, dq, dk, dv, out_p, place_t, TILE)
    input_grad, layer_out = window([], [job_1, job_2, job_3], grad_layer)
    one, two, three = [job.run() for job in (job_1, job_2, job_3)]
    up_a_grad, dn_a_grad = one[:, :cut], one[:, cut:]
    up_b_grad, out_grad, dn_b_grad = two[:, :cut], two[:, cut : cut + d], two[:, cut + d :]
    rest_a, rest_b = three[:, : 2 * d], three[:, 2 * d :]
    tail = rest_b[:, d + buckets :]
    d_bq, d_bk, d_bv = [tail[:, i] for i in range(3)]
    d_up_bias = tail[:, 3 : 3 + spread].T.reshape(-1)
    d_bo, d_gain1, d_shift1, d_bd, d_gain2, d_shift2 = [tail[:, 16 + i] for i in range(6)]
    return (
        layer_out[None], input_grad[None],
        rest_a[:, :d], d_bq, rest_a[:, d:], d_bk, rest_b[:, :d], d_bv,
        out_grad.T, d_bo, d_gain1, d_shift1, jnp.concatenate([up_a_grad, up_b_grad], 1), d_up_bias,
        jnp.concatenate([dn_a_grad.T, dn_b_grad.T], 0), d_bd, d_gain2, d_shift2,
        rest_b[:, d : d + buckets].T,
    )


def solution(mesh):
    both = ("dp", "fsdp")
    row, col, vec = P(both, None), P(None, both), P(both)
    seq = P(both, None, None)
    params = (row, vec, row, vec, row, vec, col, vec, vec, vec, row, vec, col, vec, vec, vec, col)
    return jax.shard_map(
        per_device, mesh=mesh, in_specs=(seq, row, P()) + params + (seq,), out_specs=(seq, seq) + params, check_vma=False
    )
```

```python
import math
import jax, jax.numpy as jnp
from jax import lax
from jax.sharding import PartitionSpec as P
import jax.experimental.pallas as pl, jax.experimental.pallas.tpu as pltpu
HEADS=16
BF=jnp.bfloat16
F32=jnp.float32
COST=pl.CostEstimate(flops=10**9,bytes_accessed=10**6,transcendentals=0)

def mm(a,b,ca,cb):
    return lax.dot_general(a,b,(((ca,),(cb,)),((),())),preferred_element_type=F32)

def attend_kernel(scale, q_ref,k_ref,v_ref,ek_ref,eq_ref,segc_ref,segr_ref,ctx_ref,p_ref):
    t=q_ref.shape[0]; half=t//2
    hd=q_ref.shape[1]//2
    same=segc_ref[...]==segr_ref[...]
    lane=lax.broadcasted_iota(jnp.int32,q_ref.shape,1)
    ctx=None
    for h in range(2):
        mine=(lane>=h*hd)&(lane<(h+1)*hd)
        pick=lambda r: jnp.where(mine,r[...],jnp.zeros((),BF))
        q=pick(q_ref); k=pick(k_ref)
        s=mm(q,k_ref[...],1,1)
        to=pltpu.roll(mm(q,ek_ref[...],1,1),half,1,stride=1,stride_axis=0)
        fr=pltpu.roll(mm(k,eq_ref[...],1,1),half,1,stride=1,stride_axis=0)
        s=jnp.where(same,s+to+fr.T,-1e30)
        top=jnp.max(s,axis=1,keepdims=True)
        e=jnp.exp((s-top)*scale)
        p=(e*(1.0/jnp.sum(e,axis=1,keepdims=True))).astype(BF)
        p_ref[h]=p
        part=mm(p,pick(v_ref),1,0)
        ctx=part if ctx is None else ctx+part
    ctx_ref[...]=ctx.astype(BF)

def attend(q,k,v,ek,eq,seg,scale,made,at,count):
    t,d=q.shape
    w=2*d//HEADS
    col=pl.BlockSpec((t,w),lambda i:(0,i+at))
    made=[] if made is None else list(made)
    return pl.pallas_call(
        lambda *r: attend_kernel(scale,*r[:7],*r[len(r)-2:]),
        grid=(count,),
        in_specs=[col]*5+[pl.BlockSpec((t,1),lambda i:(0,0)),pl.BlockSpec((1,t),lambda i:(0,0))]+[pl.BlockSpec(memory_space=pl.ANY)]*len(made),
        out_specs=[col,pl.BlockSpec((2,t,t),lambda i:(i+at,0,0))],
        out_shape=[jax.ShapeDtypeStruct((t,d),BF),jax.ShapeDtypeStruct((HEADS,t,t),BF)],
        input_output_aliases={7+i:i for i in range(len(made))},
        cost_estimate=COST,
        compiler_params=pltpu.CompilerParams(vmem_limit_bytes=60 * 2**20),
    )(q,k,v,ek,eq,seg.reshape(t,1),seg.reshape(1,t),*made)

def attend_back_kernel(scale,q_ref,k_ref,v_ref,ek_ref,eq_ref,dc_ref,p_ref,dq_ref,dk_ref,dv_ref,dek_ref,deq_ref):
    t=q_ref.shape[0]; half=t//2
    hd=q_ref.shape[1]//2
    r=lax.broadcasted_iota(jnp.int32,(half,half),0); c=lax.broadcasted_iota(jnp.int32,(half,half),1)
    flip=(r+c==half-1).astype(BF)
    lane=lax.broadcasted_iota(jnp.int32,q_ref.shape,1)
    def turn(x):
        return jnp.concatenate([mm(flip,x[:half],1,0),mm(flip,x[half:],1,0)],0)
    def turn_t(x):
        return jnp.concatenate([mm(flip,x[:,:half],1,1),mm(flip,x[:,half:],1,1)],0)
    def unroll(x):
        return jnp.concatenate([pltpu.roll(x[:half],1,1,stride=1,stride_axis=0),pltpu.roll(x[half:],half+1,1,stride=1,stride_axis=0)],0)
    q_turned=turn(q_ref[...]).astype(BF); k_turned=turn(k_ref[...]).astype(BF)
    dqt=dkt=dv=dek=deq=None
    plus=lambda a,b: b if a is None else a+b
    for h in range(2):
        mine=(lane>=h*hd)&(lane<(h+1)*hd)
        pick=lambda x: jnp.where(mine,x,jnp.zeros((),BF))
        p=p_ref[h]; dc=pick(dc_ref[...])
        dp=mm(dc,v_ref[...],1,1)
        pf=p.astype(F32)
        w=pf*dp
        ds=(w-pf*jnp.sum(w,axis=1,keepdims=True)).astype(BF)
        dv=plus(dv,mm(p,dc,0,0))
        a=turn(ds).astype(BF); au=unroll(a)
        b=turn_t(ds).astype(BF); bu=unroll(b)
        dqt=plus(dqt,mm(a,pick(k_ref[...]),1,0)+mm(au,pick(ek_ref[...]),1,0))
        dkt=plus(dkt,mm(b,pick(q_ref[...]),1,0)+mm(bu,pick(eq_ref[...]),1,0))
        dek=plus(dek,mm(au,pick(q_turned),0,0))
        deq=plus(deq,mm(bu,pick(k_turned),0,0))
    dq_ref[...]=turn((dqt*scale).astype(BF)).astype(BF)
    dk_ref[...]=turn((dkt*scale).astype(BF)).astype(BF)
    dv_ref[...]=dv.astype(BF)
    dek_ref[...]=(dek*scale).astype(BF)
    deq_ref[...]=(deq*scale).astype(BF)

def attend_back(q,k,v,ek,eq,dc,p,scale,grads,at,count):
    t,d=q.shape
    w=2*d//HEADS
    col=pl.BlockSpec((t,w),lambda i:(0,i+at))
    grads=[] if grads is None else list(grads)
    return pl.pallas_call(
        lambda *r: attend_back_kernel(scale,*r[:7],*r[len(r)-5:]),
        grid=(count,),
        in_specs=[col]*6+[pl.BlockSpec((2,t,t),lambda i:(i+at,0,0))]+[pl.BlockSpec(memory_space=pl.ANY)]*len(grads),
        out_specs=[col]*5,
        out_shape=[jax.ShapeDtypeStruct((t,d),BF)]*5,
        input_output_aliases={7+i:i for i in range(len(grads))},
        cost_estimate=COST,
        compiler_params=pltpu.CompilerParams(vmem_limit_bytes=60 * 2**20),
    )(q,k,v,ek,eq,dc,p,*grads)


NORM_EPS = 1e-7
SPLIT = 9
TILE = 512
WIDE = 512


def norm_parts(v):
    mean = jnp.mean(v, axis=-1, keepdims=True)
    c = v - mean
    r = lax.rsqrt(jnp.mean(c * c, axis=-1, keepdims=True) + NORM_EPS)
    return c * r, r


def norm_back(g, gain, n, r):
    u = g * gain
    d = r * (u - jnp.mean(u, -1, keepdims=True) - n * jnp.mean(u * n, -1, keepdims=True))
    return d, jnp.sum(g * n, 0, keepdims=True), jnp.sum(g, 0, keepdims=True)


def stack(refs):
    return jnp.concatenate([r[...] for r in refs], 0) if len(refs) > 1 else refs[0][...]


def whole(shape):
    return pl.BlockSpec(shape, lambda j: (0,) * len(shape))


def join(blocks):
    rows, n = blocks[0].shape
    if rows % 16:
        return jnp.concatenate(blocks, 0)

    def kernel(*refs):
        for i, r in enumerate(refs[:-1]):
            refs[-1][i * rows : (i + 1) * rows, :] = r[...]

    return pl.pallas_call(
        kernel, out_shape=jax.ShapeDtypeStruct((rows * len(blocks), n), BF), cost_estimate=COST,
        compiler_params=pltpu.CompilerParams(vmem_limit_bytes=32 * 2**20),
    )(*blocks)


def arrays(pieces):
    return [a for a, _ in pieces]


def piece_blocks(pieces, width, block):
    out = []
    for array, column in pieces:
        out.append(pl.BlockSpec((array.shape[0], width), lambda j, base=column // width: (0, base + block(j))))
    return out


def column_blocks(pieces, width, first, step=1):
    return piece_blocks(pieces, width, lambda j: first + step * j)


def feed_forward(vecs, bu, up, dn, first, count, start=None, end=None):
    opening = len(start) == 3 and isinstance(start[2], list)
    n = len(up)
    if opening:
        context, x, wo = start
        t, d = x.shape
        ins = [context, x] + [a for a, _ in wo]
        specs = [whole((t, d))] * 2 + column_blocks(wo, d, 0, 0)
    else:
        t, d = start[0].shape
        ins, specs = list(start), [whole((t, d))] * 3
    n_start = len(ins)
    ins += [vecs, bu] + [a for a, _ in up] + [a for a, _ in dn] + ([] if end is None else [end])
    specs += [whole(vecs.shape), pl.BlockSpec((1, WIDE), lambda j: (0, j + first))]
    specs += column_blocks(up, WIDE, 0) + column_blocks(dn, WIDE, 0) + ([] if end is None else [whole((t, d))])
    shape = jax.ShapeDtypeStruct
    tile_out = pl.BlockSpec((t, WIDE), lambda j: (0, j))
    outs = [(shape((t, count * WIDE), BF), tile_out)] * 2
    full = lambda dt: (shape((t, d), dt), whole((t, d)))
    if opening:
        outs += [full(F32), (shape((t, 1), F32), whole((t, 1))), full(F32), full(BF)]
    if end is None:
        outs += [full(F32)]
    else:
        outs += [full(BF), full(F32), full(BF), (shape((8, d), F32), whole((8, d)))]

    def kernel(*refs):
        j = pl.program_id(0)
        begin, refs = refs[:n_start], refs[n_start:]
        vec_ref, bu_ref, refs = refs[0], refs[1], refs[2:]
        up_refs, dn_refs, refs = refs[:n], refs[n : 2 * n], refs[2 * n :]
        if end is not None:
            cot_ref, refs = refs[0], refs[1:]
        act_ref, slope_ref, refs = refs[0], refs[1], refs[2:]
        if opening:
            n1_ref, r1_ref, mixed_ref, low_ref = refs[:4]
            refs = refs[4:]
        else:
            mixed_ref, low_ref = begin[:2]
        acc = refs[-1]

        @pl.when(j == 0)
        def _():
            if opening:
                v = begin[1][...].astype(F32) + mm(begin[0][...], stack(begin[2:]), 1, 1) + vec_ref[0:1, :]
                n1, r1 = norm_parts(v)
                n1_ref[...] = n1
                r1_ref[...] = r1
                mixed = n1 * vec_ref[1:2, :] + vec_ref[2:3, :]
                mixed_ref[...] = mixed
                low_ref[...] = mixed.astype(BF)
                acc[...] = jnp.zeros(acc.shape, F32)
            else:
                acc[...] = begin[2][...]

        up_val = mm(low_ref[...], stack(up_refs), 1, 0) + bu_ref[...]
        cdf = 0.5 * (1.0 + lax.erf(up_val * math.sqrt(0.5)))
        act = (up_val * cdf).astype(BF)
        act_ref[...] = act
        slope_ref[...] = (cdf + up_val * (jnp.exp(-0.5 * up_val * up_val) * (1.0 / math.sqrt(2.0 * math.pi)))).astype(BF)
        acc[...] += mm(act, stack(dn_refs), 1, 1)

        @pl.when(j == count - 1)
        def _():
            if end is None:
                refs[0][...] = acc[...]
            else:
                out_ref, d_sum_ref, d_ffn_ref, sums_ref = refs[:4]
                n2, r2 = norm_parts(mixed_ref[...] + acc[...] + vec_ref[3:4, :])
                gain = vec_ref[4:5, :]
                out_ref[...] = (n2 * gain + vec_ref[5:6, :]).astype(BF)
                d_sum, d_gain, d_shift = norm_back(cot_ref[...].astype(F32), gain, n2, r2)
                d_sum_ref[...] = d_sum
                low = d_sum.astype(BF)
                d_ffn_ref[...] = low
                sums_ref[0:1, :] = jnp.sum(low.astype(F32), 0, keepdims=True)
                sums_ref[1:2, :] = d_gain
                sums_ref[2:3, :] = d_shift
                sums_ref[3:8, :] = jnp.zeros((5, d), F32)

    return pl.pallas_call(
        kernel, grid=(count,), in_specs=specs, out_specs=[o[1] for o in outs], out_shape=[o[0] for o in outs],
        scratch_shapes=[pltpu.VMEM((t, d), F32)], cost_estimate=COST,
        compiler_params=pltpu.CompilerParams(vmem_limit_bytes=56 * 2**20),
    )(*ins)


def write_split(tree, flipped, away_ref, column, low_ref, high_ref, kept, value):
    step = tree.nz * tree.rows
    order = tree.f_order(flipped)
    half, quarter = tree.width // 2, tree.width // 4
    n = value.shape[1]
    for at, f in enumerate(order):
        row = at * step
        away_ref[row : row + step, pl.ds(column, n)] = value[half + f * step : half + (f + 1) * step].astype(BF)
        ref, row = (low_ref, row) if row < quarter else (high_ref, row - quarter)
        ref[row : row + step, pl.ds(kept, n)] = value[f * step : (f + 1) * step].astype(BF)


def feed_back(tree, d_ffn, mixed_low, act, slope, up, dn, total, count, tail=None):
    t, d = d_ffn.shape
    n = len(up)
    tile = pl.BlockSpec((t, WIDE), lambda j: (0, j))
    ins = [d_ffn, mixed_low, act, slope, total] + [a for a, _ in up] + [a for a, _ in dn]
    specs = [whole((t, d))] * 2 + [tile] * 2 + [whole((t, d))] + column_blocks(up, WIDE, 0) + column_blocks(dn, WIDE, 0)
    shape = jax.ShapeDtypeStruct
    full = lambda dt: (shape((t, d), dt), whole((t, d)))
    n_up = count * WIDE + (0 if tail is None else d)
    n_dn = count * WIDE
    quarter = d // 4
    big = lambda r, c: (shape((r, c), BF), whole((r, c)))
    outs = [big(d // 2, n_up + n_dn), big(quarter, n_up), big(quarter, n_up), big(quarter, n_dn), big(quarter, n_dn)]
    outs += [(shape((1, count * WIDE), F32), pl.BlockSpec((1, WIDE), lambda j: (0, j)))]
    if tail is None:
        outs += [full(F32)]
    else:
        context, wo, n1, r1, gain = tail
        ins += [context, n1, r1, gain] + [a for a, _ in wo]
        specs += [whole((t, d)), whole((t, d)), whole((t, 1)), whole((1, d))] + column_blocks(wo, d, 0, 0)
        outs += [full(BF), full(BF), full(BF), (shape((8, d), F32), whole((8, d)))]

    def kernel(*refs):
        j = pl.program_id(0)
        d_ffn_ref, low_ref, act_ref, slope_ref, total_ref = refs[:5]
        refs = refs[5:]
        up_refs, dn_refs, refs = refs[:n], refs[n : 2 * n], refs[2 * n :]
        if tail is not None:
            ctx_ref, n1_ref, r1_ref, gain_ref = refs[:4]
            wo_refs, refs = refs[4 : 4 + n], refs[4 + n :]
        away_ref, up_lo, up_hi, dn_lo, dn_hi, d_bu_ref = refs[:6]
        refs = refs[6:]
        acc, d_ffn_t, low_t = refs[-3:]

        @pl.when(j == 0)
        def _():
            acc[...] = total_ref[...]
            d_ffn_t[...] = d_ffn_ref[...].T
            low_t[...] = low_ref[...].T

        d_up = (mm(d_ffn_ref[...], stack(dn_refs), 1, 0) * slope_ref[...].astype(F32)).astype(BF)
        d_bu_ref[...] = jnp.sum(d_up.astype(F32), 0, keepdims=True)
        at = pl.multiple_of(j * WIDE, WIDE)
        write_split(tree, True, away_ref, n_up + at, dn_lo, dn_hi, at, mm(d_ffn_t[...], act_ref[...], 1, 0))
        write_split(tree, False, away_ref, at, up_lo, up_hi, at, mm(low_t[...], d_up, 1, 0))
        acc[...] += mm(d_up, stack(up_refs), 1, 1)

        @pl.when(j == count - 1)
        def _():
            if tail is None:
                refs[0][...] = acc[...]
            else:
                d_attn_ref, rest_ref, d_ctx_ref, sums_ref = refs[:4]
                d_first, d_gain, d_shift = norm_back(acc[...], gain_ref[...], n1_ref[...], r1_ref[...])
                d_attn = d_first.astype(BF)
                d_attn_ref[...] = d_attn
                rest_ref[...] = (d_first - d_attn.astype(F32)).astype(BF)
                d_ctx_ref[...] = mm(d_attn, stack(wo_refs), 1, 0).astype(BF)
                d_ffn_t[...] = d_attn.T
                write_split(tree, False, away_ref, n_dn, up_lo, up_hi, n_dn, mm(d_ffn_t[...], ctx_ref[...], 1, 0))
                sums_ref[0:1, :] = jnp.sum(d_attn.astype(F32), 0, keepdims=True)
                sums_ref[1:2, :] = d_gain
                sums_ref[2:3, :] = d_shift
                sums_ref[3:8, :] = jnp.zeros((5, d), F32)

    return pl.pallas_call(
        kernel, grid=(count,), in_specs=specs, out_specs=[o[1] for o in outs], out_shape=[o[0] for o in outs],
        scratch_shapes=[pltpu.VMEM((t, d), F32), pltpu.VMEM((d, t), BF), pltpu.VMEM((d, t), BF)], cost_estimate=COST,
        compiler_params=pltpu.CompilerParams(vmem_limit_bytes=60 * 2**20),
    )(*ins)


def pack_first(query, key, value, table, vectors, up_bias):
    rows, d = query.shape
    buckets = table.shape[1]
    spread = up_bias.shape[0]
    wide = 3 * d + buckets + 128

    def kernel(q_ref, k_ref, v_ref, t_ref, *refs):
        vec_refs, ub_ref, out_ref, lines = refs[:-3], refs[-3], refs[-2], refs[-1]
        out_ref[:, 0:d] = q_ref[...].astype(BF)
        out_ref[:, d : 2 * d] = k_ref[...].astype(BF)
        out_ref[:, 2 * d : 3 * d] = v_ref[...].astype(BF)
        out_ref[:, 3 * d : 3 * d + buckets] = t_ref[...].astype(BF)
        lines[...] = jnp.zeros(lines.shape, F32)
        for i, r in enumerate(vec_refs):
            lines[i : i + 1, 0:rows] = r[...]
        lines[len(vec_refs) : len(vec_refs) + spread, 0:rows] = ub_ref[...]
        out_ref[:, 3 * d + buckets : wide] = lines[...].T[:rows].astype(BF)

    return pl.pallas_call(
        kernel, out_shape=jax.ShapeDtypeStruct((rows, wide), BF), scratch_shapes=[pltpu.VMEM((128, 128), F32)],
        cost_estimate=COST, compiler_params=pltpu.CompilerParams(vmem_limit_bytes=60 * 2**20),
    )(query, key, value, table, *[v.reshape(1, rows) for v in vectors], up_bias)


def pack_second(out_weight, up, down):
    rows, ff = up.shape
    d = out_weight.shape[1]
    cut = ff // 2

    def kernel(o_ref, u_ref, d_ref, a_ref, b_ref):
        down_t = d_ref[...].astype(BF)
        a_ref[:, 0:d] = o_ref[...].astype(BF)
        a_ref[:, d : d + cut] = u_ref[:, 0:cut].astype(BF)
        a_ref[:, d + cut : d + 2 * cut] = down_t[:, 0:cut]
        b_ref[:, 0:cut] = u_ref[:, cut:ff].astype(BF)
        b_ref[:, cut : 2 * cut] = down_t[:, cut:ff]

    return pl.pallas_call(
        kernel, out_shape=[jax.ShapeDtypeStruct((rows, d + 2 * cut), BF), jax.ShapeDtypeStruct((rows, 2 * cut), BF)],
        cost_estimate=COST, compiler_params=pltpu.CompilerParams(vmem_limit_bytes=60 * 2**20),
    )(out_weight, up, down)


def project(x_p, onehot, low, high, bias, tile):
    t, d = x_p.shape
    buckets = onehot.shape[1]
    n = len(low)
    per = d // tile
    clip = lambda j, a: jnp.clip(j - a * per, 0, per - 1)
    specs = [whole((t, d)), whole(onehot.shape), pl.BlockSpec((1, tile), lambda j: (0, j))]
    specs += piece_blocks(low, tile, lambda j: jnp.minimum(j, 2 * per - 1))
    specs += piece_blocks(high, tile, lambda j: clip(j, 2))
    specs += piece_blocks(high, buckets, lambda j: d // buckets)
    out = lambda a: pl.BlockSpec((t, tile), lambda j: (0, clip(j, a)))

    def kernel(x_ref, hot_ref, bias_ref, *refs):
        lows, highs, tables, refs = refs[:n], refs[n : 2 * n], refs[2 * n : 3 * n], refs[3 * n :]
        q_ref, k_ref, v_ref, ek_ref, eq_ref, table = refs
        j = pl.program_id(0)

        @pl.when(j == 0)
        def _():
            table[...] = mm(hot_ref[...], stack(tables), 1, 1).astype(BF)

        def both(out_ref, e_ref):
            w = stack(lows)
            out_ref[...] = (mm(x_ref[...], w, 1, 0) + bias_ref[...]).astype(BF)
            e_ref[...] = (mm(table[...], w, 1, 0) + bias_ref[...]).astype(BF)

        pl.when(j < per)(lambda: both(q_ref, eq_ref))
        pl.when((j >= per) & (j < 2 * per))(lambda: both(k_ref, ek_ref))

        @pl.when(j >= 2 * per)
        def _():
            v_ref[...] = (mm(x_ref[...], stack(highs), 1, 0) + bias_ref[...]).astype(BF)

    return pl.pallas_call(
        kernel, grid=(3 * per,), in_specs=specs, out_specs=[out(0), out(1), out(2), out(1), out(0)],
        out_shape=[jax.ShapeDtypeStruct((t, d), BF)] * 5, scratch_shapes=[pltpu.VMEM((t, d), BF)], cost_estimate=COST,
        compiler_params=pltpu.CompilerParams(vmem_limit_bytes=60 * 2**20),
    )(x_p, onehot, bias, *arrays(low), *arrays(high), *arrays(high))


def attention_grads(tree, x_p, onehot, low, high, dq, dk, dv, dek, deq, tile, part, carried=None):
    t, d = x_p.shape
    buckets = onehot.shape[1]
    n = len(low)
    per = d // tile
    last = carried is not None
    half, quarter = d // 2, d // 4
    col = pl.BlockSpec((t, tile), lambda j: (0, part))
    specs = [whole((t, d)), whole(onehot.shape)] + [col] * 5
    specs += piece_blocks(low, tile, lambda j: jnp.minimum(j, 1) * per + part)
    specs += piece_blocks(high, buckets, lambda j: d // buckets)
    ins = [x_p, onehot, dq, dk, dv, dek, deq] + arrays(low) + arrays(high)
    if last:
        ins += list(carried)
        specs += [whole(a.shape) for a in carried]
    wide = tile + (buckets + 128 if last else 0)
    shape = jax.ShapeDtypeStruct
    big = lambda r, c: (shape((r, c), BF), whole((r, c)))
    outs = [big(half, 2 * tile + wide), big(quarter, 2 * tile), big(quarter, 2 * tile), big(quarter, wide), big(quarter, wide)]
    if not last:
        outs += [(shape((d, buckets), F32), whole((d, buckets))), (shape((8, tile), F32), whole((8, tile)))]

    def kernel(*refs):
        x_ref, hot_ref, dq_ref, dk_ref, dv_ref, dek_ref, deq_ref = refs[:7]
        lows, tables, refs = refs[7 : 7 + n], refs[7 + n : 7 + 2 * n], refs[7 + 2 * n :]
        if last:
            before_ref, sums_before_ref, lines_ref, ordered_ref, place_ref = refs[:5]
            refs = refs[5:]
        away_ref, qk_lo, qk_hi, wide_lo, wide_hi = refs[:5]
        if last:
            x_t, table, d_table, sums = refs[5:]
        else:
            d_table, sums, x_t, table = refs[5:]
        j = pl.program_id(0)

        @pl.when(j == 0)
        def _():
            x_t[...] = x_ref[...].T
            table[...] = stack(tables)
            d_table[...] = before_ref[...] if last else jnp.zeros(d_table.shape, F32)
            sums[...] = jnp.zeros(sums.shape, F32)

        def wide_write(at, value):
            write_split(tree, True, away_ref, 2 * tile + at, wide_lo, wide_hi, at, value)

        def both(g_ref, e_ref, row):
            pos = mm(hot_ref[...], e_ref[...], 0, 0).astype(BF)
            g = g_ref[...]
            value = mm(x_t[...], g, 1, 0) + mm(table[...], pos, 1, 0)
            write_split(tree, False, away_ref, row * tile, qk_lo, qk_hi, row * tile, value)
            sums[row : row + 1, :] = jnp.sum(g.astype(F32), 0, keepdims=True) + jnp.sum(pos.astype(F32), 0, keepdims=True)
            d_table[...] += mm(stack(lows), pos, 1, 1)

        pl.when(j == 0)(lambda: both(dq_ref, deq_ref, 0))
        pl.when(j == 1)(lambda: both(dk_ref, dek_ref, 1))

        @pl.when(j == 2)
        def _():
            g = dv_ref[...]
            wide_write(0, mm(x_t[...], g, 1, 0))
            sums[2:3, :] = jnp.sum(g.astype(F32), 0, keepdims=True)
            if last:
                wide_write(tile, d_table[...])
                known = [sums_before_ref[0:3, i * tile : (i + 1) * tile] for i in range(per - 1)]
                vectors = jnp.concatenate([jnp.concatenate(known + [sums[0:3, :]], 1), lines_ref[...]], 0)
                pad = lambda v, lead: jnp.concatenate(
                    ([jnp.zeros((lead, d), F32)] if lead else []) + [v, jnp.zeros((128 - lead - v.shape[0], d), F32)], 0
                )
                natural = mm(place_ref[...], pad(vectors, 0).astype(BF), 1, 1)
                wide_write(tile + buckets, natural + pad(ordered_ref[...], 16).T)

    scratch = [pltpu.VMEM((d, t), BF), pltpu.VMEM((d, buckets), BF)]
    if last:
        scratch += [pltpu.VMEM((d, buckets), F32), pltpu.VMEM((8, tile), F32)]
    return pl.pallas_call(
        kernel, grid=(3,), in_specs=specs, out_specs=[o[1] for o in outs], out_shape=[o[0] for o in outs],
        scratch_shapes=scratch, cost_estimate=COST, compiler_params=pltpu.CompilerParams(vmem_limit_bytes=56 * 2**20),
    )(*ins)


def input_grads(d_attn, d_rest, low, high, dq, dk, dv, out_p, place_t, tile):
    t, d = d_attn.shape
    n = len(low)
    per = d // tile
    clip = lambda j, a: jnp.clip(j - a * per, 0, per - 1)
    col = lambda a: pl.BlockSpec((t, tile), lambda j: (0, clip(j, a)))
    specs = [whole((t, d)), whole((t, d)), col(0), col(1), col(2), whole((t, d)), whole((d, d))]
    specs += piece_blocks(low, tile, lambda j: jnp.minimum(j, 2 * per - 1))
    specs += piece_blocks(high, tile, lambda j: clip(j, 2))

    def kernel(*refs):
        a_ref, r_ref, dq_ref, dk_ref, dv_ref, out_ref, place_ref = refs[:7]
        lows, highs, refs = refs[7 : 7 + n], refs[7 + n : 7 + 2 * n], refs[7 + 2 * n :]
        grad_ref, layer_ref, acc = refs
        j = pl.program_id(0)

        @pl.when(j == 0)
        def _():
            acc[...] = a_ref[...].astype(F32) + r_ref[...].astype(F32)
            layer_ref[...] = mm(out_ref[...], place_ref[...], 1, 0).astype(BF)

        def add(g_ref, ws):
            acc[...] += mm(g_ref[...], stack(ws), 1, 1)

        pl.when(j < per)(lambda: add(dq_ref, lows))
        pl.when((j >= per) & (j < 2 * per))(lambda: add(dk_ref, lows))
        pl.when(j >= 2 * per)(lambda: add(dv_ref, highs))

        @pl.when(j == 3 * per - 1)
        def _():
            grad_ref[...] = mm(acc[...].astype(BF), place_ref[...], 1, 0).astype(BF)

    return pl.pallas_call(
        kernel, grid=(3 * per,), in_specs=specs, out_specs=[whole((t, d))] * 2,
        out_shape=[jax.ShapeDtypeStruct((t, d), BF)] * 2, scratch_shapes=[pltpu.VMEM((t, d), F32)], cost_estimate=COST,
        compiler_params=pltpu.CompilerParams(vmem_limit_bytes=48 * 2**20),
    )(d_attn, d_rest, dq, dk, dv, out_p, place_t, *arrays(low), *arrays(high))


class Tree:
    def __init__(self, width):
        self.nf, self.ndp = lax.axis_size("fsdp"), lax.axis_size("dp")
        self.n = self.nf * self.ndp
        self.nz = self.ndp // 2
        self.rows = width // self.n
        self.width = width
        self.f_bits = [1 << b for b in range(self.nf.bit_length() - 1)]
        self.z_bits = [1 << b for b in range(self.nz.bit_length() - 1)]

    def place(self, transposed):
        me = lax.axis_index("dp") * self.nf + lax.axis_index("fsdp")
        d = jnp.arange(self.width, dtype=jnp.int32)
        rel = (d // self.rows) ^ me
        f = rel % self.nf
        core = (rel // self.nf) % 2
        z = sum(((rel // (2 * self.nf * b)) % 2) * (self.nz // (2 * b)) for b in self.z_bits)
        at = ((core * self.nf + f) * self.nz + z) * self.rows + d % self.rows
        j = lax.broadcasted_iota(jnp.int32, (self.width, self.width), 0 if transposed else 1)
        return ((at[None, :] if transposed else at[:, None]) == j).astype(BF)

    def swap(self, a, axis, bit):
        size = self.nf if axis == "fsdp" else self.ndp
        return lax.ppermute(a, axis, [(i, i ^ bit) for i in range(size)])

    def f_order(self, flipped):
        order = self.f_bits[::-1] if flipped else self.f_bits
        key = lambda f: [f & bit != 0 for bit in order]
        return sorted(range(self.nf), key=key)

    def gather(self, cur, sides, direct=False):
        columns = [0]
        for width, _ in sides:
            columns.append(columns[-1] + width)
        if direct and self.nz <= 4:
            got = yield [(cur, "dp", 2 * z) for z in range(1, self.nz)]
            got = [cur] + list(got)
            near_first = sorted(range(self.nz), key=lambda z: [z & bit != 0 for bit in self.z_bits])
            cur = join([got[z] for z in near_first])
        else:
            for bit in self.z_bits[::-1]:
                (got,) = yield [(cur, "dp", 2 * bit)]
                cur = join([cur, got])
        found = [{0: (cur, c)} for c in columns[:-1]]
        orders = [self.f_bits[::-1] if flipped else self.f_bits for _, flipped in sides]

        def keep(keys, array, whole_row):
            for s, i in keys:
                found[s][i] = (array, columns[s] if whole_row else 0)

        every = range(len(sides))
        sends = [([(s, bit) for s in every], True, (cur, "fsdp", bit)) for bit in self.f_bits]
        cores = [([(s, self.nf) for s in every], True, (cur, "dp", 1))]
        while sends or cores:
            got = yield [x for _, _, x in sends + cores]
            for (keys, whole_row, _), g in zip(sends + cores, got):
                keep(keys, g, whole_row)
            arrived, sends, cores = sends, [], []
            for keys, whole_row, _ in arrived:
                i = keys[0][1]
                cores.append(([(s, self.nf + i) for s, _ in keys], whole_row, (found[keys[0][0]][i][0], "dp", 1)))
                for s, _ in keys:
                    array, column = found[s][i]
                    last = max(at for at, bit in enumerate(orders[s]) if i & bit)
                    for bit in orders[s][last + 1 :]:
                        part = array[:, column : column + columns[s + 1] - columns[s]]
                        sends.append(([(s, i | bit)], False, (part, "fsdp", bit)))
        return [[f[i] for i in range(2 * self.nf)] for f in found]


class Job:
    def __init__(self, tree, away, *sides):
        self.tree = tree
        self.away = away
        self.sides = [list(side) for side in sides]
        self.stages = ([] if away is None else ["core"]) + list(range(len(tree.f_bits))) + [("z", b) for b in tree.z_bits]
        self.total = None

    def wanted(self):
        if not self.stages:
            return []
        stage = self.stages[0]
        if stage == "core":
            return [(self.away, "dp", 1)]
        if isinstance(stage, int):
            bits = self.tree.f_bits
            return [(side[1], "fsdp", (bits[::-1] if side[2] else bits)[stage]) for side in self.sides]
        return [(self.total[1], "dp", 2 * stage[1])]

    def add(self, got):
        stage = self.stages.pop(0)
        more = bool(self.stages)
        sums = lambda a, g: (a.astype(F32) + g.astype(F32)).astype(BF)
        if stage == "core":
            column = 0
            for side in self.sides:
                r, n = side[0].shape
                side[0] = sums(side[0], got[0][:r, column : column + n])
                side[1] = sums(side[1], got[0][r:, column : column + n])
                column += n
        elif isinstance(stage, int):
            for side, g in zip(self.sides, got):
                r = side[0].shape[0] // 2
                side[0], side[1] = sums(side[0][:r], g[:r]), sums(side[0][r:], g[r:])
            if not isinstance(self.stages[0], int):
                cat = lambda xs: xs[0] if len(xs) == 1 else jnp.concatenate(xs, 1)
                self.total = [cat([side[i] for side in self.sides]) for i in range(2)]
        else:
            keep = self.total[0]
            if more:
                r = keep.shape[0] // 2
                self.total = [sums(keep[:r], got[0][:r]), sums(keep[r:], got[0][r:])]
            else:
                self.total = keep.astype(F32) + got[0].astype(F32)

    def hold(self, arrays):
        stage = self.stages[0]
        if stage == "core":
            (self.away,) = arrays
        elif isinstance(stage, int):
            for side, a in zip(self.sides, arrays):
                side[1] = a
        else:
            self.total[1] = arrays[0]


class Flow:
    def __init__(self, steps):
        self.steps = steps
        self.value = None
        self.sends = next(steps)

    def wanted(self):
        return list(self.sends)

    def add(self, got):
        try:
            self.sends = self.steps.send(got)
        except StopIteration as end:
            self.sends, self.value = [], end.value

    def hold(self, arrays):
        self.sends = [(a,) + rest[1:] for a, rest in zip(arrays, self.sends)]


class Pair:
    def __init__(self, *arrays):
        self.arrays = arrays
        self.value = None

    def wanted(self):
        return [] if self.value is not None else [(a, "dp", 1) for a in self.arrays]

    def add(self, got):
        self.value = got


def drain(tree, flow):
    while flow.value is None:
        window(tree, [flow])


def window(tree, works, others=(), later=()):
    works = [w for w in works if w.wanted()]
    later = [w for w in later if w.wanted()]
    sent = [[tree.swap(*x) for x in w.wanted()] for w in works]
    kept = [[x[0] for x in w.wanted()] for w in later]
    sent, kept, others = lax.optimization_barrier((sent, kept, tuple(others)))
    for w, arrays_in in zip(later, kept):
        w.hold(list(arrays_in))
    for w, got in zip(works, sent):
        w.add(list(got))
    return others


def per_device(
    tokens, segment_ids, rel_bucket, query_weight, query_bias, key_weight, key_bias, value_weight, value_bias,
    out_weight, out_bias, attention_gain, attention_shift, up_weight, up_bias, down_weight, down_bias,
    output_gain, output_shift, position_table, cotangent,
):
    x = tokens[0]
    t, d = x.shape
    seg = segment_ids[0]
    tree = Tree(d)
    rows = tree.rows
    ff = up_weight.shape[1]
    spread = ff // d
    buckets = position_table.shape[0]
    scale = 1.0 / math.sqrt(3.0 * (d // HEADS))
    vectors = (query_bias, key_bias, value_bias, out_bias, attention_gain, attention_shift, down_bias, output_gain, output_shift)
    cut = ff // 2
    lead = pack_first(query_weight, key_weight, value_weight, position_table.T, vectors, up_bias.reshape(spread, rows))
    one = Flow(tree.gather(lead, [(2 * d, False), (d + buckets + 128, True)], True))
    place = tree.place(False)
    place_t = tree.place(True)
    half = t // 2
    picked = lax.rev(rel_bucket[t - half : 2 * t - half], (0,))
    onehot = (picked[:, None] == lax.broadcasted_iota(jnp.int32, (t, buckets), 1)).astype(BF)
    early, late = pack_second(out_weight.T, up_weight, down_weight.T)
    early, late, place, place_t, onehot = window(tree, [one], (early, late, place, place_t, onehot))
    two = Flow(tree.gather(early, [(d + cut, False), (cut, True)]))
    arrange = lambda m: mm(m, place, 1, 0).astype(BF)
    x_p = arrange(x)
    late, x_p = window(tree, [one, two], (late, x_p))
    cot_p = arrange(cotangent[0])
    late, cot_p = window(tree, [one, two], (late, cot_p))
    three = Flow(tree.gather(late, [(cut, False), (cut, True)]))
    drain(tree, one)
    low, high = one.value

    small = jnp.concatenate([a[:, c + d + buckets : c + d + buckets + 128] for a, c in high], 0)
    vec = mm(small, place, 0, 1)
    vecs = small.T[3:11].astype(F32)
    bias = vec[:3].reshape(1, 3 * d)
    bu = vec[SPLIT : SPLIT + spread].reshape(spread, tree.n, rows).transpose(1, 0, 2).reshape(1, ff)
    q, k, v, ek, eq = project(x_p, onehot, low, high, bias, TILE)
    n_pairs = HEADS // 2
    plan = (
        (0, n_pairs // 4, [two, three], []),
        (n_pairs // 4, n_pairs * 5 // 8, [two, three], []),
        (n_pairs * 5 // 8, n_pairs, [two, three], []),
    )
    made = None
    for begin, after, works, later in plan:
        made = attend(q, k, v, ek, eq, seg, scale, made, begin, after - begin)
        made = window(tree, works, made, later)
    context, probs = made

    drain(tree, two)
    wo = two.value[0]
    shifted = lambda pieces, by: [(a, c + by) for a, c in pieces]
    up_a, dn_early = shifted(wo, d), two.value[1]
    count = cut // WIDE
    act_a, slope_a, n1, r1, mixed, mixed_low, so_far = feed_forward(vecs, bu, up_a, dn_early, 0, count, (context, x_p, wo))
    (so_far,) = window(tree, [three], (so_far,))
    drain(tree, three)
    up_b, dn_late = three.value
    act_b, slope_b, out_p, d_sum, d_ffn, sums2 = feed_forward(
        vecs, bu, up_b, dn_late, count, count, (mixed, mixed_low, so_far), cot_p
    )
    back = feed_back(tree, d_ffn, mixed_low, act_a, slope_a, up_a, dn_early, d_sum, count)
    job_1 = Job(tree, back[0], (*back[1:3], False), (*back[3:5], True))
    d_bu_a, total = back[5:]
    back = feed_back(
        tree, d_ffn, mixed_low, act_b, slope_b, up_b, dn_late, total, count, (context, wo, n1, r1, vecs[1:2])
    )
    job_2 = Job(tree, back[0], (*back[1:3], False), (*back[3:5], True))
    d_bu_b, d_attn, d_rest, d_context, sums1 = back[5:]
    (d_context,) = window(tree, [job_1], (d_context,))

    args = (q, k, v, ek, eq, d_context, probs, scale)
    grads = attend_back(*args, None, 0, n_pairs // 2)
    grads = window(tree, [job_1, job_2], grads)
    split = attention_grads(tree, x_p, onehot, low, high, *grads, d // 2, 0)
    (*grads, d_table, sums) = window(tree, [job_1], (*grads, *split[5:]))
    job_3 = Job(tree, split[0], (*split[1:3], False), (*split[3:5], True))
    grads = attend_back(*args, grads, n_pairs // 2, n_pairs // 2)
    grads = window(tree, [job_2, job_3, job_1], grads)
    d_bu = jnp.concatenate([d_bu_a, d_bu_b], 1)
    lines = d_bu.reshape(tree.n, spread, rows).transpose(1, 0, 2).reshape(spread, d)
    ordered = jnp.concatenate([sums1[:3], sums2[:3]], 0)
    ordered = jnp.concatenate([ordered, jnp.zeros((2, d), F32)], 0)
    carried = (d_table, sums, lines, ordered, place_t)
    split = attention_grads(tree, x_p, onehot, low, high, *grads, d // 2, 1, carried)
    split = window(tree, [job_3, job_1], split)
    job_4 = Job(tree, split[0], (*split[1:3], False), (*split[3:5], True))
    dq, dk, dv, _, _ = grads
    d_attn, d_rest = window(tree, [job_4, job_2], (d_attn, d_rest))
    grad_layer = input_grads(d_attn, d_rest, low, high, dq, dk, dv, out_p, place_t, TILE)
    input_grad, layer_out = window(tree, [job_4, job_3], grad_layer)
    works = [job_4, job_3, job_2, job_1]
    while any(w.stages for w in works):
        window(tree, works)
    four, three, two, one = [w.total for w in works]
    h = d // 2
    up_a_grad, dn_a_grad = one[:, :cut], one[:, cut:]
    up_b_grad, out_grad, dn_b_grad = two[:, :cut], two[:, cut : cut + d], two[:, cut + d :]
    query_grad, key_grad, value_grad = [
        jnp.concatenate([three[:, i * h : (i + 1) * h], four[:, i * h : (i + 1) * h]], 1) for i in range(3)
    ]
    table_grad, tail = four[:, 3 * h : 3 * h + buckets], four[:, 3 * h + buckets :]
    d_bq, d_bk, d_bv = [tail[:, i] for i in range(3)]
    d_up_bias = tail[:, 3 : 3 + spread].T.reshape(-1)
    d_bo, d_gain1, d_shift1, d_bd, d_gain2, d_shift2 = [tail[:, 16 + i] for i in range(6)]
    return (
        layer_out[None], input_grad[None],
        query_grad, d_bq, key_grad, d_bk, value_grad, d_bv,
        out_grad.T, d_bo, d_gain1, d_shift1, jnp.concatenate([up_a_grad, up_b_grad], 1), d_up_bias,
        jnp.concatenate([dn_a_grad.T, dn_b_grad.T], 0), d_bd, d_gain2, d_shift2,
        table_grad.T,
    )


def solution(mesh):
    both = ("dp", "fsdp")
    row, col, vec = P(both, None), P(None, both), P(both)
    seq = P(both, None, None)
    params = (row, vec, row, vec, row, vec, col, vec, vec, vec, row, vec, col, vec, vec, vec, col)
    return jax.shard_map(
        per_device, mesh=mesh, in_specs=(seq, row, P()) + params + (seq,), out_specs=(seq, seq) + params, check_vma=False
    )
```

```python
import math
import jax, jax.numpy as jnp
from jax import lax
from jax.sharding import PartitionSpec as P
import jax.experimental.pallas as pl, jax.experimental.pallas.tpu as pltpu
HEADS=16
BF=jnp.bfloat16
F32=jnp.float32
COST=pl.CostEstimate(flops=10**9,bytes_accessed=10**6,transcendentals=0)

def mm(a,b,ca,cb):
    return lax.dot_general(a,b,(((ca,),(cb,)),((),())),preferred_element_type=F32)

def attend_kernel(scale, q_ref,k_ref,v_ref,ek_ref,eq_ref,segc_ref,segr_ref,ctx_ref,p_ref):
    t=q_ref.shape[0]; half=t//2
    hd=q_ref.shape[1]//2
    same=segc_ref[...]==segr_ref[...]
    lane=lax.broadcasted_iota(jnp.int32,q_ref.shape,1)
    ctx=None
    for h in range(2):
        mine=(lane>=h*hd)&(lane<(h+1)*hd)
        pick=lambda r: jnp.where(mine,r[...],jnp.zeros((),BF))
        q=pick(q_ref); k=pick(k_ref)
        s=mm(q,k_ref[...],1,1)
        to=pltpu.roll(mm(q,ek_ref[...],1,1),half,1,stride=1,stride_axis=0)
        fr=pltpu.roll(mm(k,eq_ref[...],1,1),half,1,stride=1,stride_axis=0)
        s=jnp.where(same,s+to+fr.T,-1e30)
        top=jnp.max(s,axis=1,keepdims=True)
        e=jnp.exp((s-top)*scale)
        p=(e*(1.0/jnp.sum(e,axis=1,keepdims=True))).astype(BF)
        p_ref[h]=p
        part=mm(p,pick(v_ref),1,0)
        ctx=part if ctx is None else ctx+part
    ctx_ref[...]=ctx.astype(BF)

def attend(q,k,v,ek,eq,seg,scale,made,at,count):
    t,d=q.shape
    w=2*d//HEADS
    col=pl.BlockSpec((t,w),lambda i:(0,i+at))
    made=[] if made is None else list(made)
    return pl.pallas_call(
        lambda *r: attend_kernel(scale,*r[:7],*r[len(r)-2:]),
        grid=(count,),
        in_specs=[col]*5+[pl.BlockSpec((t,1),lambda i:(0,0)),pl.BlockSpec((1,t),lambda i:(0,0))]+[pl.BlockSpec(memory_space=pl.ANY)]*len(made),
        out_specs=[col,pl.BlockSpec((2,t,t),lambda i:(i+at,0,0))],
        out_shape=[jax.ShapeDtypeStruct((t,d),BF),jax.ShapeDtypeStruct((HEADS,t,t),BF)],
        input_output_aliases={7+i:i for i in range(len(made))},
        cost_estimate=COST,
        compiler_params=pltpu.CompilerParams(vmem_limit_bytes=60 * 2**20),
    )(q,k,v,ek,eq,seg.reshape(t,1),seg.reshape(1,t),*made)

def attend_back_kernel(scale,q_ref,k_ref,v_ref,ek_ref,eq_ref,dc_ref,p_ref,dq_ref,dk_ref,dv_ref,dek_ref,deq_ref):
    t=q_ref.shape[0]; half=t//2
    hd=q_ref.shape[1]//2
    r=lax.broadcasted_iota(jnp.int32,(half,half),0); c=lax.broadcasted_iota(jnp.int32,(half,half),1)
    flip=(r+c==half-1).astype(BF)
    lane=lax.broadcasted_iota(jnp.int32,q_ref.shape,1)
    def turn(x):
        return jnp.concatenate([mm(flip,x[:half],1,0),mm(flip,x[half:],1,0)],0)
    def turn_t(x):
        return jnp.concatenate([mm(flip,x[:,:half],1,1),mm(flip,x[:,half:],1,1)],0)
    def unroll(x):
        return jnp.concatenate([pltpu.roll(x[:half],1,1,stride=1,stride_axis=0),pltpu.roll(x[half:],half+1,1,stride=1,stride_axis=0)],0)
    q_turned=turn(q_ref[...]).astype(BF); k_turned=turn(k_ref[...]).astype(BF)
    dqt=dkt=dv=dek=deq=None
    plus=lambda a,b: b if a is None else a+b
    for h in range(2):
        mine=(lane>=h*hd)&(lane<(h+1)*hd)
        pick=lambda x: jnp.where(mine,x,jnp.zeros((),BF))
        p=p_ref[h]; dc=pick(dc_ref[...])
        dp=mm(dc,v_ref[...],1,1)
        pf=p.astype(F32)
        w=pf*dp
        ds=(w-pf*jnp.sum(w,axis=1,keepdims=True)).astype(BF)
        dv=plus(dv,mm(p,dc,0,0))
        a=turn(ds).astype(BF); au=unroll(a)
        b=turn_t(ds).astype(BF); bu=unroll(b)
        dqt=plus(dqt,mm(a,pick(k_ref[...]),1,0)+mm(au,pick(ek_ref[...]),1,0))
        dkt=plus(dkt,mm(b,pick(q_ref[...]),1,0)+mm(bu,pick(eq_ref[...]),1,0))
        dek=plus(dek,mm(au,pick(q_turned),0,0))
        deq=plus(deq,mm(bu,pick(k_turned),0,0))
    dq_ref[...]=turn((dqt*scale).astype(BF)).astype(BF)
    dk_ref[...]=turn((dkt*scale).astype(BF)).astype(BF)
    dv_ref[...]=dv.astype(BF)
    dek_ref[...]=(dek*scale).astype(BF)
    deq_ref[...]=(deq*scale).astype(BF)

def attend_back(q,k,v,ek,eq,dc,p,scale,grads,at,count):
    t,d=q.shape
    w=2*d//HEADS
    col=pl.BlockSpec((t,w),lambda i:(0,i+at))
    grads=[] if grads is None else list(grads)
    return pl.pallas_call(
        lambda *r: attend_back_kernel(scale,*r[:7],*r[len(r)-5:]),
        grid=(count,),
        in_specs=[col]*6+[pl.BlockSpec((2,t,t),lambda i:(i+at,0,0))]+[pl.BlockSpec(memory_space=pl.ANY)]*len(grads),
        out_specs=[col]*5,
        out_shape=[jax.ShapeDtypeStruct((t,d),BF)]*5,
        input_output_aliases={7+i:i for i in range(len(grads))},
        cost_estimate=COST,
        compiler_params=pltpu.CompilerParams(vmem_limit_bytes=60 * 2**20),
    )(q,k,v,ek,eq,dc,p,*grads)


NORM_EPS = 1e-7
SPLIT = 9
TILE = 512
WIDE = 512


def norm_parts(v):
    mean = jnp.mean(v, axis=-1, keepdims=True)
    c = v - mean
    r = lax.rsqrt(jnp.mean(c * c, axis=-1, keepdims=True) + NORM_EPS)
    return c * r, r


def norm_back(g, gain, n, r):
    u = g * gain
    d = r * (u - jnp.mean(u, -1, keepdims=True) - n * jnp.mean(u * n, -1, keepdims=True))
    return d, jnp.sum(g * n, 0, keepdims=True), jnp.sum(g, 0, keepdims=True)


def stack(refs):
    return jnp.concatenate([r[...] for r in refs], 0) if len(refs) > 1 else refs[0][...]


def whole(shape):
    return pl.BlockSpec(shape, lambda j: (0,) * len(shape))


def join(blocks):
    rows, n = blocks[0].shape
    if rows % 16:
        return jnp.concatenate(blocks, 0)

    def kernel(*refs):
        for i, r in enumerate(refs[:-1]):
            refs[-1][i * rows : (i + 1) * rows, :] = r[...]

    return pl.pallas_call(
        kernel, out_shape=jax.ShapeDtypeStruct((rows * len(blocks), n), BF), cost_estimate=COST,
        compiler_params=pltpu.CompilerParams(vmem_limit_bytes=32 * 2**20),
    )(*blocks)


def arrays(pieces):
    return [a for a, _ in pieces]


def piece_blocks(pieces, width, block):
    out = []
    for array, column in pieces:
        out.append(pl.BlockSpec((array.shape[0], width), lambda j, base=column // width: (0, base + block(j))))
    return out


def column_blocks(pieces, width, first, step=1):
    return piece_blocks(pieces, width, lambda j: first + step * j)


def feed_forward(vecs, bu, up, dn, first, count, start=None, end=None):
    opening = len(start) == 3 and isinstance(start[2], list)
    n = len(up)
    if opening:
        context, x, wo = start
        t, d = x.shape
        ins = [context, x] + [a for a, _ in wo]
        specs = [whole((t, d))] * 2 + column_blocks(wo, d, 0, 0)
    else:
        t, d = start[0].shape
        ins, specs = list(start), [whole((t, d))] * 3
    n_start = len(ins)
    ins += [vecs, bu] + [a for a, _ in up] + [a for a, _ in dn] + ([] if end is None else [end])
    specs += [whole(vecs.shape), pl.BlockSpec((1, WIDE), lambda j: (0, j + first))]
    specs += column_blocks(up, WIDE, 0) + column_blocks(dn, WIDE, 0) + ([] if end is None else [whole((t, d))])
    shape = jax.ShapeDtypeStruct
    tile_out = pl.BlockSpec((t, WIDE), lambda j: (0, j))
    outs = [(shape((t, count * WIDE), BF), tile_out)] * 2
    full = lambda dt: (shape((t, d), dt), whole((t, d)))
    if opening:
        outs += [full(F32), (shape((t, 1), F32), whole((t, 1))), full(F32), full(BF)]
    if end is None:
        outs += [full(F32)]
    else:
        outs += [full(BF), full(F32), full(BF), (shape((8, d), F32), whole((8, d)))]

    def kernel(*refs):
        j = pl.program_id(0)
        begin, refs = refs[:n_start], refs[n_start:]
        vec_ref, bu_ref, refs = refs[0], refs[1], refs[2:]
        up_refs, dn_refs, refs = refs[:n], refs[n : 2 * n], refs[2 * n :]
        if end is not None:
            cot_ref, refs = refs[0], refs[1:]
        act_ref, slope_ref, refs = refs[0], refs[1], refs[2:]
        if opening:
            n1_ref, r1_ref, mixed_ref, low_ref = refs[:4]
            refs = refs[4:]
        else:
            mixed_ref, low_ref = begin[:2]
        acc = refs[-1]

        @pl.when(j == 0)
        def _():
            if opening:
                v = begin[1][...].astype(F32) + mm(begin[0][...], stack(begin[2:]), 1, 1) + vec_ref[0:1, :]
                n1, r1 = norm_parts(v)
                n1_ref[...] = n1
                r1_ref[...] = r1
                mixed = n1 * vec_ref[1:2, :] + vec_ref[2:3, :]
                mixed_ref[...] = mixed
                low_ref[...] = mixed.astype(BF)
                acc[...] = jnp.zeros(acc.shape, F32)
            else:
                acc[...] = begin[2][...]

        up_val = mm(low_ref[...], stack(up_refs), 1, 0) + bu_ref[...]
        cdf = 0.5 * (1.0 + lax.erf(up_val * math.sqrt(0.5)))
        act = (up_val * cdf).astype(BF)
        act_ref[...] = act
        slope_ref[...] = (cdf + up_val * (jnp.exp(-0.5 * up_val * up_val) * (1.0 / math.sqrt(2.0 * math.pi)))).astype(BF)
        acc[...] += mm(act, stack(dn_refs), 1, 1)

        @pl.when(j == count - 1)
        def _():
            if end is None:
                refs[0][...] = acc[...]
            else:
                out_ref, d_sum_ref, d_ffn_ref, sums_ref = refs[:4]
                n2, r2 = norm_parts(mixed_ref[...] + acc[...] + vec_ref[3:4, :])
                gain = vec_ref[4:5, :]
                out_ref[...] = (n2 * gain + vec_ref[5:6, :]).astype(BF)
                d_sum, d_gain, d_shift = norm_back(cot_ref[...].astype(F32), gain, n2, r2)
                d_sum_ref[...] = d_sum
                low = d_sum.astype(BF)
                d_ffn_ref[...] = low
                sums_ref[0:1, :] = jnp.sum(low.astype(F32), 0, keepdims=True)
                sums_ref[1:2, :] = d_gain
                sums_ref[2:3, :] = d_shift
                sums_ref[3:8, :] = jnp.zeros((5, d), F32)

    return pl.pallas_call(
        kernel, grid=(count,), in_specs=specs, out_specs=[o[1] for o in outs], out_shape=[o[0] for o in outs],
        scratch_shapes=[pltpu.VMEM((t, d), F32)], cost_estimate=COST,
        compiler_params=pltpu.CompilerParams(vmem_limit_bytes=56 * 2**20),
    )(*ins)


def write_split(tree, flipped, away_ref, column, low_ref, high_ref, kept, value):
    step = tree.nz * tree.rows
    order = tree.f_order(flipped)
    half, quarter = tree.width // 2, tree.width // 4
    n = value.shape[1]
    for at, f in enumerate(order):
        row = at * step
        away_ref[row : row + step, pl.ds(column, n)] = value[half + f * step : half + (f + 1) * step].astype(BF)
        ref, row = (low_ref, row) if row < quarter else (high_ref, row - quarter)
        ref[row : row + step, pl.ds(kept, n)] = value[f * step : (f + 1) * step].astype(BF)


def feed_back(tree, d_ffn, mixed_low, act, slope, up, dn, total, count, tail=None):
    t, d = d_ffn.shape
    n = len(up)
    tile = pl.BlockSpec((t, WIDE), lambda j: (0, j))
    ins = [d_ffn, mixed_low, act, slope, total] + [a for a, _ in up] + [a for a, _ in dn]
    specs = [whole((t, d))] * 2 + [tile] * 2 + [whole((t, d))] + column_blocks(up, WIDE, 0) + column_blocks(dn, WIDE, 0)
    shape = jax.ShapeDtypeStruct
    full = lambda dt: (shape((t, d), dt), whole((t, d)))
    n_up = count * WIDE + (0 if tail is None else d)
    n_dn = count * WIDE
    quarter = d // 4
    big = lambda r, c: (shape((r, c), BF), whole((r, c)))
    outs = [big(d // 2, n_up + n_dn), big(quarter, n_up), big(quarter, n_up), big(quarter, n_dn), big(quarter, n_dn)]
    outs += [(shape((1, count * WIDE), F32), pl.BlockSpec((1, WIDE), lambda j: (0, j)))]
    if tail is None:
        outs += [full(F32)]
    else:
        context, wo, n1, r1, gain = tail
        ins += [context, n1, r1, gain] + [a for a, _ in wo]
        specs += [whole((t, d)), whole((t, d)), whole((t, 1)), whole((1, d))] + column_blocks(wo, d, 0, 0)
        outs += [full(BF), full(BF), full(BF), (shape((8, d), F32), whole((8, d)))]

    def kernel(*refs):
        j = pl.program_id(0)
        d_ffn_ref, low_ref, act_ref, slope_ref, total_ref = refs[:5]
        refs = refs[5:]
        up_refs, dn_refs, refs = refs[:n], refs[n : 2 * n], refs[2 * n :]
        if tail is not None:
            ctx_ref, n1_ref, r1_ref, gain_ref = refs[:4]
            wo_refs, refs = refs[4 : 4 + n], refs[4 + n :]
        away_ref, up_lo, up_hi, dn_lo, dn_hi, d_bu_ref = refs[:6]
        refs = refs[6:]
        acc, d_ffn_t, low_t = refs[-3:]

        @pl.when(j == 0)
        def _():
            acc[...] = total_ref[...]
            d_ffn_t[...] = d_ffn_ref[...].T
            low_t[...] = low_ref[...].T

        d_up = (mm(d_ffn_ref[...], stack(dn_refs), 1, 0) * slope_ref[...].astype(F32)).astype(BF)
        d_bu_ref[...] = jnp.sum(d_up.astype(F32), 0, keepdims=True)
        at = pl.multiple_of(j * WIDE, WIDE)
        write_split(tree, True, away_ref, n_up + at, dn_lo, dn_hi, at, mm(d_ffn_t[...], act_ref[...], 1, 0))
        write_split(tree, False, away_ref, at, up_lo, up_hi, at, mm(low_t[...], d_up, 1, 0))
        acc[...] += mm(d_up, stack(up_refs), 1, 1)

        @pl.when(j == count - 1)
        def _():
            if tail is None:
                refs[0][...] = acc[...]
            else:
                d_attn_ref, rest_ref, d_ctx_ref, sums_ref = refs[:4]
                d_first, d_gain, d_shift = norm_back(acc[...], gain_ref[...], n1_ref[...], r1_ref[...])
                d_attn = d_first.astype(BF)
                d_attn_ref[...] = d_attn
                rest_ref[...] = (d_first - d_attn.astype(F32)).astype(BF)
                d_ctx_ref[...] = mm(d_attn, stack(wo_refs), 1, 0).astype(BF)
                d_ffn_t[...] = d_attn.T
                write_split(tree, False, away_ref, n_dn, up_lo, up_hi, n_dn, mm(d_ffn_t[...], ctx_ref[...], 1, 0))
                sums_ref[0:1, :] = jnp.sum(d_attn.astype(F32), 0, keepdims=True)
                sums_ref[1:2, :] = d_gain
                sums_ref[2:3, :] = d_shift
                sums_ref[3:8, :] = jnp.zeros((5, d), F32)

    return pl.pallas_call(
        kernel, grid=(count,), in_specs=specs, out_specs=[o[1] for o in outs], out_shape=[o[0] for o in outs],
        scratch_shapes=[pltpu.VMEM((t, d), F32), pltpu.VMEM((d, t), BF), pltpu.VMEM((d, t), BF)], cost_estimate=COST,
        compiler_params=pltpu.CompilerParams(vmem_limit_bytes=60 * 2**20),
    )(*ins)


def pack_first(query, key, value, table, vectors, up_bias):
    rows, d = query.shape
    buckets = table.shape[1]
    spread = up_bias.shape[0]
    wide = 3 * d + buckets + 128

    def kernel(q_ref, k_ref, v_ref, t_ref, *refs):
        vec_refs, ub_ref, out_ref, lines = refs[:-3], refs[-3], refs[-2], refs[-1]
        out_ref[:, 0:d] = q_ref[...].astype(BF)
        out_ref[:, d : 2 * d] = k_ref[...].astype(BF)
        out_ref[:, 2 * d : 3 * d] = v_ref[...].astype(BF)
        out_ref[:, 3 * d : 3 * d + buckets] = t_ref[...].astype(BF)
        lines[...] = jnp.zeros(lines.shape, F32)
        for i, r in enumerate(vec_refs):
            lines[i : i + 1, 0:rows] = r[...]
        lines[len(vec_refs) : len(vec_refs) + spread, 0:rows] = ub_ref[...]
        out_ref[:, 3 * d + buckets : wide] = lines[...].T[:rows].astype(BF)

    return pl.pallas_call(
        kernel, out_shape=jax.ShapeDtypeStruct((rows, wide), BF), scratch_shapes=[pltpu.VMEM((128, 128), F32)],
        cost_estimate=COST, compiler_params=pltpu.CompilerParams(vmem_limit_bytes=60 * 2**20),
    )(query, key, value, table, *[v.reshape(1, rows) for v in vectors], up_bias)


def pack_second(out_weight, up, down, cut):
    rows, ff = up.shape
    d = out_weight.shape[1]

    def kernel(o_ref, u_ref, d_ref, a_ref, b_ref):
        down_t = d_ref[...].astype(BF)
        a_ref[:, 0:d] = o_ref[...].astype(BF)
        a_ref[:, d : d + cut] = u_ref[:, 0:cut].astype(BF)
        a_ref[:, d + cut : d + 2 * cut] = down_t[:, 0:cut]
        b_ref[:, 0 : ff - cut] = u_ref[:, cut:ff].astype(BF)
        b_ref[:, ff - cut : 2 * (ff - cut)] = down_t[:, cut:ff]

    return pl.pallas_call(
        kernel, out_shape=[jax.ShapeDtypeStruct((rows, d + 2 * cut), BF), jax.ShapeDtypeStruct((rows, 2 * (ff - cut)), BF)],
        cost_estimate=COST, compiler_params=pltpu.CompilerParams(vmem_limit_bytes=60 * 2**20),
    )(out_weight, up, down)


def project(x_p, onehot, low, high, bias, tile):
    t, d = x_p.shape
    buckets = onehot.shape[1]
    n = len(low)
    per = d // tile
    clip = lambda j, a: jnp.clip(j - a * per, 0, per - 1)
    specs = [whole((t, d)), whole(onehot.shape), pl.BlockSpec((1, tile), lambda j: (0, j))]
    specs += piece_blocks(low, tile, lambda j: jnp.minimum(j, 2 * per - 1))
    specs += piece_blocks(high, tile, lambda j: clip(j, 2))
    specs += piece_blocks(high, buckets, lambda j: d // buckets)
    out = lambda a: pl.BlockSpec((t, tile), lambda j: (0, clip(j, a)))

    def kernel(x_ref, hot_ref, bias_ref, *refs):
        lows, highs, tables, refs = refs[:n], refs[n : 2 * n], refs[2 * n : 3 * n], refs[3 * n :]
        q_ref, k_ref, v_ref, ek_ref, eq_ref, table = refs
        j = pl.program_id(0)

        @pl.when(j == 0)
        def _():
            table[...] = mm(hot_ref[...], stack(tables), 1, 1).astype(BF)

        def both(out_ref, e_ref):
            w = stack(lows)
            out_ref[...] = (mm(x_ref[...], w, 1, 0) + bias_ref[...]).astype(BF)
            e_ref[...] = (mm(table[...], w, 1, 0) + bias_ref[...]).astype(BF)

        pl.when(j < per)(lambda: both(q_ref, eq_ref))
        pl.when((j >= per) & (j < 2 * per))(lambda: both(k_ref, ek_ref))

        @pl.when(j >= 2 * per)
        def _():
            v_ref[...] = (mm(x_ref[...], stack(highs), 1, 0) + bias_ref[...]).astype(BF)

    return pl.pallas_call(
        kernel, grid=(3 * per,), in_specs=specs, out_specs=[out(0), out(1), out(2), out(1), out(0)],
        out_shape=[jax.ShapeDtypeStruct((t, d), BF)] * 5, scratch_shapes=[pltpu.VMEM((t, d), BF)], cost_estimate=COST,
        compiler_params=pltpu.CompilerParams(vmem_limit_bytes=60 * 2**20),
    )(x_p, onehot, bias, *arrays(low), *arrays(high), *arrays(high))


def attention_grads(tree, x_p, onehot, low, high, dq, dk, dv, dek, deq, tile, part, carried=None):
    t, d = x_p.shape
    buckets = onehot.shape[1]
    n = len(low)
    per = d // tile
    last = carried is not None
    half, quarter = d // 2, d // 4
    col = pl.BlockSpec((t, tile), lambda j: (0, part))
    specs = [whole((t, d)), whole(onehot.shape)] + [col] * 5
    specs += piece_blocks(low, tile, lambda j: jnp.minimum(j, 1) * per + part)
    specs += piece_blocks(high, buckets, lambda j: d // buckets)
    ins = [x_p, onehot, dq, dk, dv, dek, deq] + arrays(low) + arrays(high)
    if last:
        ins += list(carried)
        specs += [whole(a.shape) for a in carried]
    wide = tile + (buckets + 128 if last else 0)
    shape = jax.ShapeDtypeStruct
    big = lambda r, c: (shape((r, c), BF), whole((r, c)))
    outs = [big(half, 2 * tile + wide), big(quarter, 2 * tile), big(quarter, 2 * tile), big(quarter, wide), big(quarter, wide)]
    if not last:
        outs += [(shape((d, buckets), F32), whole((d, buckets))), (shape((8, tile), F32), whole((8, tile)))]

    def kernel(*refs):
        x_ref, hot_ref, dq_ref, dk_ref, dv_ref, dek_ref, deq_ref = refs[:7]
        lows, tables, refs = refs[7 : 7 + n], refs[7 + n : 7 + 2 * n], refs[7 + 2 * n :]
        if last:
            before_ref, sums_before_ref, lines_ref, ordered_ref, place_ref = refs[:5]
            refs = refs[5:]
        away_ref, qk_lo, qk_hi, wide_lo, wide_hi = refs[:5]
        if last:
            x_t, table, d_table, sums = refs[5:]
        else:
            d_table, sums, x_t, table = refs[5:]
        j = pl.program_id(0)

        @pl.when(j == 0)
        def _():
            x_t[...] = x_ref[...].T
            table[...] = stack(tables)
            d_table[...] = before_ref[...] if last else jnp.zeros(d_table.shape, F32)
            sums[...] = jnp.zeros(sums.shape, F32)

        def wide_write(at, value):
            write_split(tree, True, away_ref, 2 * tile + at, wide_lo, wide_hi, at, value)

        def both(g_ref, e_ref, row):
            pos = mm(hot_ref[...], e_ref[...], 0, 0).astype(BF)
            g = g_ref[...]
            value = mm(x_t[...], g, 1, 0) + mm(table[...], pos, 1, 0)
            write_split(tree, False, away_ref, row * tile, qk_lo, qk_hi, row * tile, value)
            sums[row : row + 1, :] = jnp.sum(g.astype(F32), 0, keepdims=True) + jnp.sum(pos.astype(F32), 0, keepdims=True)
            d_table[...] += mm(stack(lows), pos, 1, 1)

        pl.when(j == 0)(lambda: both(dq_ref, deq_ref, 0))
        pl.when(j == 1)(lambda: both(dk_ref, dek_ref, 1))

        @pl.when(j == 2)
        def _():
            g = dv_ref[...]
            wide_write(0, mm(x_t[...], g, 1, 0))
            sums[2:3, :] = jnp.sum(g.astype(F32), 0, keepdims=True)
            if last:
                wide_write(tile, d_table[...])
                known = [sums_before_ref[0:3, i * tile : (i + 1) * tile] for i in range(per - 1)]
                vectors = jnp.concatenate([jnp.concatenate(known + [sums[0:3, :]], 1), lines_ref[...]], 0)
                pad = lambda v, lead: jnp.concatenate(
                    ([jnp.zeros((lead, d), F32)] if lead else []) + [v, jnp.zeros((128 - lead - v.shape[0], d), F32)], 0
                )
                natural = mm(place_ref[...], pad(vectors, 0).astype(BF), 1, 1)
                wide_write(tile + buckets, natural + pad(ordered_ref[...], 16).T)

    scratch = [pltpu.VMEM((d, t), BF), pltpu.VMEM((d, buckets), BF)]
    if last:
        scratch += [pltpu.VMEM((d, buckets), F32), pltpu.VMEM((8, tile), F32)]
    return pl.pallas_call(
        kernel, grid=(3,), in_specs=specs, out_specs=[o[1] for o in outs], out_shape=[o[0] for o in outs],
        scratch_shapes=scratch, cost_estimate=COST, compiler_params=pltpu.CompilerParams(vmem_limit_bytes=56 * 2**20),
    )(*ins)


def input_grads(d_attn, d_rest, low, high, dq, dk, dv, out_p, place_t, tile):
    t, d = d_attn.shape
    n = len(low)
    per = d // tile
    clip = lambda j, a: jnp.clip(j - a * per, 0, per - 1)
    col = lambda a: pl.BlockSpec((t, tile), lambda j: (0, clip(j, a)))
    specs = [whole((t, d)), whole((t, d)), col(0), col(1), col(2), whole((t, d)), whole((d, d))]
    specs += piece_blocks(low, tile, lambda j: jnp.minimum(j, 2 * per - 1))
    specs += piece_blocks(high, tile, lambda j: clip(j, 2))

    def kernel(*refs):
        a_ref, r_ref, dq_ref, dk_ref, dv_ref, out_ref, place_ref = refs[:7]
        lows, highs, refs = refs[7 : 7 + n], refs[7 + n : 7 + 2 * n], refs[7 + 2 * n :]
        grad_ref, layer_ref, acc = refs
        j = pl.program_id(0)

        @pl.when(j == 0)
        def _():
            acc[...] = a_ref[...].astype(F32) + r_ref[...].astype(F32)
            layer_ref[...] = mm(out_ref[...], place_ref[...], 1, 0).astype(BF)

        def add(g_ref, ws):
            acc[...] += mm(g_ref[...], stack(ws), 1, 1)

        pl.when(j < per)(lambda: add(dq_ref, lows))
        pl.when((j >= per) & (j < 2 * per))(lambda: add(dk_ref, lows))
        pl.when(j >= 2 * per)(lambda: add(dv_ref, highs))

        @pl.when(j == 3 * per - 1)
        def _():
            grad_ref[...] = mm(acc[...].astype(BF), place_ref[...], 1, 0).astype(BF)

    return pl.pallas_call(
        kernel, grid=(3 * per,), in_specs=specs, out_specs=[whole((t, d))] * 2,
        out_shape=[jax.ShapeDtypeStruct((t, d), BF)] * 2, scratch_shapes=[pltpu.VMEM((t, d), F32)], cost_estimate=COST,
        compiler_params=pltpu.CompilerParams(vmem_limit_bytes=48 * 2**20),
    )(d_attn, d_rest, dq, dk, dv, out_p, place_t, *arrays(low), *arrays(high))


class Tree:
    def __init__(self, width):
        self.nf, self.ndp = lax.axis_size("fsdp"), lax.axis_size("dp")
        self.n = self.nf * self.ndp
        self.nz = self.ndp // 2
        self.rows = width // self.n
        self.width = width
        self.f_bits = [1 << b for b in range(self.nf.bit_length() - 1)]
        self.z_bits = [1 << b for b in range(self.nz.bit_length() - 1)]

    def place(self, transposed):
        me = lax.axis_index("dp") * self.nf + lax.axis_index("fsdp")
        d = jnp.arange(self.width, dtype=jnp.int32)
        rel = (d // self.rows) ^ me
        f = rel % self.nf
        core = (rel // self.nf) % 2
        z = sum(((rel // (2 * self.nf * b)) % 2) * (self.nz // (2 * b)) for b in self.z_bits)
        at = ((core * self.nf + f) * self.nz + z) * self.rows + d % self.rows
        j = lax.broadcasted_iota(jnp.int32, (self.width, self.width), 0 if transposed else 1)
        return ((at[None, :] if transposed else at[:, None]) == j).astype(BF)

    def swap(self, a, axis, bit):
        size = self.nf if axis == "fsdp" else self.ndp
        return lax.ppermute(a, axis, [(i, i ^ bit) for i in range(size)])

    def f_order(self, flipped):
        order = self.f_bits[::-1] if flipped else self.f_bits
        key = lambda f: [f & bit != 0 for bit in order]
        return sorted(range(self.nf), key=key)

    def gather(self, cur, sides, direct=False):
        columns = [0]
        for width, _ in sides:
            columns.append(columns[-1] + width)
        if direct and self.nz <= 4:
            got = yield [(cur, "dp", 2 * z) for z in range(1, self.nz)]
            got = [cur] + list(got)
            near_first = sorted(range(self.nz), key=lambda z: [z & bit != 0 for bit in self.z_bits])
            cur = join([got[z] for z in near_first])
        else:
            for bit in self.z_bits[::-1]:
                (got,) = yield [(cur, "dp", 2 * bit)]
                cur = join([cur, got])
        found = [{0: (cur, c)} for c in columns[:-1]]
        orders = [self.f_bits[::-1] if flipped else self.f_bits for _, flipped in sides]
        every = range(len(sides))
        pending = [([(s, 0) for s in every], True, cur)]
        yield found, pending, columns
        sends = [([(s, bit) for s in every], True, (cur, "fsdp", bit)) for bit in self.f_bits]
        while sends:
            got = yield [x for _, _, x in sends]
            arrived, sends = sends, []
            for (keys, whole_row, _), g in zip(arrived, got):
                for s, i in keys:
                    found[s][i] = (g, columns[s] if whole_row else 0)
                pending.append((keys, whole_row, g))
            for keys, whole_row, _ in arrived:
                i = keys[0][1]
                for s, _ in keys:
                    array, column = found[s][i]
                    last = max(at for at, bit in enumerate(orders[s]) if i & bit)
                    for bit in orders[s][last + 1 :]:
                        part = array[:, column : column + columns[s + 1] - columns[s]]
                        sends.append(([(s, i | bit)], False, (part, "fsdp", bit)))


class Job:
    def __init__(self, tree, away, *sides):
        self.tree = tree
        self.away = away
        self.sides = [list(side) for side in sides]
        self.stages = ([] if away is None else ["core"]) + list(range(len(tree.f_bits))) + [("z", b) for b in tree.z_bits]
        self.total = None

    def wanted(self):
        if not self.stages:
            return []
        stage = self.stages[0]
        if stage == "core":
            return [(self.away, "dp", 1)]
        if isinstance(stage, int):
            bits = self.tree.f_bits
            return [(side[1], "fsdp", (bits[::-1] if side[2] else bits)[stage]) for side in self.sides]
        return [(self.total[1], "dp", 2 * stage[1])]

    def add(self, got):
        stage = self.stages.pop(0)
        more = bool(self.stages)
        total = lambda *xs: sum(x.astype(F32) for x in xs)
        sums = lambda *xs: total(*xs).astype(BF)
        if stage == "core":
            column = 0
            for side in self.sides:
                r, n = side[1].shape
                side[0] = [side[0], got[0][:r, column : column + n]]
                side[1] = sums(side[1], got[0][r:, column : column + n])
                column += n
        elif isinstance(stage, int):
            for side, g in zip(self.sides, got):
                known = side[0] if isinstance(side[0], list) else [side[0]]
                r = g.shape[0] // 2
                side[0], side[1] = sums(*[a[:r] for a in known], g[:r]), sums(*[a[r:] for a in known], g[r:])
            if not isinstance(self.stages[0], int):
                cat = lambda xs: xs[0] if len(xs) == 1 else jnp.concatenate(xs, 1)
                self.total = [cat([side[i] for side in self.sides]) for i in range(2)]
        else:
            keep = self.total[0]
            if more:
                r = keep.shape[0] // 2
                self.total = [sums(keep[:r], got[0][:r]), sums(keep[r:], got[0][r:])]
            else:
                self.total = keep.astype(F32) + got[0].astype(F32)

    def hold(self, arrays):
        stage = self.stages[0]
        if stage == "core":
            (self.away,) = arrays
        elif isinstance(stage, int):
            for side, a in zip(self.sides, arrays):
                side[1] = a
        else:
            self.total[1] = arrays[0]


class Flow:
    def __init__(self, tree, cur, sides, direct=False):
        self.tree = tree
        self.steps = tree.gather(cur, sides, direct)
        self.found = None
        self.linked = False
        self.next(None)

    def next(self, got):
        try:
            out = self.steps.send(got)
            if isinstance(out, tuple):
                self.found, self.pending, self.columns = out
                out = self.steps.send(None)
            self.sends = out
        except StopIteration:
            self.sends, self.linked = [], True

    def wanted(self):
        return list(self.sends)

    def add(self, got):
        self.next(got)

    def hold(self, arrays):
        self.sends = [(a,) + rest[1:] for a, rest in zip(arrays, self.sends)]

    def cores(self, most):
        return Cores(self, most)

    def rest(self):
        return Rest(self)

    @property
    def value(self):
        nf = self.tree.nf
        if not self.linked or any(len(f) < 2 * nf for f in self.found):
            return None
        return [[f[i] for i in range(2 * nf)] for f in self.found]


class Rest:
    def __init__(self, flow):
        self.flow = flow

    def wanted(self):
        return [] if self.flow.found is None else [(array, "dp", 1) for _, _, array in self.flow.pending]

    def hold(self, arrays):
        self.flow.pending[:] = [p[:2] + (a,) for p, a in zip(self.flow.pending, arrays)]


class Cores:
    def __init__(self, flow, most):
        self.flow = flow
        self.taken = [] if flow.found is None else flow.pending[:most]
        if self.taken:
            del flow.pending[: len(self.taken)]

    def wanted(self):
        return [(array, "dp", 1) for _, _, array in self.taken]

    def add(self, got):
        for (keys, whole_row, _), g in zip(self.taken, got):
            for s, i in keys:
                self.flow.found[s][self.flow.tree.nf + i] = (g, self.flow.columns[s] if whole_row else 0)


def drain(tree, flow):
    while flow.value is None:
        window(tree, [flow, flow.cores(5)])


def window(tree, works, others=(), later=()):
    works = [w for w in works if w.wanted()]
    later = [w for w in later if w.wanted()]
    sent = [[tree.swap(*x) for x in w.wanted()] for w in works]
    kept = [[x[0] for x in w.wanted()] for w in later]
    sent, kept, others = lax.optimization_barrier((sent, kept, tuple(others)))
    for w, arrays_in in zip(later, kept):
        w.hold(list(arrays_in))
    for w, got in zip(works, sent):
        w.add(list(got))
    return others


def per_device(
    tokens, segment_ids, rel_bucket, query_weight, query_bias, key_weight, key_bias, value_weight, value_bias,
    out_weight, out_bias, attention_gain, attention_shift, up_weight, up_bias, down_weight, down_bias,
    output_gain, output_shift, position_table, cotangent,
):
    x = tokens[0]
    t, d = x.shape
    seg = segment_ids[0]
    tree = Tree(d)
    rows = tree.rows
    ff = up_weight.shape[1]
    spread = ff // d
    buckets = position_table.shape[0]
    scale = 1.0 / math.sqrt(3.0 * (d // HEADS))
    vectors = (query_bias, key_bias, value_bias, out_bias, attention_gain, attention_shift, down_bias, output_gain, output_shift)
    cut = ff * 5 // 8
    late_cut = ff - cut
    lead = pack_first(query_weight, key_weight, value_weight, position_table.T, vectors, up_bias.reshape(spread, rows))
    one = Flow(tree, lead, [(2 * d, False), (d + buckets + 128, True)], True)
    place = tree.place(False)
    place_t = tree.place(True)
    half = t // 2
    picked = lax.rev(rel_bucket[t - half : 2 * t - half], (0,))
    onehot = (picked[:, None] == lax.broadcasted_iota(jnp.int32, (t, buckets), 1)).astype(BF)
    early, late = pack_second(out_weight.T, up_weight, down_weight.T, cut)
    early, late, place, place_t, onehot = window(tree, [one], (early, late, place, place_t, onehot))
    two = Flow(tree, early, [(d + cut, False), (cut, True)])
    arrange = lambda m: mm(m, place, 1, 0).astype(BF)
    x_p = arrange(x)
    late, x_p = window(tree, [one, one.cores(1), two], (late, x_p))
    three = Flow(tree, late, [(late_cut, False), (late_cut, True)])
    cot_p = arrange(cotangent[0])
    (cot_p,) = window(tree, [one, one.cores(1), two], (cot_p,))
    window(tree, [one, one.cores(3)], (), [two.rest()])
    drain(tree, one)
    low, high = one.value

    small = jnp.concatenate([a[:, c + d + buckets : c + d + buckets + 128] for a, c in high], 0)
    vec = mm(small, place, 0, 1)
    same = (lax.broadcasted_iota(jnp.int32, (d, d), 0) == lax.broadcasted_iota(jnp.int32, (d, d), 1)).astype(BF)
    vecs = mm(small[:, 3:11], same, 0, 0)
    bias = vec[:3].reshape(1, 3 * d)
    bu = vec[SPLIT : SPLIT + spread].reshape(spread, tree.n, rows).transpose(1, 0, 2).reshape(1, ff)
    q, k, v, ek, eq = project(x_p, onehot, low, high, bias, TILE)
    q, k, v, ek, eq, vecs, bu = window(tree, [three], (q, k, v, ek, eq, vecs, bu), [two.rest()])
    n_pairs = HEADS // 2
    cuts = (0, n_pairs // 8, n_pairs // 2, n_pairs)
    plans = (
        lambda: ([two, two.cores(1), three], [two.rest()]),
        lambda: ([two, two.cores(1)], [two.rest(), three.rest()]),
        lambda: ([two.cores(3), three], [three.rest()]),
    )
    made = None
    for begin, after, plan in zip(cuts, cuts[1:], plans):
        made = attend(q, k, v, ek, eq, seg, scale, made, begin, after - begin)
        works, later = plan()
        made = window(tree, works, made, later)
    context, probs = made

    drain(tree, two)
    wo = two.value[0]
    shifted = lambda pieces, by: [(a, c + by) for a, c in pieces]
    up_a, dn_early = shifted(wo, d), two.value[1]
    count, late_count = cut // WIDE, late_cut // WIDE
    act_a, slope_a, n1, r1, mixed, mixed_low, so_far = feed_forward(vecs, bu, up_a, dn_early, 0, count, (context, x_p, wo))
    (so_far,) = window(tree, [three, three.cores(3)], (so_far,))
    drain(tree, three)
    up_b, dn_late = three.value
    act_b, slope_b, out_p, d_sum, d_ffn, sums2 = feed_forward(
        vecs, bu, up_b, dn_late, count, late_count, (mixed, mixed_low, so_far), cot_p
    )
    back = feed_back(tree, d_ffn, mixed_low, act_a, slope_a, up_a, dn_early, d_sum, count)
    job_1 = Job(tree, back[0], (*back[1:3], False), (*back[3:5], True))
    d_bu_a, total = back[5:]
    back = feed_back(
        tree, d_ffn, mixed_low, act_b, slope_b, up_b, dn_late, total, late_count, (context, wo, n1, r1, vecs[1:2])
    )
    job_2 = Job(tree, back[0], (*back[1:3], False), (*back[3:5], True))
    d_bu_b, d_attn, d_rest, d_context, sums1 = back[5:]
    (d_context,) = window(tree, [job_1], (d_context,))

    args = (q, k, v, ek, eq, d_context, probs, scale)
    grads = attend_back(*args, None, 0, n_pairs * 3 // 4)
    grads = window(tree, [job_1, job_2], grads)
    split = attention_grads(tree, x_p, onehot, low, high, *grads, d // 2, 0)
    (*grads, d_table, sums) = window(tree, [job_1], (*grads, *split[5:]))
    job_3 = Job(tree, split[0], (*split[1:3], False), (*split[3:5], True))
    grads = attend_back(*args, grads, n_pairs * 3 // 4, n_pairs // 4)
    grads = window(tree, [job_3, job_1], grads)
    d_bu = jnp.concatenate([d_bu_a, d_bu_b], 1)
    lines = d_bu.reshape(tree.n, spread, rows).transpose(1, 0, 2).reshape(spread, d)
    ordered = jnp.concatenate([sums1[:3], sums2[:3]], 0)
    ordered = jnp.concatenate([ordered, jnp.zeros((2, d), F32)], 0)
    carried = (d_table, sums, lines, ordered, place_t)
    split = attention_grads(tree, x_p, onehot, low, high, *grads, d // 2, 1, carried)
    split = window(tree, [job_2, job_1], split)
    job_4 = Job(tree, split[0], (*split[1:3], False), (*split[3:5], True))
    dq, dk, dv, _, _ = grads
    d_attn, d_rest = window(tree, [job_4, job_2], (d_attn, d_rest))
    grad_layer = input_grads(d_attn, d_rest, low, high, dq, dk, dv, out_p, place_t, TILE)
    input_grad, layer_out = window(tree, [job_4, job_3, job_2], grad_layer)
    works = [job_4, job_3, job_2, job_1]
    while any(w.stages for w in works):
        window(tree, works)
    four, three, two, one = [w.total for w in works]
    h = d // 2
    up_a_grad, dn_a_grad = one[:, :cut], one[:, cut:]
    up_b_grad, out_grad, dn_b_grad = two[:, :late_cut], two[:, late_cut : late_cut + d], two[:, late_cut + d :]
    query_grad, key_grad, value_grad = [
        jnp.concatenate([three[:, i * h : (i + 1) * h], four[:, i * h : (i + 1) * h]], 1) for i in range(3)
    ]
    table_grad, tail = four[:, 3 * h : 3 * h + buckets], four[:, 3 * h + buckets :]
    d_bq, d_bk, d_bv = [tail[:, i] for i in range(3)]
    d_up_bias = tail[:, 3 : 3 + spread].T.reshape(-1)
    d_bo, d_gain1, d_shift1, d_bd, d_gain2, d_shift2 = [tail[:, 16 + i] for i in range(6)]
    return (
        layer_out[None], input_grad[None],
        query_grad, d_bq, key_grad, d_bk, value_grad, d_bv,
        out_grad.T, d_bo, d_gain1, d_shift1, jnp.concatenate([up_a_grad, up_b_grad], 1), d_up_bias,
        jnp.concatenate([dn_a_grad.T, dn_b_grad.T], 0), d_bd, d_gain2, d_shift2,
        table_grad.T,
    )


def solution(mesh):
    both = ("dp", "fsdp")
    row, col, vec = P(both, None), P(None, both), P(both)
    seq = P(both, None, None)
    params = (row, vec, row, vec, row, vec, col, vec, vec, vec, row, vec, col, vec, vec, vec, col)
    return jax.shard_map(
        per_device, mesh=mesh, in_specs=(seq, row, P()) + params + (seq,), out_specs=(seq, seq) + params, check_vma=False
    )
```

```python
import math
import jax, jax.numpy as jnp
from jax import lax
from jax.sharding import PartitionSpec as P
import jax.experimental.pallas as pl, jax.experimental.pallas.tpu as pltpu
HEADS=16
BF=jnp.bfloat16
F32=jnp.float32
COST=pl.CostEstimate(flops=10**9,bytes_accessed=10**6,transcendentals=0)

def mm(a,b,ca,cb):
    return lax.dot_general(a,b,(((ca,),(cb,)),((),())),preferred_element_type=F32)

def attend_kernel(scale, q_ref,k_ref,v_ref,ek_ref,eq_ref,segc_ref,segr_ref,ctx_ref,p_ref):
    t=q_ref.shape[0]; half=t//2
    hd=q_ref.shape[1]//2
    same=segc_ref[...]==segr_ref[...]
    lane=lax.broadcasted_iota(jnp.int32,q_ref.shape,1)
    ctx=None
    for h in range(2):
        mine=(lane>=h*hd)&(lane<(h+1)*hd)
        pick=lambda r: jnp.where(mine,r[...],jnp.zeros((),BF))
        q=pick(q_ref); k=pick(k_ref)
        s=mm(q,k_ref[...],1,1)
        to=pltpu.roll(mm(q,ek_ref[...],1,1),half,1,stride=1,stride_axis=0)
        fr=pltpu.roll(mm(k,eq_ref[...],1,1),half,1,stride=1,stride_axis=0)
        s=jnp.where(same,s+to+fr.T,-1e30)
        top=jnp.max(s,axis=1,keepdims=True)
        e=jnp.exp((s-top)*scale)
        p=(e*(1.0/jnp.sum(e,axis=1,keepdims=True))).astype(BF)
        p_ref[h]=p
        part=mm(p,pick(v_ref),1,0)
        ctx=part if ctx is None else ctx+part
    ctx_ref[...]=ctx.astype(BF)

def attend(q,k,v,ek,eq,seg,scale,made,at,count):
    t,d=q.shape
    w=2*d//HEADS
    col=pl.BlockSpec((t,w),lambda i:(0,i+at))
    made=[] if made is None else list(made)
    return pl.pallas_call(
        lambda *r: attend_kernel(scale,*r[:7],*r[len(r)-2:]),
        grid=(count,),
        in_specs=[col]*5+[pl.BlockSpec((t,1),lambda i:(0,0)),pl.BlockSpec((1,t),lambda i:(0,0))]+[pl.BlockSpec(memory_space=pl.ANY)]*len(made),
        out_specs=[col,pl.BlockSpec((2,t,t),lambda i:(i+at,0,0))],
        out_shape=[jax.ShapeDtypeStruct((t,d),BF),jax.ShapeDtypeStruct((HEADS,t,t),BF)],
        input_output_aliases={7+i:i for i in range(len(made))},
        cost_estimate=COST,
        compiler_params=pltpu.CompilerParams(vmem_limit_bytes=60 * 2**20),
    )(q,k,v,ek,eq,seg.reshape(t,1),seg.reshape(1,t),*made)

def attend_back_kernel(scale,q_ref,k_ref,v_ref,ek_ref,eq_ref,dc_ref,p_ref,dq_ref,dk_ref,dv_ref,dek_ref,deq_ref):
    t=q_ref.shape[0]; half=t//2
    hd=q_ref.shape[1]//2
    r=lax.broadcasted_iota(jnp.int32,(half,half),0); c=lax.broadcasted_iota(jnp.int32,(half,half),1)
    flip=(r+c==half-1).astype(BF)
    lane=lax.broadcasted_iota(jnp.int32,q_ref.shape,1)
    def turn(x):
        return jnp.concatenate([mm(flip,x[:half],1,0),mm(flip,x[half:],1,0)],0)
    def turn_t(x):
        return jnp.concatenate([mm(flip,x[:,:half],1,1),mm(flip,x[:,half:],1,1)],0)
    def unroll(x):
        return jnp.concatenate([pltpu.roll(x[:half],1,1,stride=1,stride_axis=0),pltpu.roll(x[half:],half+1,1,stride=1,stride_axis=0)],0)
    q_turned=turn(q_ref[...]).astype(BF); k_turned=turn(k_ref[...]).astype(BF)
    dqt=dkt=dv=dek=deq=None
    plus=lambda a,b: b if a is None else a+b
    for h in range(2):
        mine=(lane>=h*hd)&(lane<(h+1)*hd)
        pick=lambda x: jnp.where(mine,x,jnp.zeros((),BF))
        p=p_ref[h]; dc=pick(dc_ref[...])
        dp=mm(dc,v_ref[...],1,1)
        pf=p.astype(F32)
        w=pf*dp
        ds=(w-pf*jnp.sum(w,axis=1,keepdims=True)).astype(BF)
        dv=plus(dv,mm(p,dc,0,0))
        a=turn(ds).astype(BF); au=unroll(a)
        b=turn_t(ds).astype(BF); bu=unroll(b)
        dqt=plus(dqt,mm(a,pick(k_ref[...]),1,0)+mm(au,pick(ek_ref[...]),1,0))
        dkt=plus(dkt,mm(b,pick(q_ref[...]),1,0)+mm(bu,pick(eq_ref[...]),1,0))
        dek=plus(dek,mm(au,pick(q_turned),0,0))
        deq=plus(deq,mm(bu,pick(k_turned),0,0))
    dq_ref[...]=turn((dqt*scale).astype(BF)).astype(BF)
    dk_ref[...]=turn((dkt*scale).astype(BF)).astype(BF)
    dv_ref[...]=dv.astype(BF)
    dek_ref[...]=(dek*scale).astype(BF)
    deq_ref[...]=(deq*scale).astype(BF)

def attend_back(q,k,v,ek,eq,dc,p,scale,grads,at,count):
    t,d=q.shape
    w=2*d//HEADS
    col=pl.BlockSpec((t,w),lambda i:(0,i+at))
    grads=[] if grads is None else list(grads)
    return pl.pallas_call(
        lambda *r: attend_back_kernel(scale,*r[:7],*r[len(r)-5:]),
        grid=(count,),
        in_specs=[col]*6+[pl.BlockSpec((2,t,t),lambda i:(i+at,0,0))]+[pl.BlockSpec(memory_space=pl.ANY)]*len(grads),
        out_specs=[col]*5,
        out_shape=[jax.ShapeDtypeStruct((t,d),BF)]*5,
        input_output_aliases={7+i:i for i in range(len(grads))},
        cost_estimate=COST,
        compiler_params=pltpu.CompilerParams(vmem_limit_bytes=60 * 2**20),
    )(q,k,v,ek,eq,dc,p,*grads)


NORM_EPS = 1e-7
SPLIT = 9
TILE = 512
WIDE = 512


def norm_parts(v):
    mean = jnp.mean(v, axis=-1, keepdims=True)
    c = v - mean
    r = lax.rsqrt(jnp.mean(c * c, axis=-1, keepdims=True) + NORM_EPS)
    return c * r, r


def norm_back(g, gain, n, r):
    u = g * gain
    d = r * (u - jnp.mean(u, -1, keepdims=True) - n * jnp.mean(u * n, -1, keepdims=True))
    return d, jnp.sum(g * n, 0, keepdims=True), jnp.sum(g, 0, keepdims=True)


def stack(refs):
    return jnp.concatenate([r[...] for r in refs], 0) if len(refs) > 1 else refs[0][...]


def whole(shape):
    return pl.BlockSpec(shape, lambda j: (0,) * len(shape))


def join(blocks):
    rows, n = blocks[0].shape
    if rows % 16:
        return jnp.concatenate(blocks, 0)

    def kernel(*refs):
        for i, r in enumerate(refs[:-1]):
            refs[-1][i * rows : (i + 1) * rows, :] = r[...]

    return pl.pallas_call(
        kernel, out_shape=jax.ShapeDtypeStruct((rows * len(blocks), n), BF), cost_estimate=COST,
        compiler_params=pltpu.CompilerParams(vmem_limit_bytes=16 * 2**20),
    )(*blocks)


def arrays(pieces):
    return [a for a, _ in pieces]


def piece_blocks(pieces, width, block):
    out = []
    for array, column in pieces:
        out.append(pl.BlockSpec((array.shape[0], width), lambda j, base=column // width: (0, base + block(j))))
    return out


def column_blocks(pieces, width, first, step=1):
    return piece_blocks(pieces, width, lambda j: first + step * j)


def feed_forward(vecs, bu, up, dn, first, count, start=None, end=None):
    opening = len(start) == 3 and isinstance(start[2], list)
    n = len(up)
    if opening:
        context, x, wo = start
        t, d = x.shape
        ins = [context, x] + [a for a, _ in wo]
        specs = [whole((t, d))] * 2 + column_blocks(wo, d, 0, 0)
    else:
        t, d = start[0].shape
        ins, specs = list(start), [whole((t, d))] * 3
    n_start = len(ins)
    ins += [vecs, bu] + [a for a, _ in up] + [a for a, _ in dn] + ([] if end is None else [end])
    specs += [whole(vecs.shape), pl.BlockSpec((1, WIDE), lambda j: (0, j + first))]
    specs += column_blocks(up, WIDE, 0) + column_blocks(dn, WIDE, 0) + ([] if end is None else [whole((t, d))])
    shape = jax.ShapeDtypeStruct
    tile_out = pl.BlockSpec((t, WIDE), lambda j: (0, j))
    outs = [(shape((t, count * WIDE), BF), tile_out)] * 2
    full = lambda dt: (shape((t, d), dt), whole((t, d)))
    if opening:
        outs += [full(F32), (shape((t, 1), F32), whole((t, 1))), full(F32), full(BF)]
    if end is None:
        outs += [full(F32)]
    else:
        outs += [full(BF), full(F32), full(BF), (shape((8, d), F32), whole((8, d)))]

    def kernel(*refs):
        j = pl.program_id(0)
        begin, refs = refs[:n_start], refs[n_start:]
        vec_ref, bu_ref, refs = refs[0], refs[1], refs[2:]
        up_refs, dn_refs, refs = refs[:n], refs[n : 2 * n], refs[2 * n :]
        if end is not None:
            cot_ref, refs = refs[0], refs[1:]
        act_ref, slope_ref, refs = refs[0], refs[1], refs[2:]
        if opening:
            n1_ref, r1_ref, mixed_ref, low_ref = refs[:4]
            refs = refs[4:]
        else:
            mixed_ref, low_ref = begin[:2]
        acc = refs[-1]

        @pl.when(j == 0)
        def _():
            if opening:
                v = begin[1][...].astype(F32) + mm(begin[0][...], stack(begin[2:]), 1, 1) + vec_ref[0:1, :]
                n1, r1 = norm_parts(v)
                n1_ref[...] = n1
                r1_ref[...] = r1
                mixed = n1 * vec_ref[1:2, :] + vec_ref[2:3, :]
                mixed_ref[...] = mixed
                low_ref[...] = mixed.astype(BF)
                acc[...] = jnp.zeros(acc.shape, F32)
            else:
                acc[...] = begin[2][...]

        up_val = mm(low_ref[...], stack(up_refs), 1, 0) + bu_ref[...]
        cdf = 0.5 * (1.0 + lax.erf(up_val * math.sqrt(0.5)))
        act = (up_val * cdf).astype(BF)
        act_ref[...] = act
        slope_ref[...] = (cdf + up_val * (jnp.exp(-0.5 * up_val * up_val) * (1.0 / math.sqrt(2.0 * math.pi)))).astype(BF)
        acc[...] += mm(act, stack(dn_refs), 1, 1)

        @pl.when(j == count - 1)
        def _():
            if end is None:
                refs[0][...] = acc[...]
            else:
                out_ref, d_sum_ref, d_ffn_ref, sums_ref = refs[:4]
                n2, r2 = norm_parts(mixed_ref[...] + acc[...] + vec_ref[3:4, :])
                gain = vec_ref[4:5, :]
                out_ref[...] = (n2 * gain + vec_ref[5:6, :]).astype(BF)
                d_sum, d_gain, d_shift = norm_back(cot_ref[...].astype(F32), gain, n2, r2)
                d_sum_ref[...] = d_sum
                low = d_sum.astype(BF)
                d_ffn_ref[...] = low
                sums_ref[0:1, :] = jnp.sum(low.astype(F32), 0, keepdims=True)
                sums_ref[1:2, :] = d_gain
                sums_ref[2:3, :] = d_shift
                sums_ref[3:8, :] = jnp.zeros((5, d), F32)

    return pl.pallas_call(
        kernel, grid=(count,), in_specs=specs, out_specs=[o[1] for o in outs], out_shape=[o[0] for o in outs],
        scratch_shapes=[pltpu.VMEM((t, d), F32)], cost_estimate=COST,
        compiler_params=pltpu.CompilerParams(vmem_limit_bytes=50 * 2**20),
    )(*ins)


def write_split(tree, flipped, away_ref, column, low_ref, high_ref, kept, value):
    step = tree.nz * tree.rows
    order = tree.f_order(flipped)
    half, quarter = tree.width // 2, tree.width // 4
    n = value.shape[1]
    for at, f in enumerate(order):
        row = at * step
        away_ref[row : row + step, pl.ds(column, n)] = value[half + f * step : half + (f + 1) * step].astype(BF)
        ref, row = (low_ref, row) if row < quarter else (high_ref, row - quarter)
        ref[row : row + step, pl.ds(kept, n)] = value[f * step : (f + 1) * step].astype(BF)


def feed_back(tree, d_ffn, mixed_low, act, slope, up, dn, total, count, tail=None):
    t, d = d_ffn.shape
    n = len(up)
    tile = pl.BlockSpec((t, WIDE), lambda j: (0, j))
    ins = [d_ffn, mixed_low, act, slope, total] + [a for a, _ in up] + [a for a, _ in dn]
    specs = [whole((t, d))] * 2 + [tile] * 2 + [whole((t, d))] + column_blocks(up, WIDE, 0) + column_blocks(dn, WIDE, 0)
    shape = jax.ShapeDtypeStruct
    full = lambda dt: (shape((t, d), dt), whole((t, d)))
    n_up = count * WIDE + (0 if tail is None else d)
    n_dn = count * WIDE
    quarter = d // 4
    big = lambda r, c: (shape((r, c), BF), whole((r, c)))
    outs = [big(d // 2, n_up + n_dn), big(quarter, n_up), big(quarter, n_up), big(quarter, n_dn), big(quarter, n_dn)]
    outs += [(shape((1, count * WIDE), F32), pl.BlockSpec((1, WIDE), lambda j: (0, j)))]
    if tail is None:
        outs += [full(F32)]
    else:
        context, wo, n1, r1, gain = tail
        ins += [context, n1, r1, gain] + [a for a, _ in wo]
        specs += [whole((t, d)), whole((t, d)), whole((t, 1)), whole((1, d))] + column_blocks(wo, d, 0, 0)
        outs += [full(BF), full(BF), full(BF), (shape((8, d), F32), whole((8, d)))]

    def kernel(*refs):
        j = pl.program_id(0)
        d_ffn_ref, low_ref, act_ref, slope_ref, total_ref = refs[:5]
        refs = refs[5:]
        up_refs, dn_refs, refs = refs[:n], refs[n : 2 * n], refs[2 * n :]
        if tail is not None:
            ctx_ref, n1_ref, r1_ref, gain_ref = refs[:4]
            wo_refs, refs = refs[4 : 4 + n], refs[4 + n :]
        away_ref, up_lo, up_hi, dn_lo, dn_hi, d_bu_ref = refs[:6]
        refs = refs[6:]
        acc, d_ffn_t, low_t = refs[-3:]

        @pl.when(j == 0)
        def _():
            acc[...] = total_ref[...]
            d_ffn_t[...] = d_ffn_ref[...].T
            low_t[...] = low_ref[...].T

        d_up = (mm(d_ffn_ref[...], stack(dn_refs), 1, 0) * slope_ref[...].astype(F32)).astype(BF)
        d_bu_ref[...] = jnp.sum(d_up.astype(F32), 0, keepdims=True)
        at = pl.multiple_of(j * WIDE, WIDE)
        write_split(tree, True, away_ref, n_up + at, dn_lo, dn_hi, at, mm(d_ffn_t[...], act_ref[...], 1, 0))
        write_split(tree, False, away_ref, at, up_lo, up_hi, at, mm(low_t[...], d_up, 1, 0))
        acc[...] += mm(d_up, stack(up_refs), 1, 1)

        @pl.when(j == count - 1)
        def _():
            if tail is None:
                refs[0][...] = acc[...]
            else:
                d_attn_ref, rest_ref, d_ctx_ref, sums_ref = refs[:4]
                d_first, d_gain, d_shift = norm_back(acc[...], gain_ref[...], n1_ref[...], r1_ref[...])
                d_attn = d_first.astype(BF)
                d_attn_ref[...] = d_attn
                rest_ref[...] = (d_first - d_attn.astype(F32)).astype(BF)
                d_ctx_ref[...] = mm(d_attn, stack(wo_refs), 1, 0).astype(BF)
                d_ffn_t[...] = d_attn.T
                write_split(tree, False, away_ref, n_dn, up_lo, up_hi, n_dn, mm(d_ffn_t[...], ctx_ref[...], 1, 0))
                sums_ref[0:1, :] = jnp.sum(d_attn.astype(F32), 0, keepdims=True)
                sums_ref[1:2, :] = d_gain
                sums_ref[2:3, :] = d_shift
                sums_ref[3:8, :] = jnp.zeros((5, d), F32)

    return pl.pallas_call(
        kernel, grid=(count,), in_specs=specs, out_specs=[o[1] for o in outs], out_shape=[o[0] for o in outs],
        scratch_shapes=[pltpu.VMEM((t, d), F32), pltpu.VMEM((d, t), BF), pltpu.VMEM((d, t), BF)], cost_estimate=COST,
        compiler_params=pltpu.CompilerParams(vmem_limit_bytes=60 * 2**20),
    )(*ins)


def pack_first(query, key, value, table, vectors, up_bias):
    rows, d = query.shape
    buckets = table.shape[1]
    spread = up_bias.shape[0]
    wide = 3 * d + buckets + 128

    def kernel(q_ref, k_ref, v_ref, t_ref, *refs):
        vec_refs, ub_ref, out_ref, lines = refs[:-3], refs[-3], refs[-2], refs[-1]
        out_ref[:, 0:d] = q_ref[...].astype(BF)
        out_ref[:, d : 2 * d] = k_ref[...].astype(BF)
        out_ref[:, 2 * d : 3 * d] = v_ref[...].astype(BF)
        out_ref[:, 3 * d : 3 * d + buckets] = t_ref[...].astype(BF)
        lines[...] = jnp.zeros(lines.shape, F32)
        for i, r in enumerate(vec_refs):
            lines[i : i + 1, 0:rows] = r[...]
        lines[len(vec_refs) : len(vec_refs) + spread, 0:rows] = ub_ref[...]
        out_ref[:, 3 * d + buckets : wide] = lines[...].T[:rows].astype(BF)

    return pl.pallas_call(
        kernel, out_shape=jax.ShapeDtypeStruct((rows, wide), BF), scratch_shapes=[pltpu.VMEM((128, 128), F32)],
        cost_estimate=COST, compiler_params=pltpu.CompilerParams(vmem_limit_bytes=60 * 2**20),
    )(query, key, value, table, *[v.reshape(1, rows) for v in vectors], up_bias)


def pack_second(out_weight, up, down, cut):
    rows, ff = up.shape
    d = out_weight.shape[1]

    def kernel(o_ref, u_ref, d_ref, a_ref, b_ref):
        down_t = d_ref[...].astype(BF)
        a_ref[:, 0:d] = o_ref[...].astype(BF)
        a_ref[:, d : d + cut] = u_ref[:, 0:cut].astype(BF)
        a_ref[:, d + cut : d + 2 * cut] = down_t[:, 0:cut]
        b_ref[:, 0 : ff - cut] = u_ref[:, cut:ff].astype(BF)
        b_ref[:, ff - cut : 2 * (ff - cut)] = down_t[:, cut:ff]

    return pl.pallas_call(
        kernel, out_shape=[jax.ShapeDtypeStruct((rows, d + 2 * cut), BF), jax.ShapeDtypeStruct((rows, 2 * (ff - cut)), BF)],
        cost_estimate=COST, compiler_params=pltpu.CompilerParams(vmem_limit_bytes=60 * 2**20),
    )(out_weight, up, down)


def project(x_p, onehot, low, high, bias, tile):
    t, d = x_p.shape
    buckets = onehot.shape[1]
    n = len(low)
    per = d // tile
    clip = lambda j, a: jnp.clip(j - a * per, 0, per - 1)
    specs = [whole((t, d)), whole(onehot.shape), pl.BlockSpec((1, tile), lambda j: (0, j))]
    specs += piece_blocks(low, tile, lambda j: jnp.minimum(j, 2 * per - 1))
    specs += piece_blocks(high, tile, lambda j: clip(j, 2))
    specs += piece_blocks(high, buckets, lambda j: d // buckets)
    out = lambda a: pl.BlockSpec((t, tile), lambda j: (0, clip(j, a)))

    def kernel(x_ref, hot_ref, bias_ref, *refs):
        lows, highs, tables, refs = refs[:n], refs[n : 2 * n], refs[2 * n : 3 * n], refs[3 * n :]
        q_ref, k_ref, v_ref, ek_ref, eq_ref, table = refs
        j = pl.program_id(0)

        @pl.when(j == 0)
        def _():
            table[...] = mm(hot_ref[...], stack(tables), 1, 1).astype(BF)

        def both(out_ref, e_ref):
            w = stack(lows)
            out_ref[...] = (mm(x_ref[...], w, 1, 0) + bias_ref[...]).astype(BF)
            e_ref[...] = (mm(table[...], w, 1, 0) + bias_ref[...]).astype(BF)

        pl.when(j < per)(lambda: both(q_ref, eq_ref))
        pl.when((j >= per) & (j < 2 * per))(lambda: both(k_ref, ek_ref))

        @pl.when(j >= 2 * per)
        def _():
            v_ref[...] = (mm(x_ref[...], stack(highs), 1, 0) + bias_ref[...]).astype(BF)

    return pl.pallas_call(
        kernel, grid=(3 * per,), in_specs=specs, out_specs=[out(0), out(1), out(2), out(1), out(0)],
        out_shape=[jax.ShapeDtypeStruct((t, d), BF)] * 5, scratch_shapes=[pltpu.VMEM((t, d), BF)], cost_estimate=COST,
        compiler_params=pltpu.CompilerParams(vmem_limit_bytes=60 * 2**20),
    )(x_p, onehot, bias, *arrays(low), *arrays(high), *arrays(high))


def attention_grads(tree, x_p, onehot, low, high, dq, dk, dv, dek, deq, tile, part, carried=None):
    t, d = x_p.shape
    buckets = onehot.shape[1]
    n = len(low)
    per = d // tile
    last = carried is not None
    half, quarter = d // 2, d // 4
    col = pl.BlockSpec((t, tile), lambda j: (0, part))
    specs = [whole((t, d)), whole(onehot.shape)] + [col] * 5
    specs += piece_blocks(low, tile, lambda j: jnp.minimum(j, 1) * per + part)
    specs += piece_blocks(high, buckets, lambda j: d // buckets)
    ins = [x_p, onehot, dq, dk, dv, dek, deq] + arrays(low) + arrays(high)
    if last:
        ins += list(carried)
        specs += [whole(a.shape) for a in carried]
    wide = tile + (buckets + 128 if last else 0)
    shape = jax.ShapeDtypeStruct
    big = lambda r, c: (shape((r, c), BF), whole((r, c)))
    outs = [big(half, 2 * tile + wide), big(quarter, 2 * tile), big(quarter, 2 * tile), big(quarter, wide), big(quarter, wide)]
    if not last:
        outs += [(shape((d, buckets), F32), whole((d, buckets))), (shape((8, tile), F32), whole((8, tile)))]

    def kernel(*refs):
        x_ref, hot_ref, dq_ref, dk_ref, dv_ref, dek_ref, deq_ref = refs[:7]
        lows, tables, refs = refs[7 : 7 + n], refs[7 + n : 7 + 2 * n], refs[7 + 2 * n :]
        if last:
            before_ref, sums_before_ref, lines_ref, ordered_ref, place_ref = refs[:5]
            refs = refs[5:]
        away_ref, qk_lo, qk_hi, wide_lo, wide_hi = refs[:5]
        if last:
            x_t, table, d_table, sums = refs[5:]
        else:
            d_table, sums, x_t, table = refs[5:]
        j = pl.program_id(0)

        @pl.when(j == 0)
        def _():
            x_t[...] = x_ref[...].T
            table[...] = stack(tables)
            d_table[...] = before_ref[...] if last else jnp.zeros(d_table.shape, F32)
            sums[...] = jnp.zeros(sums.shape, F32)

        def wide_write(at, value):
            write_split(tree, True, away_ref, 2 * tile + at, wide_lo, wide_hi, at, value)

        def both(g_ref, e_ref, row):
            pos = mm(hot_ref[...], e_ref[...], 0, 0).astype(BF)
            g = g_ref[...]
            value = mm(x_t[...], g, 1, 0) + mm(table[...], pos, 1, 0)
            write_split(tree, False, away_ref, row * tile, qk_lo, qk_hi, row * tile, value)
            sums[row : row + 1, :] = jnp.sum(g.astype(F32), 0, keepdims=True) + jnp.sum(pos.astype(F32), 0, keepdims=True)
            d_table[...] += mm(stack(lows), pos, 1, 1)

        pl.when(j == 0)(lambda: both(dq_ref, deq_ref, 0))
        pl.when(j == 1)(lambda: both(dk_ref, dek_ref, 1))

        @pl.when(j == 2)
        def _():
            g = dv_ref[...]
            wide_write(0, mm(x_t[...], g, 1, 0))
            sums[2:3, :] = jnp.sum(g.astype(F32), 0, keepdims=True)
            if last:
                wide_write(tile, d_table[...])
                known = [sums_before_ref[0:3, i * tile : (i + 1) * tile] for i in range(per - 1)]
                vectors = jnp.concatenate([jnp.concatenate(known + [sums[0:3, :]], 1), lines_ref[...]], 0)
                pad = lambda v, lead: jnp.concatenate(
                    ([jnp.zeros((lead, d), F32)] if lead else []) + [v, jnp.zeros((128 - lead - v.shape[0], d), F32)], 0
                )
                natural = mm(place_ref[...], pad(vectors, 0).astype(BF), 1, 1)
                wide_write(tile + buckets, natural + pad(ordered_ref[...], 16).T)

    scratch = [pltpu.VMEM((d, t), BF), pltpu.VMEM((d, buckets), BF)]
    if last:
        scratch += [pltpu.VMEM((d, buckets), F32), pltpu.VMEM((8, tile), F32)]
    return pl.pallas_call(
        kernel, grid=(3,), in_specs=specs, out_specs=[o[1] for o in outs], out_shape=[o[0] for o in outs],
        scratch_shapes=scratch, cost_estimate=COST, compiler_params=pltpu.CompilerParams(vmem_limit_bytes=56 * 2**20),
    )(*ins)


def input_grads(d_attn, d_rest, low, high, dq, dk, dv, out_p, place_t, tile):
    t, d = d_attn.shape
    n = len(low)
    per = d // tile
    clip = lambda j, a: jnp.clip(j - a * per, 0, per - 1)
    col = lambda a: pl.BlockSpec((t, tile), lambda j: (0, clip(j, a)))
    specs = [whole((t, d)), whole((t, d)), col(0), col(1), col(2), whole((t, d)), whole((d, d))]
    specs += piece_blocks(low, tile, lambda j: jnp.minimum(j, 2 * per - 1))
    specs += piece_blocks(high, tile, lambda j: clip(j, 2))

    def kernel(*refs):
        a_ref, r_ref, dq_ref, dk_ref, dv_ref, out_ref, place_ref = refs[:7]
        lows, highs, refs = refs[7 : 7 + n], refs[7 + n : 7 + 2 * n], refs[7 + 2 * n :]
        grad_ref, layer_ref, acc = refs
        j = pl.program_id(0)

        @pl.when(j == 0)
        def _():
            acc[...] = a_ref[...].astype(F32) + r_ref[...].astype(F32)
            layer_ref[...] = mm(out_ref[...], place_ref[...], 1, 0).astype(BF)

        def add(g_ref, ws):
            acc[...] += mm(g_ref[...], stack(ws), 1, 1)

        pl.when(j < per)(lambda: add(dq_ref, lows))
        pl.when((j >= per) & (j < 2 * per))(lambda: add(dk_ref, lows))
        pl.when(j >= 2 * per)(lambda: add(dv_ref, highs))

        @pl.when(j == 3 * per - 1)
        def _():
            grad_ref[...] = mm(acc[...].astype(BF), place_ref[...], 1, 0).astype(BF)

    return pl.pallas_call(
        kernel, grid=(3 * per,), in_specs=specs, out_specs=[whole((t, d))] * 2,
        out_shape=[jax.ShapeDtypeStruct((t, d), BF)] * 2, scratch_shapes=[pltpu.VMEM((t, d), F32)], cost_estimate=COST,
        compiler_params=pltpu.CompilerParams(vmem_limit_bytes=48 * 2**20),
    )(d_attn, d_rest, dq, dk, dv, out_p, place_t, *arrays(low), *arrays(high))


class Tree:
    def __init__(self, width):
        self.nf, self.ndp = lax.axis_size("fsdp"), lax.axis_size("dp")
        self.n = self.nf * self.ndp
        self.nz = self.ndp // 2
        self.rows = width // self.n
        self.width = width
        self.f_bits = [1 << b for b in range(self.nf.bit_length() - 1)]
        self.z_bits = [1 << b for b in range(self.nz.bit_length() - 1)]

    def place(self, transposed):
        me = lax.axis_index("dp") * self.nf + lax.axis_index("fsdp")
        d = jnp.arange(self.width, dtype=jnp.int32)
        rel = (d // self.rows) ^ me
        f = rel % self.nf
        core = (rel // self.nf) % 2
        z = sum(((rel // (2 * self.nf * b)) % 2) * (self.nz // (2 * b)) for b in self.z_bits)
        at = ((core * self.nf + f) * self.nz + z) * self.rows + d % self.rows
        j = lax.broadcasted_iota(jnp.int32, (self.width, self.width), 0 if transposed else 1)
        return ((at[None, :] if transposed else at[:, None]) == j).astype(BF)

    def swap(self, a, axis, bit):
        size = self.nf if axis == "fsdp" else self.ndp
        return lax.ppermute(a, axis, [(i, i ^ bit) for i in range(size)])

    def f_order(self, flipped):
        order = self.f_bits[::-1] if flipped else self.f_bits
        key = lambda f: [f & bit != 0 for bit in order]
        return sorted(range(self.nf), key=key)

    def gather(self, cur, sides, direct=False):
        columns = [0]
        for width, _ in sides:
            columns.append(columns[-1] + width)
        if direct and self.nz <= 4:
            got = yield [(cur, "dp", 2 * z) for z in range(1, self.nz)]
            got = [cur] + list(got)
            near_first = sorted(range(self.nz), key=lambda z: [z & bit != 0 for bit in self.z_bits])
            cur = join([got[z] for z in near_first])
        else:
            for bit in self.z_bits[::-1]:
                (got,) = yield [(cur, "dp", 2 * bit)]
                cur = join([cur, got])
        found = [{0: (cur, c)} for c in columns[:-1]]
        orders = [self.f_bits[::-1] if flipped else self.f_bits for _, flipped in sides]
        every = range(len(sides))
        pending = [([(s, 0) for s in every], True, cur)]
        yield found, pending, columns
        sends = [([(s, bit) for s in every], True, (cur, "fsdp", bit)) for bit in self.f_bits]
        while sends:
            got = yield [x for _, _, x in sends]
            arrived, sends = sends, []
            for (keys, whole_row, _), g in zip(arrived, got):
                for s, i in keys:
                    found[s][i] = (g, columns[s] if whole_row else 0)
                pending.append((keys, whole_row, g))
            for keys, whole_row, _ in arrived:
                i = keys[0][1]
                for s, _ in keys:
                    array, column = found[s][i]
                    last = max(at for at, bit in enumerate(orders[s]) if i & bit)
                    for bit in orders[s][last + 1 :]:
                        part = array[:, column : column + columns[s + 1] - columns[s]]
                        sends.append(([(s, i | bit)], False, (part, "fsdp", bit)))


class Job:
    def __init__(self, tree, away, *sides):
        self.tree = tree
        self.away = away
        self.sides = [list(side) for side in sides]
        self.stages = ([] if away is None else ["core"]) + list(range(len(tree.f_bits))) + [("z", b) for b in tree.z_bits]
        self.total = None

    def wanted(self):
        if not self.stages:
            return []
        stage = self.stages[0]
        if stage == "core":
            return [(self.away, "dp", 1)]
        if isinstance(stage, int):
            bits = self.tree.f_bits
            return [(side[1], "fsdp", (bits[::-1] if side[2] else bits)[stage]) for side in self.sides]
        return [(self.total[1], "dp", 2 * stage[1])]

    def add(self, got):
        stage = self.stages.pop(0)
        more = bool(self.stages)
        total = lambda *xs: sum(x.astype(F32) for x in xs)
        sums = lambda *xs: total(*xs).astype(BF)
        if stage == "core":
            column = 0
            for side in self.sides:
                r, n = side[1].shape
                side[0] = [side[0], got[0][:r, column : column + n]]
                side[1] = sums(side[1], got[0][r:, column : column + n])
                column += n
        elif isinstance(stage, int):
            for side, g in zip(self.sides, got):
                known = side[0] if isinstance(side[0], list) else [side[0]]
                r = g.shape[0] // 2
                side[0], side[1] = sums(*[a[:r] for a in known], g[:r]), sums(*[a[r:] for a in known], g[r:])
            if not isinstance(self.stages[0], int):
                cat = lambda xs: xs[0] if len(xs) == 1 else jnp.concatenate(xs, 1)
                self.total = [cat([side[i] for side in self.sides]) for i in range(2)]
        else:
            keep = self.total[0]
            if more:
                r = keep.shape[0] // 2
                self.total = [sums(keep[:r], got[0][:r]), sums(keep[r:], got[0][r:])]
            else:
                self.total = keep.astype(F32) + got[0].astype(F32)

    def hold(self, arrays):
        stage = self.stages[0]
        if stage == "core":
            (self.away,) = arrays
        elif isinstance(stage, int):
            for side, a in zip(self.sides, arrays):
                side[1] = a
        else:
            self.total[1] = arrays[0]


class Flow:
    def __init__(self, tree, cur, sides, direct=False):
        self.tree = tree
        self.steps = tree.gather(cur, sides, direct)
        self.found = None
        self.linked = False
        self.next(None)

    def next(self, got):
        try:
            out = self.steps.send(got)
            if isinstance(out, tuple):
                self.found, self.pending, self.columns = out
                out = self.steps.send(None)
            self.sends = out
        except StopIteration:
            self.sends, self.linked = [], True

    def wanted(self):
        return list(self.sends)

    def add(self, got):
        self.next(got)

    def hold(self, arrays):
        self.sends = [(a,) + rest[1:] for a, rest in zip(arrays, self.sends)]

    def cores(self, most):
        return Cores(self, most)

    def rest(self):
        return Rest(self)

    @property
    def value(self):
        nf = self.tree.nf
        if not self.linked or any(len(f) < 2 * nf for f in self.found):
            return None
        return [[f[i] for i in range(2 * nf)] for f in self.found]


class Rest:
    def __init__(self, flow):
        self.flow = flow

    def wanted(self):
        return [] if self.flow.found is None else [(array, "dp", 1) for _, _, array in self.flow.pending]

    def hold(self, arrays):
        self.flow.pending[:] = [p[:2] + (a,) for p, a in zip(self.flow.pending, arrays)]


class Cores:
    def __init__(self, flow, most):
        self.flow = flow
        self.taken = [] if flow.found is None else flow.pending[:most]
        if self.taken:
            del flow.pending[: len(self.taken)]

    def wanted(self):
        return [(array, "dp", 1) for _, _, array in self.taken]

    def add(self, got):
        for (keys, whole_row, _), g in zip(self.taken, got):
            for s, i in keys:
                self.flow.found[s][self.flow.tree.nf + i] = (g, self.flow.columns[s] if whole_row else 0)


def drain(tree, flow):
    while flow.value is None:
        window(tree, [flow, flow.cores(5)])


def window(tree, works, others=(), later=()):
    works = [w for w in works if w.wanted()]
    later = [w for w in later if w.wanted()]
    sent = [[tree.swap(*x) for x in w.wanted()] for w in works]
    kept = [[x[0] for x in w.wanted()] for w in later]
    sent, kept, others = lax.optimization_barrier((sent, kept, tuple(others)))
    for w, arrays_in in zip(later, kept):
        w.hold(list(arrays_in))
    for w, got in zip(works, sent):
        w.add(list(got))
    return others


def per_device(
    tokens, segment_ids, rel_bucket, query_weight, query_bias, key_weight, key_bias, value_weight, value_bias,
    out_weight, out_bias, attention_gain, attention_shift, up_weight, up_bias, down_weight, down_bias,
    output_gain, output_shift, position_table, cotangent,
):
    x = tokens[0]
    t, d = x.shape
    seg = segment_ids[0]
    tree = Tree(d)
    rows = tree.rows
    ff = up_weight.shape[1]
    spread = ff // d
    buckets = position_table.shape[0]
    scale = 1.0 / math.sqrt(3.0 * (d // HEADS))
    vectors = (query_bias, key_bias, value_bias, out_bias, attention_gain, attention_shift, down_bias, output_gain, output_shift)
    cut = ff * 5 // 8
    late_cut = ff - cut
    lead = pack_first(query_weight, key_weight, value_weight, position_table.T, vectors, up_bias.reshape(spread, rows))
    one = Flow(tree, lead, [(2 * d, False), (d + buckets + 128, True)], True)
    place = tree.place(False)
    place_t = tree.place(True)
    half = t // 2
    picked = lax.rev(rel_bucket[t - half : 2 * t - half], (0,))
    onehot = (picked[:, None] == lax.broadcasted_iota(jnp.int32, (t, buckets), 1)).astype(BF)
    early, late = pack_second(out_weight.T, up_weight, down_weight.T, cut)
    early, late, place, place_t, onehot = window(tree, [one], (early, late, place, place_t, onehot))
    two = Flow(tree, early, [(d + cut, False), (cut, True)])
    arrange = lambda m: mm(m, place, 1, 0).astype(BF)
    x_p = arrange(x)
    late, x_p = window(tree, [one, one.cores(1), two], (late, x_p))
    three = Flow(tree, late, [(late_cut, False), (late_cut, True)])
    cot_p = arrange(cotangent[0])
    (cot_p,) = window(tree, [one, one.cores(1), two], (cot_p,))
    window(tree, [one, one.cores(3)], (), [two.rest()])
    drain(tree, one)
    low, high = one.value

    small = jnp.concatenate([a[:, c + d + buckets : c + d + buckets + 128] for a, c in high], 0)
    vec = mm(small, place, 0, 1)
    same = (lax.broadcasted_iota(jnp.int32, (d, d), 0) == lax.broadcasted_iota(jnp.int32, (d, d), 1)).astype(BF)
    vecs = mm(small[:, 3:11], same, 0, 0)
    bias = vec[:3].reshape(1, 3 * d)
    bu = vec[SPLIT : SPLIT + spread].reshape(spread, tree.n, rows).transpose(1, 0, 2).reshape(1, ff)
    q, k, v, ek, eq = project(x_p, onehot, low, high, bias, TILE)
    q, k, v, ek, eq, vecs, bu = window(tree, [three], (q, k, v, ek, eq, vecs, bu), [two.rest()])
    n_pairs = HEADS // 2
    cuts = (0, n_pairs // 8, n_pairs // 2, n_pairs)
    plans = (
        lambda: ([two, two.cores(1), three], [two.rest()]),
        lambda: ([two, two.cores(1)], [two.rest(), three.rest()]),
        lambda: ([two.cores(3), three], [three.rest()]),
    )
    made = None
    for begin, after, plan in zip(cuts, cuts[1:], plans):
        made = attend(q, k, v, ek, eq, seg, scale, made, begin, after - begin)
        works, later = plan()
        made = window(tree, works, made, later)
    context, probs = made

    drain(tree, two)
    wo = two.value[0]
    shifted = lambda pieces, by: [(a, c + by) for a, c in pieces]
    up_a, dn_early = shifted(wo, d), two.value[1]
    count, late_count = cut // WIDE, late_cut // WIDE
    act_a, slope_a, n1, r1, mixed, mixed_low, so_far = feed_forward(vecs, bu, up_a, dn_early, 0, count, (context, x_p, wo))
    (so_far,) = window(tree, [three, three.cores(3)], (so_far,))
    drain(tree, three)
    up_b, dn_late = three.value
    act_b, slope_b, out_p, d_sum, d_ffn, sums2 = feed_forward(
        vecs, bu, up_b, dn_late, count, late_count, (mixed, mixed_low, so_far), cot_p
    )
    back = feed_back(tree, d_ffn, mixed_low, act_a, slope_a, up_a, dn_early, d_sum, count)
    job_1 = Job(tree, back[0], (*back[1:3], False), (*back[3:5], True))
    d_bu_a, total = back[5:]
    back = feed_back(
        tree, d_ffn, mixed_low, act_b, slope_b, up_b, dn_late, total, late_count, (context, wo, n1, r1, vecs[1:2])
    )
    job_2 = Job(tree, back[0], (*back[1:3], False), (*back[3:5], True))
    d_bu_b, d_attn, d_rest, d_context, sums1 = back[5:]
    (d_context,) = window(tree, [job_1], (d_context,))

    args = (q, k, v, ek, eq, d_context, probs, scale)
    grads = attend_back(*args, None, 0, n_pairs * 3 // 4)
    grads = window(tree, [job_1, job_2], grads)
    split = attention_grads(tree, x_p, onehot, low, high, *grads, d // 2, 0)
    (*grads, d_table, sums) = window(tree, [job_1], (*grads, *split[5:]))
    job_3 = Job(tree, split[0], (*split[1:3], False), (*split[3:5], True))
    grads = attend_back(*args, grads, n_pairs * 3 // 4, n_pairs // 4)
    grads = window(tree, [job_3, job_1], grads)
    d_bu = jnp.concatenate([d_bu_a, d_bu_b], 1)
    lines = d_bu.reshape(tree.n, spread, rows).transpose(1, 0, 2).reshape(spread, d)
    ordered = jnp.concatenate([sums1[:3], sums2[:3]], 0)
    ordered = jnp.concatenate([ordered, jnp.zeros((2, d), F32)], 0)
    carried = (d_table, sums, lines, ordered, place_t)
    split = attention_grads(tree, x_p, onehot, low, high, *grads, d // 2, 1, carried)
    split = window(tree, [job_2, job_1], split)
    job_4 = Job(tree, split[0], (*split[1:3], False), (*split[3:5], True))
    dq, dk, dv, _, _ = grads
    d_attn, d_rest = window(tree, [job_4, job_2], (d_attn, d_rest))
    grad_layer = input_grads(d_attn, d_rest, low, high, dq, dk, dv, out_p, place_t, TILE)
    input_grad, layer_out = window(tree, [job_4, job_3, job_2], grad_layer)
    works = [job_4, job_3, job_2, job_1]
    while any(w.stages for w in works):
        window(tree, works)
    four, three, two, one = [w.total for w in works]
    h = d // 2
    up_a_grad, dn_a_grad = one[:, :cut], one[:, cut:]
    up_b_grad, out_grad, dn_b_grad = two[:, :late_cut], two[:, late_cut : late_cut + d], two[:, late_cut + d :]
    query_grad, key_grad, value_grad = [
        jnp.concatenate([three[:, i * h : (i + 1) * h], four[:, i * h : (i + 1) * h]], 1) for i in range(3)
    ]
    table_grad, tail = four[:, 3 * h : 3 * h + buckets], four[:, 3 * h + buckets :]
    d_bq, d_bk, d_bv = [tail[:, i] for i in range(3)]
    d_up_bias = tail[:, 3 : 3 + spread].T.reshape(-1)
    d_bo, d_gain1, d_shift1, d_bd, d_gain2, d_shift2 = [tail[:, 16 + i] for i in range(6)]
    return (
        layer_out[None], input_grad[None],
        query_grad, d_bq, key_grad, d_bk, value_grad, d_bv,
        out_grad.T, d_bo, d_gain1, d_shift1, jnp.concatenate([up_a_grad, up_b_grad], 1), d_up_bias,
        jnp.concatenate([dn_a_grad.T, dn_b_grad.T], 0), d_bd, d_gain2, d_shift2,
        table_grad.T,
    )


def solution(mesh):
    both = ("dp", "fsdp")
    row, col, vec = P(both, None), P(None, both), P(both)
    seq = P(both, None, None)
    params = (row, vec, row, vec, row, vec, col, vec, vec, vec, row, vec, col, vec, vec, vec, col)
    return jax.shard_map(
        per_device, mesh=mesh, in_specs=(seq, row, P()) + params + (seq,), out_specs=(seq, seq) + params, check_vma=False
    )
```
